32 devices in a mesh: read: 32 (over z, y, x, core), pos: 1.
Axes of the slice: x: 2, y: 2, z: 4, core: 2. Of those that a mesh axis runs over, the one named last changes fastest.
Arguments:
- features: bfloat16 [128, 32, 768], P('read', 'pos'), may hold values from -6 to 6
- grad_out: bfloat16 [128, 32, 768], P('read', 'pos'), may hold values from -16 to 16
- weights: bfloat16 [4, 768, 768], replicated, may hold values from -0.21875 to 0.21875
- read_start: int32 [128], replicated, may hold values from 0 to 15
- read_end: int32 [128], replicated, may hold values from 17 to 32
Outputs:
- grad_input: bfloat16 [128, 32, 768], P('read', 'pos')
- weight_grads: float32 [768, 3072], P(('read', 'pos'))
The draws below stay inside these ranges and needn't reach their ends.
Inputs may be any that keep to these rules, and one draw needn't show every extreme that they name: read_end is above read_start for every read.
All inputs are finite; a program needn't handle non-finite values.
Results may differ from the reference program's by a relative error of at most 0.0086.
Values may be sent and summed in bfloat16 or wider, within the bound.
No kernel may reach another device: no remote copies, remote signals or barrier semaphores. Data moves between devices by JAX's collectives and lax.ppermute only.
A program may use at most 128 MiB of HBM per device.

```python
import math
import jax
import jax.numpy as jnp
from jax import lax

D = 768
HEADS = 12
HEAD_DIM = 64
READS = 128
COLS = 32


def touch_ends(values, stream_key, least, high):
    dims = values.shape
    spot = [jax.random.randint(jax.random.fold_in(stream_key, axis), (), 0, dims[axis]) for axis in range(len(dims))]
    values = values.at[tuple(spot)].set(least)
    longest = dims.index(max(dims))
    spot[longest] = (spot[longest] + 1) % dims[longest]
    return values.at[tuple(spot)].set(high)


def raised(result, stream_key, source, target, parts, factor):
    owner, partner = [(jnp.arange(result.shape[axis_at]) // (result.shape[axis_at] // parts)).reshape([-1 if axis == axis_at else 1 for axis in range(result.ndim)]) for axis_at in (source, target)]
    chosen = jax.random.permutation(stream_key, parts)[partner]
    strong = (owner == chosen) | (owner == (partner + parts // 2) % parts)
    return jnp.where(strong, factor * result, result)


def block_levels(key, dims, cuts, least, largest):
    def one(position, parts):
        steps = jax.random.uniform(jax.random.fold_in(jax.random.fold_in(key, 6), position), (parts,), jnp.float32, least / len(cuts), largest / len(cuts))
        return jnp.repeat(jnp.exp(steps), dims[position] // parts).reshape((-1,) + (1,) * (len(dims) - position - 1))

    loudness = one(*cuts[0])
    for cut in cuts[1:]:
        loudness = loudness * one(*cut)
    return loudness


def scatter_about(own_key, shape, spread, most, pieces=(), kind=jnp.bfloat16):
    result = jax.random.normal(own_key, shape, jnp.float32) * spread
    if len(pieces) > 0:
        result = block_levels(own_key, shape, pieces, -0.22, 0.18) * result
    return jnp.clip(result, min=-most, max=most).astype(kind)


def bell_draw_with(stream_key, extent, scale, reach, shards, heavy, held_as=jnp.bfloat16):
    array = scale * jax.random.normal(stream_key, extent, jnp.float32)
    if shards:
        array = array * block_levels(stream_key, extent, shards, -0.22, 0.18)
    return jnp.clip(raised(array, jax.random.fold_in(stream_key, 3), *heavy), -reach, reach).astype(held_as)


def setup_inputs(seed: int = 0) -> dict:
    arg_keys = jax.random.split(jax.random.key(seed), 6)
    return {
        "features": bell_draw_with(arg_keys[0], (READS, COLS, D), 1.0, 6.0, ((0, 32),), (0, 2, 32, 2.75)),
        "grad_out": scatter_about(arg_keys[1], (READS, COLS, D), 4.0, 16.0, ((0, 32),)),
        "weights": scatter_about(arg_keys[2], (4, D, D), D ** -0.5, 0.21875),
        "read_start": touch_ends(jax.random.randint(arg_keys[3], (READS,), 0, COLS // 2), jax.random.fold_in(arg_keys[3], 1), 0, (COLS // 2) - 1).astype(jnp.int32),
        "read_end": touch_ends(jax.random.randint(arg_keys[4], (READS,), COLS // 2 + 1, COLS + 1), jax.random.fold_in(arg_keys[4], 1), COLS // 2 + 1, COLS).astype(jnp.int32),
    }


def reference(features, grad_out, weights, read_start, read_end):
    reads, cols, width = features.shape
    columns = jnp.arange(cols, dtype=jnp.int32)
    covered = ((columns[None, :] >= read_start[:, None]) & (columns[None, :] < read_end[:, None])).astype(jnp.float32)
    values32 = features.reshape(-1, width).astype(jnp.float32)
    inverse = lax.rsqrt(lax.optimization_barrier(jnp.mean(values32 * values32, -1, keepdims=True)) + 1e-05)
    normed = values32 * inverse
    normed_b = normed.astype(jnp.bfloat16)
    keep_mask = covered.reshape(-1, 1)
    query = (jnp.dot(normed_b, weights[0], preferred_element_type=jnp.float32) * keep_mask).astype(jnp.bfloat16)
    keys = (jnp.dot(normed_b, weights[1], preferred_element_type=jnp.float32) * keep_mask).astype(jnp.bfloat16)
    vals = (jnp.dot(normed_b, weights[2], preferred_element_type=jnp.float32) * keep_mask).astype(jnp.bfloat16)
    grad_flat = grad_out.reshape(-1, width)
    back_out = jnp.dot(grad_flat, weights[3].T, preferred_element_type=jnp.float32).astype(jnp.bfloat16)
    shape4 = (reads, cols, HEADS, HEAD_DIM)
    query4 = query.reshape(shape4).astype(jnp.float32)
    keys4 = keys.reshape(shape4).astype(jnp.float32)
    vals4 = vals.reshape(shape4).astype(jnp.float32)
    back4 = back_out.reshape(shape4).astype(jnp.float32)
    scale = 1.0 / math.sqrt(HEAD_DIM * COLS)
    logits = jnp.einsum('rchd,schd->hrs', query4, keys4) * scale
    expon = jnp.exp(logits)
    probs = expon / lax.optimization_barrier(jnp.sum(expon, -1, keepdims=True))
    probs_b = probs.astype(jnp.bfloat16).astype(jnp.float32)
    output = jnp.einsum('hrs,schd->rchd', probs_b, vals4).astype(jnp.bfloat16)
    slopes = jnp.einsum('rchd,schd->hrs', back4, vals4)
    mixed = (scale * probs * (slopes - lax.optimization_barrier(jnp.sum(probs * slopes, -1, keepdims=True)))).astype(jnp.bfloat16).astype(jnp.float32)
    keep4 = covered[:, :, None, None]
    grad_query = (jnp.einsum('hrs,schd->rchd', mixed, keys4) * keep4).astype(jnp.bfloat16).reshape(-1, width)
    grad_keys = (jnp.einsum('hrs,rchd->schd', mixed, query4) * keep4).astype(jnp.bfloat16).reshape(-1, width)
    grad_values = (jnp.einsum('hrs,rchd->schd', probs_b, back4) * keep4).astype(jnp.bfloat16).reshape(-1, width)
    output_flat = output.reshape(-1, width)
    blocks = [jnp.dot(normed_b.T, grad_query, preferred_element_type=jnp.float32), jnp.dot(normed_b.T, grad_keys, preferred_element_type=jnp.float32), jnp.dot(normed_b.T, grad_values, preferred_element_type=jnp.float32), jnp.dot(output_flat.T, grad_flat, preferred_element_type=jnp.float32)]
    weight_grads = jnp.concatenate(blocks, axis=1)
    grad_norm = jnp.dot(grad_query, weights[0].T, preferred_element_type=jnp.float32)
    grad_norm = grad_norm + jnp.dot(grad_keys, weights[1].T, preferred_element_type=jnp.float32)
    grad_norm = grad_norm + jnp.dot(grad_values, weights[2].T, preferred_element_type=jnp.float32)
    grad_input = inverse * (grad_norm - normed * lax.optimization_barrier(jnp.mean(grad_norm * normed, -1, keepdims=True)))
    return (grad_input.astype(jnp.bfloat16).reshape(reads, cols, width), weight_grads)
```

```python
import math

import jax
import jax.numpy as jnp
from jax import lax
from jax.sharding import PartitionSpec as P

HEADS = 12
HEAD_DIM = 64
CORES = 2
KINDS = 4


def coverage(starts, ends, columns):
    inside = (columns[:, None] >= starts[None, :]) & (columns[:, None] < ends[None, :])
    return inside.astype(jnp.float32)


def dot_back(left, right):
    return lax.dot_general(
        left, right, (((1,), (1,)), ((), ())), preferred_element_type=jnp.float32
    )


def dot_cells(left, right):
    return lax.dot_general(
        left, right, (((0,), (0,)), ((), ())), preferred_element_type=jnp.float32
    )


def exchange(array, groups):
    return lax.all_to_all(
        array, "read", split_axis=0, concat_axis=0, tiled=True, axis_index_groups=groups
    )


def shards(features, grad_out, weights, read_start, read_end):
    rows, col_dev, width = features.shape
    count = lax.axis_size("read")
    pos_count = lax.axis_size("pos")
    me = lax.axis_index("read")
    pos_at = lax.axis_index("pos")
    scale = 1.0 / math.sqrt(HEAD_DIM * col_dev * pos_count)
    reads = rows * count
    chips = count // CORES
    part_heads = HEADS // CORES
    half = width // CORES
    core = me % CORES
    kind = (me // CORES) % KINDS
    tied_rows = reads // chips

    same_core = [list(range(c, count, CORES)) for c in range(CORES)]
    plane = [
        [base + c + CORES * j for j in range(KINDS)]
        for base in range(0, count, CORES * KINDS)
        for c in range(CORES)
    ]
    partner = [(i, i ^ 1) for i in range(count)]

    send = jnp.stack([features, grad_out]).transpose(2, 0, 1, 3).reshape(-1, width)
    own = exchange(send, None)
    other = lax.ppermute(own, "read", partner)
    both = jnp.stack([own, other]).reshape(2, count, 2, rows, width)
    source = both[:, :, 0].reshape(2 * reads, width)
    upstream = both[:, :, 1].reshape(2 * reads, width)
    columns = pos_at * col_dev + jnp.stack([me, me ^ 1])
    covered = coverage(read_start, read_end, columns).reshape(-1, 1)

    heads_in = lax.dynamic_slice_in_dim(weights[:3], core * half, half, 2)
    heads_out = lax.dynamic_slice_in_dim(weights[3], core * half, half, 0)
    source32 = source.astype(jnp.float32)
    inverse = lax.rsqrt(jnp.mean(source32 * source32, -1, keepdims=True) + 1e-05)
    normed = source32 * inverse
    normed_b = normed.astype(jnp.bfloat16)
    query, keys, values = (
        (jnp.dot(normed_b, heads_in[i], preferred_element_type=jnp.float32) * covered).astype(
            jnp.bfloat16
        )
        for i in range(3)
    )
    back_out = dot_back(upstream, heads_out).astype(jnp.bfloat16)

    shape4 = (2, reads, part_heads, HEAD_DIM)
    query4, keys4, values4, back4 = (
        a.reshape(shape4) for a in (query, keys, values, back_out)
    )
    partial = jnp.stack(
        [
            jnp.einsum("crhd,cshd->hrs", query4, keys4, preferred_element_type=jnp.float32),
            jnp.einsum("crhd,cshd->hrs", back4, values4, preferred_element_type=jnp.float32),
        ],
        1,
    ).astype(jnp.bfloat16)
    partial = partial.reshape(part_heads, 2, chips, tied_rows, reads).transpose(2, 0, 1, 3, 4)
    parts = exchange(partial, same_core).astype(jnp.float32)
    tied = lax.psum(jnp.sum(parts, 0), "pos")
    logits = tied[:, 0] * scale
    slopes = tied[:, 1]
    expon = jnp.exp(logits)
    probs = expon / jnp.sum(expon, -1, keepdims=True)
    mixed = scale * probs * (slopes - jnp.sum(probs * slopes, -1, keepdims=True))
    pair = jnp.stack([probs, mixed], 1).astype(jnp.bfloat16)
    copies = jnp.broadcast_to(pair[None], (chips,) + pair.shape)
    pairs = exchange(copies, same_core).transpose(1, 2, 0, 3, 4)
    pairs = pairs.reshape(part_heads, 2, reads, reads)
    probs_b, mixed = pairs[:, 0], pairs[:, 1]

    keep4 = covered.reshape(2, reads, 1, 1)

    def spread(form, left, right, keep=None):
        result = jnp.einsum(form, left, right, preferred_element_type=jnp.float32)
        if keep is not None:
            result = result * keep
        return result.astype(jnp.bfloat16).reshape(2 * reads, half)

    output = spread("hrs,cshd->crhd", probs_b, values4)
    grad_query = spread("hrs,cshd->crhd", mixed, keys4, keep4)
    grad_keys = spread("hrs,crhd->cshd", mixed, query4, keep4)
    grad_values = spread("hrs,crhd->cshd", probs_b, back4, keep4)

    grad_norm = (
        dot_back(grad_query, heads_in[0])
        + dot_back(grad_keys, heads_in[1])
        + dot_back(grad_values, heads_in[2])
    )
    grad_norm = grad_norm[:reads] + lax.ppermute(grad_norm[reads:], "read", partner)
    grad_in = inverse[:reads] * (
        grad_norm - normed[:reads] * jnp.mean(grad_norm * normed[:reads], -1, keepdims=True)
    )
    grad_in = exchange(grad_in.astype(jnp.bfloat16), None)
    grad_input = grad_in.reshape(col_dev, rows, width).transpose(1, 0, 2)

    left = jnp.stack([normed_b[:reads]] * 3 + [upstream[:reads]])
    left = exchange(left, plane)
    left = jnp.stack([left, lax.ppermute(left, "read", partner)], 1).reshape(-1, width)
    right = exchange(jnp.stack([grad_query, grad_keys, grad_values, output]), plane)
    right = right.reshape(-1, half)
    right_other = lax.ppermute(right, "read", partner)
    right_other = right_other.reshape(KINDS, 2, reads, half)[:, ::-1].reshape(-1, half)
    outputs = jnp.concatenate(
        [
            jnp.where(core == 0, right, right_other),
            jnp.where(core == 0, right_other, right),
        ],
        1,
    )
    last = kind == KINDS - 1
    product = dot_cells(
        jnp.where(last, outputs, left),
        jnp.where(last, lax.dynamic_slice_in_dim(left, core * half, half, 1), right),
    ).astype(jnp.bfloat16)
    pieces = exchange(product.reshape(count, width // count, half), None)
    pieces = pieces.reshape(-1, KINDS, CORES, width // count, half).astype(jnp.float32)
    sums = jnp.sum(pieces, 0).transpose(2, 0, 1, 3).reshape(width // count, KINDS * width)
    weight_grads = lax.psum_scatter(sums, "pos", scatter_dimension=0, tiled=True)
    return (grad_input, weight_grads)


def solution(mesh):
    in_specs = (P("read", "pos", None), P("read", "pos", None), P(), P(), P())
    out_specs = (P("read", "pos", None), P(("read", "pos"), None))
    return jax.shard_map(shards, mesh=mesh, in_specs=in_specs, out_specs=out_specs, check_vma=False)
```

```python
import functools
import math

import jax
import jax.numpy as jnp
from jax import lax
from jax.experimental import pallas as pl
from jax.experimental.pallas import tpu as pltpu
from jax.sharding import PartitionSpec as P

HEADS = 12
HEAD_DIM = 64
CORES = 2
KINDS = 4
LANES = 128
VMEM_LIMIT = 48 * 1024 * 1024

BF16 = jnp.bfloat16
F32 = jnp.float32


def dot(left, right, contract=(1, 0)):
    return lax.dot_general(
        left, right, (((contract[0],), (contract[1],)), ((), ())), preferred_element_type=F32
    )


def row_mask(start, end, column):
    return ((start <= column) & (column < end)).astype(F32)


def first_heads(rows, lanes):
    at = lax.broadcasted_iota(jnp.int32, (rows, lanes), 1)
    return lax.rem(at, LANES) < HEAD_DIM


def slab(array, at):
    reads = array.shape[0] // 2
    lanes = slice(at * LANES, (at + 1) * LANES)
    return jnp.concatenate([array[:reads, lanes], array[reads:, lanes]], axis=1)


def project_kernel(
    scalars, own, other, heads_in, heads_out, start, end, proj, tied, left_own, left_other, *, rows
):
    cells = own.shape[0] // 2
    at = lax.broadcasted_iota(jnp.int32, (cells, 2 * cells), 0)
    spot = lax.broadcasted_iota(jnp.int32, (cells, 2 * cells), 1)
    place = lax.div(at, rows) * (2 * rows) + lax.rem(at, rows)
    pick_source = (spot == place).astype(F32).astype(BF16)
    pick_upstream = (spot == place + rows).astype(F32).astype(BF16)
    mine, theirs = own[...], other[...]
    source = jnp.concatenate([dot(pick_source, mine), dot(pick_source, theirs)], axis=0)
    upstream32 = jnp.concatenate([dot(pick_upstream, mine), dot(pick_upstream, theirs)], axis=0)
    upstream = upstream32.astype(BF16)
    inverse = lax.rsqrt(jnp.mean(source * source, -1, keepdims=True) + 1e-05)
    normed = (source * inverse).astype(BF16)
    covered = jnp.concatenate(
        [
            row_mask(start[...], end[...], scalars[2]),
            row_mask(start[...], end[...], scalars[3]),
        ],
        axis=0,
    )
    query = (dot(normed, heads_in[0]) * covered).astype(BF16)
    keys = (dot(normed, heads_in[1]) * covered).astype(BF16)
    values = (dot(normed, heads_in[2]) * covered).astype(BF16)
    back_out = dot(upstream, heads_out[0], (1, 1)).astype(BF16)
    proj[0] = query
    proj[1] = keys
    proj[2] = values
    proj[3] = back_out

    normed32 = normed.astype(F32)
    for step in range(KINDS):
        last = jnp.bitwise_xor(scalars[1], step) == KINDS - 1
        left_own[step] = jnp.where(last, upstream32[:cells], normed32[:cells]).astype(BF16)
    last = scalars[1] == KINDS - 1
    left_other[...] = jnp.where(last, upstream32[cells:], normed32[cells:]).astype(BF16)

    low = first_heads(cells, 2 * LANES)
    chips = tied.shape[0]
    part = cells // chips
    for pair in range(query.shape[1] // LANES):
        queries, backs = slab(query, pair), slab(back_out, pair)
        key, value = slab(keys, pair), slab(values, pair)
        for odd in range(2):
            keep = jnp.logical_not(low) if odd else low
            logits = dot(jnp.where(keep, queries, 0), key, (1, 1))
            slopes = dot(jnp.where(keep, backs, 0), value, (1, 1))
            both = jnp.concatenate(
                [logits.reshape(chips, part, cells), slopes.reshape(chips, part, cells)], axis=1
            )
            spot = (2 * pair + odd) * 2 * part
            tied[:, spot : spot + 2 * part, :] = both.astype(BF16)


def soften_kernel(parts, copies, *, scale, part):
    total = jnp.sum(parts[...].astype(F32), axis=0)
    blocks = total.reshape(-1, 2 * part, total.shape[-1])
    logits = blocks[:, :part] * scale
    slopes = blocks[:, part:]
    expon = jnp.exp(logits)
    probs = expon / jnp.sum(expon, -1, keepdims=True)
    mixed = scale * probs * (slopes - jnp.sum(probs * slopes, -1, keepdims=True))
    result = jnp.concatenate([probs, mixed], axis=1).reshape(total.shape).astype(BF16)
    for chip in range(copies.shape[0]):
        copies[chip] = result


def attend_kernel(scalars, pairs, proj, start, end, grads):
    cells = proj.shape[1] // 2
    chips = pairs.shape[0]
    part = cells // chips
    covered = jnp.concatenate(
        [
            jnp.broadcast_to(row_mask(start[...], end[...], scalars[2]), (cells, LANES)),
            jnp.broadcast_to(row_mask(start[...], end[...], scalars[3]), (cells, LANES)),
        ],
        axis=1,
    )
    low = first_heads(cells, 2 * LANES)

    def store(kind, pair, first, second, masked):
        result = jnp.where(low, first, second)
        if masked:
            result = result * covered
        result = result.astype(BF16)
        lanes = slice(pair * LANES, (pair + 1) * LANES)
        grads[kind, :cells, lanes] = result[:, :LANES]
        grads[kind, cells:, lanes] = result[:, LANES:]

    for pair in range(proj.shape[2] // LANES):
        probs, mixed = [], []
        for odd in range(2):
            spot = (2 * pair + odd) * 2 * part
            both = pairs[:, spot : spot + 2 * part, :].astype(F32)
            probs.append(both[:, :part].reshape(cells, cells))
            mixed.append(both[:, part:].reshape(cells, cells))
        probs_t = [a.T.astype(BF16) for a in probs]
        mixed_t = [a.T.astype(BF16) for a in mixed]
        probs = [a.astype(BF16) for a in probs]
        mixed = [a.astype(BF16) for a in mixed]
        query, key, value, back = (slab(proj[kind], pair) for kind in range(KINDS))
        store(0, pair, dot(mixed[0], key), dot(mixed[1], key), True)
        store(1, pair, dot(mixed_t[0], query), dot(mixed_t[1], query), True)
        store(2, pair, dot(probs_t[0], back), dot(probs_t[1], back), True)
        store(3, pair, dot(probs[0], value), dot(probs[1], value), False)


def back_kernel(scalars, grads, heads_in, own, other):
    cells = own.shape[0]
    total = dot(grads[0], heads_in[0], (1, 1))
    total = total + dot(grads[1], heads_in[1], (1, 1))
    total = total + dot(grads[2], heads_in[2], (1, 1))
    own[...] = total[:cells]
    other[...] = total[cells:]


def weight_kernel(scalars, *refs):
    lefts_own, lefts_other = refs[:KINDS], refs[KINDS : 2 * KINDS]
    right, right_other, product = refs[2 * KINDS :]
    cells = right.shape[1] // 2
    half = right.shape[2]
    core, kind = scalars[0], scalars[1]

    @pl.when(kind < KINDS - 1)
    def _():
        total = None
        for step in range(KINDS):
            grads = right[jnp.bitwise_xor(kind, step)]
            term = dot(lefts_own[step][...], grads[:cells], (0, 0))
            term = term + dot(lefts_other[step][...], grads[cells:], (0, 0))
            total = term if total is None else total + term
        product[...] = total.astype(BF16)

    for side in range(CORES):

        @pl.when((kind == KINDS - 1) & (core == side))
        def _():
            lanes = slice(side * half, (side + 1) * half)
            mine, theirs = None, None
            for step in range(KINDS):
                chip = jnp.bitwise_xor(kind, step)
                ups = [lefts_own[step][:, lanes], lefts_other[step][:, lanes]]
                term = dot(right[chip, :cells], ups[0], (0, 0))
                term = term + dot(right[chip, cells:], ups[1], (0, 0))
                mine = term if mine is None else mine + term
                term = dot(right_other[chip, cells:], ups[0], (0, 0))
                term = term + dot(right_other[chip, :cells], ups[1], (0, 0))
                theirs = term if theirs is None else theirs + term
            product[side * half : (side + 1) * half, :] = mine.astype(BF16)
            product[(1 - side) * half : (2 - side) * half, :] = theirs.astype(BF16)


def exchange(array, groups):
    return lax.all_to_all(
        array, "read", split_axis=0, concat_axis=0, tiled=True, axis_index_groups=groups
    )


def whole(shape):
    return pl.BlockSpec(shape, lambda i, s: (0,) * len(shape))


def run(kernel, scalars, args, specs, outs):
    return pl.pallas_call(
        kernel,
        grid_spec=pltpu.PrefetchScalarGridSpec(
            num_scalar_prefetch=1,
            grid=(1,),
            in_specs=[spec or whole(arg.shape) for arg, spec in zip(args, specs)],
            out_specs=[whole(out.shape) for out in outs],
        ),
        out_shape=outs,
        compiler_params=pltpu.CompilerParams(vmem_limit_bytes=VMEM_LIMIT),
    )(scalars, *args)


def shards(features, grad_out, weights, read_start, read_end):
    rows, col_dev, width = features.shape
    count = lax.axis_size("read")
    pos_count = lax.axis_size("pos")
    me = lax.axis_index("read")
    pos_at = lax.axis_index("pos")
    scale = 1.0 / math.sqrt(HEAD_DIM * col_dev * pos_count)
    reads = rows * count
    chips = count // CORES
    half = width // CORES
    core = lax.rem(me, CORES)
    kind = lax.rem(me // CORES, KINDS)
    part = reads // chips
    tied_rows = (HEADS // CORES) * 2 * part
    first = pos_at * col_dev
    scalars = jnp.stack([core, kind, first + me, first + jnp.bitwise_xor(me, 1)]).astype(jnp.int32)
    start = read_start.reshape(reads, 1)
    end = read_end.reshape(reads, 1)

    same_core = [list(range(c, count, CORES)) for c in range(CORES)]
    plane = [
        [base + c + CORES * j for j in range(KINDS)]
        for base in range(0, count, CORES * KINDS)
        for c in range(CORES)
    ]

    def swap(array, bits):
        return lax.ppermute(array, "read", [(i, i ^ bits) for i in range(count)])

    shape = jax.ShapeDtypeStruct
    heads_in = pl.BlockSpec((3, width, half), lambda i, s: (0, 0, s[0]))
    heads_out = pl.BlockSpec((1, half, width), lambda i, s: (3, s[0], 0))

    send = jnp.stack([features, grad_out]).transpose(2, 0, 1, 3).reshape(-1, width)
    own = exchange(send, None)
    other = swap(own, 1)
    proj, tied, left_own, left_other = run(
        functools.partial(project_kernel, rows=rows),
        scalars,
        (own, other, weights, weights, start, end),
        (None, None, heads_in, heads_out, None, None),
        (
            shape((KINDS, 2 * reads, half), BF16),
            shape((chips, tied_rows, reads), BF16),
            shape((KINDS, reads, width), BF16),
            shape((reads, width), BF16),
        ),
    )

    parts = exchange(tied, same_core)
    lefts_own = [left_own[0]] + [swap(left_own[k], CORES * k) for k in range(1, KINDS)]
    lefts_other = [left_other] + [swap(a, 1) for a in lefts_own[1:]]
    if pos_count > 1:
        parts = lax.psum(jnp.sum(parts.astype(F32), 0, keepdims=True), "pos")
    copies = pl.pallas_call(
        functools.partial(soften_kernel, scale=scale, part=part),
        out_shape=shape((chips, tied_rows, reads), BF16),
        compiler_params=pltpu.CompilerParams(vmem_limit_bytes=VMEM_LIMIT),
    )(parts)
    pairs = exchange(copies, same_core)

    (grads,) = run(
        attend_kernel,
        scalars,
        (pairs, proj, start, end),
        (None,) * 4,
        (shape((KINDS, 2 * reads, half), BF16),),
    )
    right = exchange(grads, plane)

    grad_own, grad_other = run(
        back_kernel,
        scalars,
        (grads, weights),
        (None, heads_in),
        (shape((reads, width), F32), shape((reads, width), F32)),
    )
    source = own.reshape(count, 2, rows, width)[:, 0].reshape(reads, width).astype(F32)
    inverse = lax.rsqrt(jnp.mean(source * source, -1, keepdims=True) + 1e-05)
    normed = source * inverse
    grad_norm = grad_own + swap(grad_other, 1)
    grad_in = inverse * (grad_norm - normed * jnp.mean(grad_norm * normed, -1, keepdims=True))
    grad_in = exchange(grad_in.astype(BF16), None)
    grad_input = grad_in.reshape(col_dev, rows, width).transpose(1, 0, 2)

    right_other = swap(right, 1)
    (product,) = run(
        weight_kernel,
        scalars,
        (*lefts_own, *lefts_other, right, right_other),
        (None,) * (2 * KINDS + 2),
        (shape((width, half), BF16),),
    )
    pieces = exchange(product.reshape(count, width // count, half), None)
    pieces = pieces.reshape(-1, KINDS, CORES, width // count, half).astype(F32)
    sums = jnp.sum(pieces, 0).transpose(2, 0, 1, 3).reshape(width // count, KINDS * width)
    weight_grads = lax.psum_scatter(sums, "pos", scatter_dimension=0, tiled=True)
    return (grad_input, weight_grads)


def solution(mesh):
    in_specs = (P("read", "pos", None), P("read", "pos", None), P(), P(), P())
    out_specs = (P("read", "pos", None), P(("read", "pos"), None))
    return jax.shard_map(shards, mesh=mesh, in_specs=in_specs, out_specs=out_specs, check_vma=False)
```

```python
import functools
import math

import jax
import jax.numpy as jnp
from jax import lax
from jax.experimental import pallas as pl
from jax.experimental.pallas import tpu as pltpu
from jax.sharding import PartitionSpec as P

HEADS = 12
HEAD_DIM = 64
CORES = 2
KINDS = 4
LANES = 128
VMEM_LIMIT = 48 * 1024 * 1024

BF16 = jnp.bfloat16
F32 = jnp.float32


def dot(left, right, contract=(1, 0)):
    return lax.dot_general(
        left, right, (((contract[0],), (contract[1],)), ((), ())), preferred_element_type=F32
    )


def upright(lanes):
    size = lanes.shape[1]
    rows = lax.broadcasted_iota(jnp.int32, (size, size), 0)
    cols = lax.broadcasted_iota(jnp.int32, (size, size), 1)
    spread = jnp.broadcast_to(lanes.astype(F32), (size, size))
    return jnp.sum(jnp.where(rows == cols, spread, 0.0), -1, keepdims=True)


def row_mask(start, end, column):
    column = column.astype(F32)
    return ((start <= column) & (column < end)).astype(F32)


def first_heads(rows, lanes):
    at = lax.broadcasted_iota(jnp.int32, (rows, lanes), 1)
    return lax.rem(at, LANES) < HEAD_DIM


def slab(array, at):
    reads = array.shape[0] // 2
    lanes = slice(at * LANES, (at + 1) * LANES)
    return jnp.concatenate([array[:reads, lanes], array[reads:, lanes]], axis=1)


def indicator(rows, cols, place):
    at = lax.broadcasted_iota(jnp.int32, (rows, cols), 0)
    spot = lax.broadcasted_iota(jnp.int32, (rows, cols), 1)
    return place(at, spot).astype(F32).astype(BF16)


def project_kernel(
    scalars, own, other, heads_in, heads_out, start, end, proj, tied, normed_own, inverse_own,
    left_other, *pieces, rows
):
    ops, lefts = pieces[:KINDS], pieces[KINDS:]
    cells = own.shape[0] // 2

    def pick(shift):
        return indicator(
            cells,
            2 * cells,
            lambda at, spot: spot == lax.div(at, rows) * (2 * rows) + lax.rem(at, rows) + shift,
        )

    mine, theirs = own[...], other[...]
    source = jnp.concatenate([dot(pick(0), mine), dot(pick(0), theirs)], axis=0)
    upstream = jnp.concatenate([dot(pick(rows), mine), dot(pick(rows), theirs)], axis=0)
    upstream = upstream.astype(BF16)
    inverse = lax.rsqrt(jnp.mean(source * source, -1, keepdims=True) + 1e-05)
    normed32 = source * inverse
    normed = normed32.astype(BF16)
    normed_own[...] = normed32[:cells]
    inverse_own[...] = jnp.broadcast_to(inverse[:cells], inverse_own.shape)
    first, last = upright(start[...]), upright(end[...])
    covered = jnp.concatenate(
        [row_mask(first, last, scalars[2]), row_mask(first, last, scalars[3])], axis=0
    )
    query = (dot(normed, heads_in[0]) * covered).astype(BF16)
    keys = (dot(normed, heads_in[1]) * covered).astype(BF16)
    values = (dot(normed, heads_in[2]) * covered).astype(BF16)
    back_out = dot(upstream, heads_out[0], (1, 1)).astype(BF16)
    proj[0] = query
    proj[1] = keys
    proj[2] = values
    proj[3] = back_out

    for kind in range(KINDS):

        @pl.when(scalars[1] == kind)
        def _():
            needs = (keys, query, back_out, values)
            for step in range(KINDS):
                ops[step][...] = needs[kind ^ step]
                side = upstream if kind ^ step == KINDS - 1 else normed
                lefts[step][...] = side[:cells]
                if step == 0:
                    left_other[...] = side[cells:]

    low = first_heads(cells, 2 * LANES)
    chips = tied.shape[0]
    part = cells // chips
    for pair in range(query.shape[1] // LANES):
        queries, backs = slab(query, pair), slab(back_out, pair)
        key, value = slab(keys, pair), slab(values, pair)
        for odd in range(2):
            keep = jnp.logical_not(low) if odd else low
            logits = dot(jnp.where(keep, queries, 0), key, (1, 1))
            slopes = dot(jnp.where(keep, backs, 0), value, (1, 1))
            both = jnp.concatenate(
                [logits.reshape(chips, part, cells), slopes.reshape(chips, part, cells)], axis=1
            )
            spot = (2 * pair + odd) * 2 * part
            tied[:, spot : spot + 2 * part, :] = both.astype(BF16)


def soften_kernel(parts, copies, *, scale, part):
    total = jnp.sum(parts[...].astype(F32), axis=0)
    blocks = total.reshape(-1, 2 * part, total.shape[-1])
    logits = blocks[:, :part] * scale
    slopes = blocks[:, part:]
    expon = jnp.exp(logits)
    probs = expon / jnp.sum(expon, -1, keepdims=True)
    mixed = scale * probs * (slopes - jnp.sum(probs * slopes, -1, keepdims=True))
    result = jnp.concatenate([probs, mixed], axis=1).reshape(total.shape).astype(BF16)
    for chip in range(copies.shape[0]):
        copies[chip] = result


def head_maps(pairs, head, cells):
    part = cells // pairs.shape[0]
    both = pairs[:, head * 2 * part : (head + 1) * 2 * part, :].astype(F32)
    return both[:, :part].reshape(cells, cells), both[:, part:].reshape(cells, cells)


def back_kernel(scalars, pairs, proj, heads_in, start, end, own, other, grads):
    cells = proj.shape[1] // 2
    first, last = upright(start[...]), upright(end[...])
    covered = jnp.concatenate(
        [
            jnp.broadcast_to(row_mask(first, last, scalars[2]), (cells, LANES)),
            jnp.broadcast_to(row_mask(first, last, scalars[3]), (cells, LANES)),
        ],
        axis=1,
    )
    low = first_heads(cells, 2 * LANES)
    for pair in range(proj.shape[2] // LANES):
        lanes = slice(pair * LANES, (pair + 1) * LANES)

        def store(kind, one, two):
            result = (jnp.where(low, one, two) * covered).astype(BF16)
            grads[kind, :cells, lanes] = result[:, :LANES]
            grads[kind, cells:, lanes] = result[:, LANES:]

        maps = [head_maps(pairs, 2 * pair + odd, cells) for odd in range(2)]
        probs_t = [a.T.astype(BF16) for a, _ in maps]
        mixed_t = [b.T.astype(BF16) for _, b in maps]
        mixed = [b.astype(BF16) for _, b in maps]
        query, key, back = slab(proj[0], pair), slab(proj[1], pair), slab(proj[3], pair)
        store(0, dot(mixed[0], key), dot(mixed[1], key))
        store(1, dot(mixed_t[0], query), dot(mixed_t[1], query))
        store(2, dot(probs_t[0], back), dot(probs_t[1], back))

    total = dot(grads[0], heads_in[0], (1, 1))
    total = total + dot(grads[1], heads_in[1], (1, 1))
    total = total + dot(grads[2], heads_in[2], (1, 1))
    own[...] = total[:cells]
    other[...] = total[cells:]


def weight_kernel(scalars, pairs, pairs_other, start, end, *refs):
    ops, ops_other, lefts, lefts_other = (
        refs[at * KINDS : (at + 1) * KINDS] for at in range(4)
    )
    product, right, right_other = refs[4 * KINDS :]
    cells, width = lefts[0].shape
    half = ops[0].shape[1]
    core, kind = scalars[0], scalars[1]
    low = first_heads(cells, 2 * KINDS * LANES)
    use_probs = kind >= 2
    use_flip = (kind == 1) | (kind == 2)

    def gradient(source, operands, covered, out, swapped):
        for pair in range(half // LANES):
            cat = jnp.concatenate([slab(operand[...], pair) for operand in operands], axis=1)
            sides = []
            for odd in range(2):
                probs, mixed = head_maps(source, 2 * pair + odd, cells)
                if swapped:
                    chosen = probs
                else:
                    chosen = jnp.where(use_probs, probs, mixed)
                    chosen = jnp.where(use_flip, chosen.T, chosen)
                sides.append(dot(chosen.astype(BF16), cat))
            result = jnp.where(low, sides[0], sides[1])
            if covered is not None:
                result = result * covered
            result = result.astype(BF16)
            lanes = slice(pair * LANES, (pair + 1) * LANES)
            for at in range(2 * KINDS):
                to = at ^ 1 if swapped else at
                out[to * cells : (to + 1) * cells, lanes] = result[
                    :, at * LANES : (at + 1) * LANES
                ]

    first, last = upright(start[...]), upright(end[...])
    masks = []
    for step in range(KINDS):
        for side in range(2):
            mask = row_mask(first, last, scalars[4 + 2 * step + side])
            masks.append(jnp.broadcast_to(mask, (cells, LANES)))
    covered = jnp.concatenate(masks, axis=1)
    covered = jnp.where(kind == KINDS - 1, 1.0, covered)
    gradient(pairs, ops, covered, right, False)

    @pl.when(kind < KINDS - 1)
    def _():
        left = jnp.concatenate(
            [ref[...] for pair in zip(lefts, lefts_other) for ref in pair], axis=0
        )
        product[...] = dot(left, right[...], (0, 0)).astype(BF16)

    @pl.when(kind == KINDS - 1)
    def _():
        gradient(pairs_other, ops_other, None, right_other, True)
        for side in range(CORES):

            @pl.when(core == side)
            def _():
                lanes = slice(side * half, (side + 1) * half)
                ups = jnp.concatenate(
                    [ref[:, lanes] for pair in zip(lefts, lefts_other) for ref in pair], axis=0
                )
                mine = dot(right[...], ups, (0, 0)).astype(BF16)
                theirs = dot(right_other[...], ups, (0, 0)).astype(BF16)
                product[side * half : (side + 1) * half, :] = mine
                product[(1 - side) * half : (2 - side) * half, :] = theirs


def pack_kernel(grad_own, grad_recv, normed, inverse, product, payload, *, rows):
    cells, width = normed.shape
    tiles = width // LANES
    half = product.shape[1]
    group = rows * tiles
    grad_norm = grad_own[...] + grad_recv[...]
    mean = jnp.mean(grad_norm * normed[...], -1, keepdims=True)
    result = (grad_norm - normed[...] * mean) * inverse[:, :1]
    result = result.astype(BF16)
    stack = jnp.concatenate(
        [result[:, t * LANES : (t + 1) * LANES] for t in range(tiles)], axis=0
    )

    def place(at, spot):
        tile, cell = lax.div(spot, cells), lax.rem(spot, cells)
        return at == lax.div(cell, rows) * group + tile * rows + lax.rem(cell, rows)

    payload[:, :half] = product[...]
    payload[:, half:] = dot(indicator(width, tiles * cells, place), stack).astype(BF16)


def finish_kernel(arrived, grad_input, sums):
    count, chunk, wide = arrived.shape
    rows, cols, width = grad_input.shape
    half = wide - LANES
    group = KINDS * CORES
    for kind in range(KINDS):
        for core in range(CORES):
            total = None
            for base in range(0, count, group):
                term = arrived[base + kind * CORES + core, :, :half].astype(F32)
                total = term if total is None else total + term
            spot = kind * width + core * half
            sums[:, spot : spot + half] = total
    flat = arrived[:, :, half:].astype(F32).reshape(count * chunk, LANES).astype(BF16)
    cells = rows * cols

    def place(at, spot):
        tile, cell = lax.div(at, cells), lax.rem(at, cells)
        return spot == lax.rem(cell, cols) * chunk + tile * rows + lax.div(cell, cols)

    tiles = width // LANES
    moved = dot(indicator(tiles * cells, count * chunk, place), flat).astype(BF16)
    for tile in range(tiles):
        for row in range(rows):
            spot = tile * cells + row * cols
            grad_input[row, :, tile * LANES : (tile + 1) * LANES] = moved[spot : spot + cols]


def exchange(array, groups):
    return lax.all_to_all(
        array, "read", split_axis=0, concat_axis=0, tiled=True, axis_index_groups=groups
    )


def whole(shape):
    return pl.BlockSpec(shape, lambda i, s: (0,) * len(shape))


def call(kernel, scalars, args, outs, specs=None, scratch=()):
    specs = specs or {}
    return pl.pallas_call(
        kernel,
        grid_spec=pltpu.PrefetchScalarGridSpec(
            num_scalar_prefetch=1,
            grid=(1,),
            in_specs=[specs.get(at) or whole(arg.shape) for at, arg in enumerate(args)],
            out_specs=[whole(out.shape) for out in outs],
            scratch_shapes=scratch,
        ),
        out_shape=outs,
        compiler_params=pltpu.CompilerParams(vmem_limit_bytes=VMEM_LIMIT),
    )(scalars, *args)


def simple(kernel, args, outs):
    return pl.pallas_call(
        kernel,
        out_shape=outs,
        compiler_params=pltpu.CompilerParams(vmem_limit_bytes=VMEM_LIMIT),
    )(*args)


def shards(features, grad_out, weights, read_start, read_end):
    rows, col_dev, width = features.shape
    count = lax.axis_size("read")
    pos_count = lax.axis_size("pos")
    me = lax.axis_index("read")
    pos_at = lax.axis_index("pos")
    scale = 1.0 / math.sqrt(HEAD_DIM * col_dev * pos_count)
    reads = rows * count
    chips = count // CORES
    half = width // CORES
    part = reads // chips
    tied_rows = (HEADS // CORES) * 2 * part
    chunk = width // count
    first = pos_at * col_dev
    core = jnp.bitwise_and(me, CORES - 1)
    kind = jnp.bitwise_and(jnp.right_shift(me, 1), KINDS - 1)
    columns = [first + jnp.bitwise_xor(me, at) for at in range(CORES * KINDS)]
    scalars = jnp.stack([core, kind, columns[0], columns[1], *columns]).astype(jnp.int32)
    start = read_start.reshape(1, reads)
    end = read_end.reshape(1, reads)

    same_core = [list(range(c, count, CORES)) for c in range(CORES)]

    def swap(array, bits):
        return lax.ppermute(array, "read", [(i, i ^ bits) for i in range(count)])

    shape = jax.ShapeDtypeStruct
    heads_in = pl.BlockSpec((3, width, half), lambda i, s: (0, 0, s[0]))
    heads_out = pl.BlockSpec((1, half, width), lambda i, s: (3, s[0], 0))

    send = jnp.stack([features, grad_out]).transpose(2, 0, 1, 3).reshape(-1, width)
    own = exchange(send, None)
    other = swap(own, 1)
    proj, tied, normed, inverse, left_other, *pieces = call(
        functools.partial(project_kernel, rows=rows),
        scalars,
        (own, other, weights, weights, start, end),
        (
            shape((KINDS, 2 * reads, half), BF16),
            shape((chips, tied_rows, reads), BF16),
            shape((reads, width), F32),
            shape((reads, LANES), F32),
            shape((reads, width), BF16),
            *[shape((2 * reads, half), BF16)] * KINDS,
            *[shape((reads, width), BF16)] * KINDS,
        ),
        {2: heads_in, 3: heads_out},
    )
    ops, lefts = pieces[:KINDS], pieces[KINDS:]

    parts = exchange(tied, same_core)
    moved = [swap(ops[k], CORES * k) for k in range(1, KINDS)]
    parts, *moved = lax.optimization_barrier((parts, *moved))
    ops = [ops[0], *moved]
    if pos_count > 1:
        parts = lax.psum(jnp.sum(parts.astype(F32), 0, keepdims=True), "pos")
    copies = simple(
        functools.partial(soften_kernel, scale=scale, part=part),
        (parts,),
        shape((chips, tied_rows, reads), BF16),
    )
    pairs = exchange(copies, same_core)
    lefts = [lefts[0]] + [swap(lefts[k], CORES * k) for k in range(1, KINDS)]
    lefts_other = [left_other] + [swap(a, 1) for a in lefts[1:]]
    ops_other = [swap(a, 1) for a in ops]
    pairs_other = swap(pairs, 1)

    grad_own, grad_other = call(
        back_kernel,
        scalars,
        (pairs, proj, weights, start, end),
        (shape((reads, width), F32), shape((reads, width), F32)),
        {2: heads_in},
        [pltpu.VMEM((3, 2 * reads, half), BF16)],
    )
    grad_recv = swap(grad_other, 1)

    cells = 2 * KINDS * reads
    (product,) = call(
        weight_kernel,
        scalars,
        (pairs, pairs_other, start, end, *ops, *ops_other, *lefts, *lefts_other),
        (shape((width, half), BF16),),
        None,
        [pltpu.VMEM((cells, half), BF16), pltpu.VMEM((cells, half), BF16)],
    )
    payload = simple(
        functools.partial(pack_kernel, rows=rows),
        (grad_own, grad_recv, normed, inverse, product),
        shape((width, half + LANES), BF16),
    )
    arrived = exchange(payload.reshape(count, chunk, half + LANES), None)
    grad_input, sums = simple(
        finish_kernel,
        (arrived,),
        (shape((rows, col_dev, width), BF16), shape((chunk, KINDS * width), F32)),
    )
    weight_grads = lax.psum_scatter(sums, "pos", scatter_dimension=0, tiled=True)
    return (grad_input, weight_grads)


def solution(mesh):
    in_specs = (P("read", "pos", None), P("read", "pos", None), P(), P(), P())
    out_specs = (P("read", "pos", None), P(("read", "pos"), None))
    return jax.shard_map(shards, mesh=mesh, in_specs=in_specs, out_specs=out_specs, check_vma=False)
```

```python
import functools
import math

import jax
import jax.numpy as jnp
from jax import lax
from jax.experimental import pallas as pl
from jax.experimental.pallas import tpu as pltpu
from jax.sharding import PartitionSpec as P

HEADS = 12
HEAD_DIM = 64
CORES = 2
KINDS = 4
LANES = 128
MIB = 1024 * 1024

BF16 = jnp.bfloat16
F32 = jnp.float32


def dot(left, right, contract=(1, 0)):
    return lax.dot_general(
        left, right, (((contract[0],), (contract[1],)), ((), ())), preferred_element_type=F32
    )


def upright(lanes):
    size = lanes.shape[1]
    rows = lax.broadcasted_iota(jnp.int32, (size, size), 0)
    cols = lax.broadcasted_iota(jnp.int32, (size, size), 1)
    spread = jnp.broadcast_to(lanes.astype(F32), (size, size))
    return jnp.sum(jnp.where(rows == cols, spread, 0.0), -1, keepdims=True)


def row_mask(start, end, column):
    column = column.astype(F32)
    return ((start <= column) & (column < end)).astype(F32)


def first_heads(rows, lanes):
    at = lax.broadcasted_iota(jnp.int32, (rows, lanes), 1)
    return lax.rem(at, LANES) < HEAD_DIM


def slab(array, at):
    reads = array.shape[0] // 2
    lanes = slice(at * LANES, (at + 1) * LANES)
    return jnp.concatenate([array[:reads, lanes], array[reads:, lanes]], axis=1)


def indicator(rows, cols, place):
    at = lax.broadcasted_iota(jnp.int32, (rows, cols), 0)
    spot = lax.broadcasted_iota(jnp.int32, (rows, cols), 1)
    return place(at, spot).astype(F32).astype(BF16)


def position():
    me = lax.axis_index("read")
    core = jnp.bitwise_and(me, CORES - 1)
    kind = jnp.bitwise_and(jnp.right_shift(me, 1), KINDS - 1)
    return me, core, kind


def head_lanes(core, half):
    return pl.ds(pl.multiple_of(core * half, LANES), half)


def project_kernel(
    own, other, weights, start, end, proj, tied, normed_own, inverse_own, bounds, left_other,
    *rest, rows, col_dev
):
    ops, lefts = rest[:KINDS], rest[KINDS : 2 * KINDS]
    heads_in, heads_out, start_here, end_here, sems = rest[2 * KINDS :]
    cells = own.shape[0] // 2
    width = own.shape[1]
    half = width // CORES
    me, core, mine_kind = position()
    first_col = lax.axis_index("pos") * col_dev
    copies = [
        pltpu.make_async_copy(
            weights.at[pl.ds(0, 3), :, head_lanes(core, half)], heads_in, sems.at[0]
        ),
        pltpu.make_async_copy(
            weights.at[3, head_lanes(core, half), :], heads_out, sems.at[1]
        ),
        pltpu.make_async_copy(start, start_here, sems.at[2]),
        pltpu.make_async_copy(end, end_here, sems.at[3]),
    ]
    for copy in copies:
        copy.start()

    def pick(shift):
        return indicator(
            cells,
            2 * cells,
            lambda at, spot: spot == lax.div(at, rows) * (2 * rows) + lax.rem(at, rows) + shift,
        )

    arrived = jnp.concatenate([own[...], other[...]], axis=1)
    source = dot(pick(0), arrived)
    source = jnp.concatenate([source[:, :width], source[:, width:]], axis=0)
    upstream = dot(pick(rows), arrived).astype(BF16)
    upstream = jnp.concatenate([upstream[:, :width], upstream[:, width:]], axis=0)
    inverse = lax.rsqrt(jnp.mean(source * source, -1, keepdims=True) + 1e-05)
    normed32 = source * inverse
    normed = normed32.astype(BF16)
    normed_own[...] = normed32[:cells]
    inverse_own[...] = jnp.broadcast_to(inverse[:cells], inverse_own.shape)
    copies[2].wait()
    copies[3].wait()
    first, last = upright(start_here[...]), upright(end_here[...])
    lane = lax.broadcasted_iota(jnp.int32, bounds.shape, 1)
    bounds[...] = jnp.where(lane == 0, first, last)
    covered = jnp.concatenate(
        [
            row_mask(first, last, first_col + me),
            row_mask(first, last, first_col + jnp.bitwise_xor(me, 1)),
        ],
        axis=0,
    )
    copies[0].wait()
    query = (dot(normed, heads_in[0]) * covered).astype(BF16)
    keys = (dot(normed, heads_in[1]) * covered).astype(BF16)
    values = (dot(normed, heads_in[2]) * covered).astype(BF16)
    copies[1].wait()
    back_out = dot(upstream, heads_out[...], (1, 1)).astype(BF16)
    proj[0] = query
    proj[1] = keys
    proj[2] = back_out

    for kind in range(KINDS):

        @pl.when(mine_kind == kind)
        def _():
            needs = (keys, query, back_out, values)
            for step in range(KINDS):
                ops[step][...] = needs[kind ^ step]
                side = upstream if kind ^ step == KINDS - 1 else normed
                lefts[step][...] = side[:cells]
                if step == 0:
                    left_other[...] = side[cells:]

    low = first_heads(cells, 2 * LANES)
    chips = tied.shape[0]
    part = cells // chips

    def both_heads(array):
        return jnp.concatenate([jnp.where(low, array, 0), jnp.where(low, 0, array)], axis=0)

    for pair in range(half // LANES):
        logits = dot(both_heads(slab(query, pair)), slab(keys, pair), (1, 1))
        slopes = dot(both_heads(slab(back_out, pair)), slab(values, pair), (1, 1))
        for odd in range(2):
            here = slice(odd * cells, (odd + 1) * cells)
            both = jnp.concatenate(
                [
                    logits[here].reshape(chips, part, cells),
                    slopes[here].reshape(chips, part, cells),
                ],
                axis=1,
            )
            spot = (2 * pair + odd) * 2 * part
            tied[:, spot : spot + 2 * part, :] = both.astype(BF16)


def soften_kernel(parts, copies, *, scale, part):
    total = jnp.sum(parts[...].astype(F32), axis=0)
    blocks = total.reshape(-1, 2 * part, total.shape[-1])
    logits = blocks[:, :part] * scale
    slopes = blocks[:, part:]
    expon = jnp.exp(logits)
    probs = expon / jnp.sum(expon, -1, keepdims=True)
    mixed = scale * probs * (slopes - jnp.sum(probs * slopes, -1, keepdims=True))
    result = jnp.concatenate([probs, mixed], axis=1).reshape(total.shape).astype(BF16)
    for chip in range(copies.shape[0]):
        copies[chip] = result


def head_maps(pairs, head, cells):
    part = cells // pairs.shape[0]
    both = pairs[:, head * 2 * part : (head + 1) * 2 * part, :].astype(F32)
    return both[:, :part].reshape(cells, cells), both[:, part:].reshape(cells, cells)


def back_kernel(pairs, proj, bounds, weights, own, other, grads, heads_in, sem, *, col_dev):
    cells = proj.shape[1] // 2
    half = proj.shape[2]
    me, core, _ = position()
    first_col = lax.axis_index("pos") * col_dev
    copy = pltpu.make_async_copy(
        weights.at[pl.ds(0, 3), :, head_lanes(core, half)], heads_in, sem
    )
    copy.start()
    first, last = bounds[:, 0:1], bounds[:, 1:2]
    masks = [
        jnp.broadcast_to(
            row_mask(first, last, first_col + jnp.bitwise_xor(me, side)), (cells, LANES)
        )
        for side in range(2)
    ]
    covered = jnp.concatenate(masks, axis=1)
    low = first_heads(cells, 2 * LANES)
    for pair in range(half // LANES):
        lanes = slice(pair * LANES, (pair + 1) * LANES)

        def store(kind, maps, operand):
            result = dot(jnp.concatenate(maps, axis=0), operand)
            result = (jnp.where(low, result[:cells], result[cells:]) * covered).astype(BF16)
            grads[kind, :cells, lanes] = result[:, :LANES]
            grads[kind, cells:, lanes] = result[:, LANES:]

        maps = [head_maps(pairs, 2 * pair + odd, cells) for odd in range(2)]
        store(0, [b.astype(BF16) for _, b in maps], slab(proj[1], pair))
        store(1, [b.T.astype(BF16) for _, b in maps], slab(proj[0], pair))
        store(2, [a.T.astype(BF16) for a, _ in maps], slab(proj[2], pair))

    copy.wait()
    total = dot(grads[0], heads_in[0], (1, 1))
    total = total + dot(grads[1], heads_in[1], (1, 1))
    total = total + dot(grads[2], heads_in[2], (1, 1))
    own[...] = total[:cells]
    other[...] = total[cells:]


def weight_kernel(pairs, pairs_other, bounds, *refs, col_dev):
    ops, ops_other, lefts, lefts_other = (
        refs[at * KINDS : (at + 1) * KINDS] for at in range(4)
    )
    product, right, right_other = refs[4 * KINDS :]
    cells, width = lefts[0].shape
    half = ops[0].shape[1]
    me, core, kind = position()
    first_col = lax.axis_index("pos") * col_dev
    low = first_heads(cells, 2 * KINDS * LANES)
    use_probs = kind >= 2
    use_flip = (kind == 1) | (kind == 2)

    def gradient(source, operands, covered, out, swapped):
        for pair in range(half // LANES):
            cat = jnp.concatenate([slab(operand[...], pair) for operand in operands], axis=1)
            maps = []
            for odd in range(2):
                probs, mixed = head_maps(source, 2 * pair + odd, cells)
                if swapped:
                    chosen = probs
                else:
                    chosen = jnp.where(use_probs, probs, mixed)
                    chosen = jnp.where(use_flip, chosen.T, chosen)
                maps.append(chosen.astype(BF16))
            result = dot(jnp.concatenate(maps, axis=0), cat)
            result = jnp.where(low, result[:cells], result[cells:])
            if covered is not None:
                result = result * covered
            result = result.astype(BF16)
            lanes = slice(pair * LANES, (pair + 1) * LANES)
            for at in range(2 * KINDS):
                to = at ^ 1 if swapped else at
                out[to * cells : (to + 1) * cells, lanes] = result[
                    :, at * LANES : (at + 1) * LANES
                ]

    first, last = bounds[:, 0:1], bounds[:, 1:2]
    masks = []
    for at in range(2 * KINDS):
        mask = row_mask(first, last, first_col + jnp.bitwise_xor(me, at))
        masks.append(jnp.broadcast_to(mask, (cells, LANES)))
    covered = jnp.concatenate(masks, axis=1)
    covered = jnp.where(kind == KINDS - 1, 1.0, covered)
    gradient(pairs, ops, covered, right, False)

    @pl.when(kind < KINDS - 1)
    def _():
        left = jnp.concatenate(
            [ref[...] for pair in zip(lefts, lefts_other) for ref in pair], axis=0
        )
        product[...] = dot(left, right[...], (0, 0)).astype(BF16)

    @pl.when(kind == KINDS - 1)
    def _():
        gradient(pairs_other, ops_other, None, right_other, True)
        for side in range(CORES):

            @pl.when(core == side)
            def _():
                lanes = slice(side * half, (side + 1) * half)
                ups = jnp.concatenate(
                    [ref[:, lanes] for pair in zip(lefts, lefts_other) for ref in pair], axis=0
                )
                mine = dot(right[...], ups, (0, 0)).astype(BF16)
                theirs = dot(right_other[...], ups, (0, 0)).astype(BF16)
                product[side * half : (side + 1) * half, :] = mine
                product[(1 - side) * half : (2 - side) * half, :] = theirs


def pack_kernel(grad_own, grad_recv, normed, inverse, product, payload, *, rows):
    cells, width = normed.shape
    tiles = width // LANES
    half = product.shape[1]
    group = rows * tiles
    grad_norm = grad_own[...] + grad_recv[...]
    mean = jnp.mean(grad_norm * normed[...], -1, keepdims=True)
    result = (grad_norm - normed[...] * mean) * inverse[:, :1]
    result = result.astype(BF16)
    stack = jnp.concatenate(
        [result[:, t * LANES : (t + 1) * LANES] for t in range(tiles)], axis=0
    )

    def place(at, spot):
        tile, cell = lax.div(spot, cells), lax.rem(spot, cells)
        return at == lax.div(cell, rows) * group + tile * rows + lax.rem(cell, rows)

    payload[:, :half] = product[...]
    payload[:, half:] = dot(indicator(width, tiles * cells, place), stack).astype(BF16)


def finish_kernel(arrived, grad_input, sums):
    count, chunk, wide = arrived.shape
    rows, cols, width = grad_input.shape
    half = wide - LANES
    group = KINDS * CORES
    for kind in range(KINDS):
        for core in range(CORES):
            total = None
            for base in range(0, count, group):
                term = arrived[base + kind * CORES + core, :, :half].astype(F32)
                total = term if total is None else total + term
            spot = kind * width + core * half
            sums[:, spot : spot + half] = total
    flat = arrived[:, :, half:].astype(F32).reshape(count * chunk, LANES).astype(BF16)
    cells = rows * cols

    def place(at, spot):
        tile, cell = lax.div(at, cells), lax.rem(at, cells)
        return spot == lax.rem(cell, cols) * chunk + tile * rows + lax.div(cell, cols)

    tiles = width // LANES
    moved = dot(indicator(tiles * cells, count * chunk, place), flat).astype(BF16)
    for tile in range(tiles):
        for row in range(rows):
            spot = tile * cells + row * cols
            grad_input[row, :, tile * LANES : (tile + 1) * LANES] = moved[spot : spot + cols]


def exchange(array, groups):
    return lax.all_to_all(
        array, "read", split_axis=0, concat_axis=0, tiled=True, axis_index_groups=groups
    )


def call(kernel, args, outs, mib, far=(), scratch=()):
    args = [
        pltpu.with_memory_space_constraint(arg, pltpu.HBM) if at in far else arg
        for at, arg in enumerate(args)
    ]
    near, away = (pl.BlockSpec(memory_space=space) for space in (pltpu.VMEM, pltpu.HBM))
    return pl.pallas_call(
        kernel,
        in_specs=[away if at in far else near for at in range(len(args))],
        out_specs=jax.tree.map(lambda _: near, outs),
        out_shape=outs,
        scratch_shapes=scratch,
        compiler_params=pltpu.CompilerParams(vmem_limit_bytes=mib * MIB),
    )(*args)


def shards(features, grad_out, weights, read_start, read_end):
    rows, col_dev, width = features.shape
    count = lax.axis_size("read")
    pos_count = lax.axis_size("pos")
    scale = 1.0 / math.sqrt(HEAD_DIM * col_dev * pos_count)
    reads = rows * count
    chips = count // CORES
    half = width // CORES
    part = reads // chips
    tied_rows = (HEADS // CORES) * 2 * part
    chunk = width // count
    start = read_start.reshape(1, reads)
    end = read_end.reshape(1, reads)

    same_core = [list(range(c, count, CORES)) for c in range(CORES)]

    def swap(array, bits):
        return lax.ppermute(array, "read", [(i, i ^ bits) for i in range(count)])

    shape = jax.ShapeDtypeStruct
    send = jnp.stack([features, grad_out]).transpose(2, 0, 1, 3).reshape(-1, width)
    own = exchange(send, None)
    other = swap(own, 1)
    proj, tied, normed, inverse, bounds, left_other, *pieces = call(
        functools.partial(project_kernel, rows=rows, col_dev=col_dev),
        (own, other, weights, start, end),
        (
            shape((KINDS - 1, 2 * reads, half), BF16),
            shape((chips, tied_rows, reads), BF16),
            shape((reads, width), F32),
            shape((reads, LANES), F32),
            shape((reads, LANES), F32),
            shape((reads, width), BF16),
            *[shape((2 * reads, half), BF16)] * KINDS,
            *[shape((reads, width), BF16)] * KINDS,
        ),
        20,
        (2, 3, 4),
        [
            pltpu.VMEM((3, width, half), BF16),
            pltpu.VMEM((half, width), BF16),
            pltpu.VMEM((1, reads), jnp.int32),
            pltpu.VMEM((1, reads), jnp.int32),
            pltpu.SemaphoreType.DMA((4,)),
        ],
    )
    ops, lefts = pieces[:KINDS], pieces[KINDS:]

    parts = exchange(tied, same_core)
    moved = [swap(ops[k], CORES * k) for k in range(1, KINDS)]
    if pos_count > 1:
        parts = lax.psum(jnp.sum(parts.astype(F32), 0, keepdims=True), "pos")
    copies = call(
        functools.partial(soften_kernel, scale=scale, part=part),
        (parts,),
        shape((chips, tied_rows, reads), BF16),
        8,
    )
    copies, *moved = lax.optimization_barrier((copies, *moved))
    ops = [ops[0], *moved]
    pairs = exchange(copies, same_core)
    lefts = [lefts[0]] + [swap(lefts[k], CORES * k) for k in range(1, KINDS)]
    ops_other = [swap(a, 1) for a in ops]
    pairs_other = swap(pairs, 1)

    grad_own, grad_other = call(
        functools.partial(back_kernel, col_dev=col_dev),
        (pairs, proj, bounds, weights),
        (shape((reads, width), F32), shape((reads, width), F32)),
        12,
        (3,),
        [
            pltpu.VMEM((3, 2 * reads, half), BF16),
            pltpu.VMEM((3, width, half), BF16),
            pltpu.SemaphoreType.DMA,
        ],
    )
    grad_other, *lefts = lax.optimization_barrier((grad_other, *lefts))
    lefts_other = [left_other] + [swap(a, 1) for a in lefts[1:]]
    grad_recv = swap(grad_other, 1)

    cells = 2 * KINDS * reads
    product = call(
        functools.partial(weight_kernel, col_dev=col_dev),
        (pairs, pairs_other, bounds, *ops, *ops_other, *lefts, *lefts_other),
        shape((width, half), BF16),
        20,
        (),
        [pltpu.VMEM((cells, half), BF16), pltpu.VMEM((cells, half), BF16)],
    )
    payload = call(
        functools.partial(pack_kernel, rows=rows),
        (grad_own, grad_recv, normed, inverse, product),
        shape((width, half + LANES), BF16),
        8,
    )
    arrived = exchange(payload.reshape(count, chunk, half + LANES), None)
    grad_input, sums = call(
        finish_kernel,
        (arrived,),
        (shape((rows, col_dev, width), BF16), shape((chunk, KINDS * width), F32)),
        8,
    )
    weight_grads = lax.psum_scatter(sums, "pos", scatter_dimension=0, tiled=True)
    return (grad_input, weight_grads)


def solution(mesh):
    in_specs = (P("read", "pos", None), P("read", "pos", None), P(), P(), P())
    out_specs = (P("read", "pos", None), P(("read", "pos"), None))
    return jax.shard_map(shards, mesh=mesh, in_specs=in_specs, out_specs=out_specs, check_vma=False)
```

```python
import functools
import math

import jax
import jax.numpy as jnp
from jax import lax
from jax.experimental import pallas as pl
from jax.experimental.pallas import tpu as pltpu
from jax.sharding import PartitionSpec as P

HEADS = 12
HEAD_DIM = 64
CORES = 2
KINDS = 4
LANES = 128
MIB = 1024 * 1024

BF16 = jnp.bfloat16
F32 = jnp.float32


def dot(left, right, contract=(1, 0)):
    return lax.dot_general(
        left, right, (((contract[0],), (contract[1],)), ((), ())), preferred_element_type=F32
    )


def upright(lanes):
    size = lanes.shape[1]
    rows = lax.broadcasted_iota(jnp.int32, (size, size), 0)
    cols = lax.broadcasted_iota(jnp.int32, (size, size), 1)
    spread = jnp.broadcast_to(lanes.astype(F32), (size, size))
    return jnp.sum(jnp.where(rows == cols, spread, 0.0), -1, keepdims=True)


def row_mask(start, end, column):
    column = column.astype(F32)
    return ((start <= column) & (column < end)).astype(F32)


def first_heads(rows, lanes):
    at = lax.broadcasted_iota(jnp.int32, (rows, lanes), 1)
    return lax.rem(at, LANES) < HEAD_DIM


def slab(array, at):
    reads = array.shape[0] // 2
    lanes = slice(at * LANES, (at + 1) * LANES)
    return jnp.concatenate([array[:reads, lanes], array[reads:, lanes]], axis=1)


def indicator(rows, cols, place):
    at = lax.broadcasted_iota(jnp.int32, (rows, cols), 0)
    spot = lax.broadcasted_iota(jnp.int32, (rows, cols), 1)
    return place(at, spot).astype(F32).astype(BF16)


def position():
    me = lax.axis_index("read")
    core = jnp.bitwise_and(me, CORES - 1)
    kind = jnp.bitwise_and(jnp.right_shift(me, 1), KINDS - 1)
    return me, core, kind


def head_lanes(core, half):
    return pl.ds(pl.multiple_of(core * half, LANES), half)


def project_kernel(
    own, other, weights, start, end, proj, tied, normed_own, inverse_own, bounds, left_other,
    *rest, rows, col_dev
):
    ops, lefts = rest[:KINDS], rest[KINDS : 2 * KINDS]
    heads_in, heads_out, start_here, end_here, sems = rest[2 * KINDS :]
    cells = own.shape[0] // 2
    width = own.shape[1]
    half = width // CORES
    me, core, mine_kind = position()
    first_col = lax.axis_index("pos") * col_dev
    copies = [
        pltpu.make_async_copy(
            weights.at[pl.ds(0, 3), :, head_lanes(core, half)], heads_in, sems.at[0]
        ),
        pltpu.make_async_copy(
            weights.at[3, head_lanes(core, half), :], heads_out, sems.at[1]
        ),
        pltpu.make_async_copy(start, start_here, sems.at[2]),
        pltpu.make_async_copy(end, end_here, sems.at[3]),
    ]
    for copy in copies:
        copy.start()

    def pick(shift):
        return indicator(
            cells,
            2 * cells,
            lambda at, spot: spot == lax.div(at, rows) * (2 * rows) + lax.rem(at, rows) + shift,
        )

    arrived = jnp.concatenate([own[...], other[...]], axis=1)
    source = dot(pick(0), arrived)
    source = jnp.concatenate([source[:, :width], source[:, width:]], axis=0)
    upstream = dot(pick(rows), arrived).astype(BF16)
    upstream = jnp.concatenate([upstream[:, :width], upstream[:, width:]], axis=0)
    inverse = lax.rsqrt(jnp.mean(source * source, -1, keepdims=True) + 1e-05)
    normed32 = source * inverse
    normed = normed32.astype(BF16)
    normed_own[...] = normed32[:cells]
    inverse_own[...] = jnp.broadcast_to(inverse[:cells], inverse_own.shape)
    copies[2].wait()
    copies[3].wait()
    first, last = upright(start_here[...]), upright(end_here[...])
    lane = lax.broadcasted_iota(jnp.int32, bounds.shape, 1)
    bounds[...] = jnp.where(lane == 0, first, last)
    covered = jnp.concatenate(
        [
            row_mask(first, last, first_col + me),
            row_mask(first, last, first_col + jnp.bitwise_xor(me, 1)),
        ],
        axis=0,
    )
    copies[0].wait()
    query = (dot(normed, heads_in[0]) * covered).astype(BF16)
    keys = (dot(normed, heads_in[1]) * covered).astype(BF16)
    values = (dot(normed, heads_in[2]) * covered).astype(BF16)
    copies[1].wait()
    back_out = dot(upstream, heads_out[...], (1, 1)).astype(BF16)
    proj[0] = query
    proj[1] = keys
    proj[2] = back_out

    for kind in range(KINDS):

        @pl.when(mine_kind == kind)
        def _():
            needs = (keys, query, back_out, values)
            for step in range(KINDS):
                ops[step][...] = needs[kind ^ step]
                side = upstream if kind ^ step == KINDS - 1 else normed
                lefts[step][...] = side[:cells]
                if step == 0:
                    left_other[...] = side[cells:]

    low = first_heads(cells, 2 * LANES)
    chips = tied.shape[0]
    part = cells // chips

    def both_heads(array):
        return jnp.concatenate([jnp.where(low, array, 0), jnp.where(low, 0, array)], axis=0)

    for pair in range(half // LANES):
        logits = dot(both_heads(slab(query, pair)), slab(keys, pair), (1, 1))
        slopes = dot(both_heads(slab(back_out, pair)), slab(values, pair), (1, 1))
        for odd in range(2):
            here = slice(odd * cells, (odd + 1) * cells)
            both = jnp.concatenate(
                [
                    logits[here].reshape(chips, part, cells),
                    slopes[here].reshape(chips, part, cells),
                ],
                axis=1,
            )
            spot = (2 * pair + odd) * 2 * part
            tied[:, spot : spot + 2 * part, :] = both.astype(BF16)


def soften_kernel(parts, copies, *, scale, part):
    total = jnp.sum(parts[...].astype(F32), axis=0)
    blocks = total.reshape(-1, 2 * part, total.shape[-1])
    logits = blocks[:, :part] * scale
    slopes = blocks[:, part:]
    expon = jnp.exp(logits)
    probs = expon / jnp.sum(expon, -1, keepdims=True)
    mixed = scale * probs * (slopes - jnp.sum(probs * slopes, -1, keepdims=True))
    result = jnp.concatenate([probs, mixed], axis=1).reshape(total.shape).astype(BF16)
    for chip in range(copies.shape[0]):
        copies[chip] = result


def head_maps(pairs, head, cells):
    part = cells // pairs.shape[0]
    both = pairs[:, head * 2 * part : (head + 1) * 2 * part, :].astype(F32)
    return both[:, :part].reshape(cells, cells), both[:, part:].reshape(cells, cells)


def back_kernel(pairs, proj, bounds, weights, own, other, grads, heads_in, sem, *, col_dev):
    cells = proj.shape[1] // 2
    half = proj.shape[2]
    me, core, _ = position()
    first_col = lax.axis_index("pos") * col_dev
    copy = pltpu.make_async_copy(
        weights.at[pl.ds(0, 3), :, head_lanes(core, half)], heads_in, sem
    )
    copy.start()
    first, last = bounds[:, 0:1], bounds[:, 1:2]
    masks = [
        jnp.broadcast_to(
            row_mask(first, last, first_col + jnp.bitwise_xor(me, side)), (cells, LANES)
        )
        for side in range(2)
    ]
    covered = jnp.concatenate(masks, axis=1)
    low = first_heads(cells, 2 * LANES)
    for pair in range(half // LANES):
        lanes = slice(pair * LANES, (pair + 1) * LANES)

        def store(kind, maps, operand):
            result = dot(jnp.concatenate(maps, axis=0), operand)
            result = (jnp.where(low, result[:cells], result[cells:]) * covered).astype(BF16)
            grads[kind, :cells, lanes] = result[:, :LANES]
            grads[kind, cells:, lanes] = result[:, LANES:]

        maps = [head_maps(pairs, 2 * pair + odd, cells) for odd in range(2)]
        store(0, [b.astype(BF16) for _, b in maps], slab(proj[1], pair))
        store(1, [b.T.astype(BF16) for _, b in maps], slab(proj[0], pair))
        store(2, [a.T.astype(BF16) for a, _ in maps], slab(proj[2], pair))

    copy.wait()
    total = dot(grads[0], heads_in[0], (1, 1))
    total = total + dot(grads[1], heads_in[1], (1, 1))
    total = total + dot(grads[2], heads_in[2], (1, 1))
    own[...] = total[:cells]
    other[...] = total[cells:]


def weight_kernel(pairs, bounds, *refs, col_dev):
    ops, lefts, lefts_other = (refs[at * KINDS : (at + 1) * KINDS] for at in range(3))
    product, spare, right = refs[3 * KINDS :]
    cells, width = lefts[0].shape
    half = ops[0].shape[1]
    me, core, kind = position()
    first_col = lax.axis_index("pos") * col_dev
    low = first_heads(cells, 2 * KINDS * LANES)
    use_probs = kind >= 2
    use_flip = (kind == 1) | (kind == 2)
    first, last = bounds[:, 0:1], bounds[:, 1:2]
    masks = []
    for at in range(2 * KINDS):
        mask = row_mask(first, last, first_col + jnp.bitwise_xor(me, at))
        masks.append(jnp.broadcast_to(mask, (cells, LANES)))
    covered = jnp.concatenate(masks, axis=1)
    covered = jnp.where(kind == KINDS - 1, 1.0, covered)

    for pair in range(half // LANES):
        cat = jnp.concatenate([slab(operand[...], pair) for operand in ops], axis=1)
        maps = []
        for odd in range(2):
            probs, mixed = head_maps(pairs, 2 * pair + odd, cells)
            chosen = jnp.where(use_probs, probs, mixed)
            chosen = jnp.where(use_flip, chosen.T, chosen)
            maps.append(chosen.astype(BF16))
        result = dot(jnp.concatenate(maps, axis=0), cat)
        result = (jnp.where(low, result[:cells], result[cells:]) * covered).astype(BF16)
        lanes = slice(pair * LANES, (pair + 1) * LANES)
        for at in range(2 * KINDS):
            right[at * cells : (at + 1) * cells, lanes] = result[
                :, at * LANES : (at + 1) * LANES
            ]

    left = jnp.concatenate(
        [ref[...] for pair in zip(lefts, lefts_other) for ref in pair], axis=0
    )

    @pl.when(kind < KINDS - 1)
    def _():
        product[...] = dot(left, right[...], (0, 0)).astype(BF16)

    @pl.when(kind == KINDS - 1)
    def _():
        rows = dot(right[...], left, (0, 0)).astype(BF16)

        @pl.when(core == 0)
        def _():
            product[:half] = rows[:, :half]
            spare[...] = rows[:, half:]

        @pl.when(core == 1)
        def _():
            product[:half] = rows[:, half:]
            spare[...] = rows[:, :half]


def pack_kernel(grad_own, grad_recv, normed, inverse, product, spare, payload, *, rows):
    cells, width = normed.shape
    tiles = width // LANES
    half = product.shape[1]
    group = rows * tiles
    grad_norm = grad_own[...] + grad_recv[...]
    mean = jnp.mean(grad_norm * normed[...], -1, keepdims=True)
    result = (grad_norm - normed[...] * mean) * inverse[:, :1]
    result = result.astype(BF16)
    stack = jnp.concatenate(
        [result[:, t * LANES : (t + 1) * LANES] for t in range(tiles)], axis=0
    )

    def place(at, spot):
        tile, cell = lax.div(spot, cells), lax.rem(spot, cells)
        return at == lax.div(cell, rows) * group + tile * rows + lax.rem(cell, rows)

    _, core, kind = position()

    @pl.when((kind < KINDS - 1) | (core == 0))
    def _():
        payload[:half, :half] = product[:half]

    @pl.when(kind < KINDS - 1)
    def _():
        payload[half:, :half] = product[half:]

    @pl.when((kind == KINDS - 1) & (core == 0))
    def _():
        payload[half:, :half] = spare[...]

    @pl.when((kind == KINDS - 1) & (core == 1))
    def _():
        payload[:half, :half] = spare[...]
        payload[half:, :half] = product[:half]

    payload[:, half:] = dot(indicator(width, tiles * cells, place), stack).astype(BF16)


def finish_kernel(arrived, grad_input, sums):
    count, chunk, wide = arrived.shape
    rows, cols, width = grad_input.shape
    half = wide - LANES
    group = KINDS * CORES
    for kind in range(KINDS):
        for core in range(CORES):
            total = None
            for base in range(0, count, group):
                term = arrived[base + kind * CORES + core, :, :half].astype(F32)
                total = term if total is None else total + term
            spot = kind * width + core * half
            sums[:, spot : spot + half] = total
    flat = arrived[:, :, half:].astype(F32).reshape(count * chunk, LANES).astype(BF16)
    cells = rows * cols

    def place(at, spot):
        tile, cell = lax.div(at, cells), lax.rem(at, cells)
        return spot == lax.rem(cell, cols) * chunk + tile * rows + lax.div(cell, cols)

    tiles = width // LANES
    moved = dot(indicator(tiles * cells, count * chunk, place), flat).astype(BF16)
    for tile in range(tiles):
        for row in range(rows):
            spot = tile * cells + row * cols
            grad_input[row, :, tile * LANES : (tile + 1) * LANES] = moved[spot : spot + cols]


def exchange(array, groups):
    return lax.all_to_all(
        array, "read", split_axis=0, concat_axis=0, tiled=True, axis_index_groups=groups
    )


def call(kernel, args, outs, mib, far=(), scratch=()):
    args = [
        pltpu.with_memory_space_constraint(arg, pltpu.HBM) if at in far else arg
        for at, arg in enumerate(args)
    ]
    near, away = (pl.BlockSpec(memory_space=space) for space in (pltpu.VMEM, pltpu.HBM))
    return pl.pallas_call(
        kernel,
        in_specs=[away if at in far else near for at in range(len(args))],
        out_specs=jax.tree.map(lambda _: near, outs),
        out_shape=outs,
        scratch_shapes=scratch,
        compiler_params=pltpu.CompilerParams(vmem_limit_bytes=mib * MIB),
    )(*args)


def shards(features, grad_out, weights, read_start, read_end):
    rows, col_dev, width = features.shape
    count = lax.axis_size("read")
    pos_count = lax.axis_size("pos")
    scale = 1.0 / math.sqrt(HEAD_DIM * col_dev * pos_count)
    reads = rows * count
    chips = count // CORES
    half = width // CORES
    part = reads // chips
    tied_rows = (HEADS // CORES) * 2 * part
    chunk = width // count
    start = read_start.reshape(1, reads)
    end = read_end.reshape(1, reads)

    same_core = [list(range(c, count, CORES)) for c in range(CORES)]

    def swap(array, bits):
        return lax.ppermute(array, "read", [(i, i ^ bits) for i in range(count)])

    shape = jax.ShapeDtypeStruct
    send = jnp.stack([features, grad_out]).transpose(2, 0, 1, 3).reshape(-1, width)
    own = exchange(send, None)
    other = swap(own, 1)
    proj, tied, normed, inverse, bounds, left_other, *pieces = call(
        functools.partial(project_kernel, rows=rows, col_dev=col_dev),
        (own, other, weights, start, end),
        (
            shape((KINDS - 1, 2 * reads, half), BF16),
            shape((chips, tied_rows, reads), BF16),
            shape((reads, width), F32),
            shape((reads, LANES), F32),
            shape((reads, LANES), F32),
            shape((reads, width), BF16),
            *[shape((2 * reads, half), BF16)] * KINDS,
            *[shape((reads, width), BF16)] * KINDS,
        ),
        20,
        (2, 3, 4),
        [
            pltpu.VMEM((3, width, half), BF16),
            pltpu.VMEM((half, width), BF16),
            pltpu.VMEM((1, reads), jnp.int32),
            pltpu.VMEM((1, reads), jnp.int32),
            pltpu.SemaphoreType.DMA((4,)),
        ],
    )
    ops, lefts = pieces[:KINDS], pieces[KINDS:]

    parts = exchange(tied, same_core)
    moved = [swap(lefts[k], CORES * k) for k in range(1, KINDS)]
    if pos_count > 1:
        parts = lax.psum(jnp.sum(parts.astype(F32), 0, keepdims=True), "pos")
    copies = call(
        functools.partial(soften_kernel, scale=scale, part=part),
        (parts,),
        shape((chips, tied_rows, reads), BF16),
        8,
    )
    copies, *moved = lax.optimization_barrier((copies, *moved))
    lefts = [lefts[0], *moved]
    lefts_other = [left_other] + [swap(a, 1) for a in moved]
    pairs = exchange(copies, same_core)
    ops = [ops[0]] + [swap(ops[k], CORES * k) for k in range(1, KINDS)]

    grad_own, grad_other = call(
        functools.partial(back_kernel, col_dev=col_dev),
        (pairs, proj, bounds, weights),
        (shape((reads, width), F32), shape((reads, width), F32)),
        12,
        (3,),
        [
            pltpu.VMEM((3, 2 * reads, half), BF16),
            pltpu.VMEM((3, width, half), BF16),
            pltpu.SemaphoreType.DMA,
        ],
    )
    grad_other, *ops = lax.optimization_barrier((grad_other, *ops))
    grad_recv = swap(grad_other, 1)

    cells = 2 * KINDS * reads
    product, spare = call(
        functools.partial(weight_kernel, col_dev=col_dev),
        (pairs, bounds, *ops, *lefts, *lefts_other),
        (shape((width, half), BF16), shape((half, half), BF16)),
        20,
        (),
        [pltpu.VMEM((cells, half), BF16)],
    )
    spare = swap(spare, 1)
    payload = call(
        functools.partial(pack_kernel, rows=rows),
        (grad_own, grad_recv, normed, inverse, product, spare),
        shape((width, half + LANES), BF16),
        8,
    )
    arrived = exchange(payload.reshape(count, chunk, half + LANES), None)
    grad_input, sums = call(
        finish_kernel,
        (arrived,),
        (shape((rows, col_dev, width), BF16), shape((chunk, KINDS * width), F32)),
        8,
    )
    weight_grads = lax.psum_scatter(sums, "pos", scatter_dimension=0, tiled=True)
    return (grad_input, weight_grads)


def solution(mesh):
    in_specs = (P("read", "pos", None), P("read", "pos", None), P(), P(), P())
    out_specs = (P("read", "pos", None), P(("read", "pos"), None))
    return jax.shard_map(shards, mesh=mesh, in_specs=in_specs, out_specs=out_specs, check_vma=False)
```

```python
import functools
import math

import jax
import jax.numpy as jnp
from jax import lax
from jax.experimental import pallas as pl
from jax.experimental.pallas import tpu as pltpu
from jax.sharding import PartitionSpec as P

HEADS = 12
HEAD_DIM = 64
CORES = 2
KINDS = 4
LANES = 128
MIB = 1024 * 1024

BF16 = jnp.bfloat16
F32 = jnp.float32


def dot(left, right, contract=(1, 0)):
    return lax.dot_general(
        left, right, (((contract[0],), (contract[1],)), ((), ())), preferred_element_type=F32
    )


def upright(lanes):
    size = lanes.shape[1]
    rows = lax.broadcasted_iota(jnp.int32, (size, size), 0)
    cols = lax.broadcasted_iota(jnp.int32, (size, size), 1)
    spread = jnp.broadcast_to(lanes.astype(F32), (size, size))
    return jnp.sum(jnp.where(rows == cols, spread, 0.0), -1, keepdims=True)


def row_mask(start, end, column):
    column = column.astype(F32)
    return ((start <= column) & (column < end)).astype(F32)


def first_heads(rows, lanes):
    at = lax.broadcasted_iota(jnp.int32, (rows, lanes), 1)
    return lax.rem(at, LANES) < HEAD_DIM


def slab(array, at):
    reads = array.shape[0] // 2
    lanes = slice(at * LANES, (at + 1) * LANES)
    return jnp.concatenate([array[:reads, lanes], array[reads:, lanes]], axis=1)


def indicator(rows, cols, place):
    at = lax.broadcasted_iota(jnp.int32, (rows, cols), 0)
    spot = lax.broadcasted_iota(jnp.int32, (rows, cols), 1)
    return place(at, spot).astype(F32).astype(BF16)


def position():
    me = lax.axis_index("read")
    core = jnp.bitwise_and(me, CORES - 1)
    kind = jnp.bitwise_and(jnp.right_shift(me, 1), KINDS - 1)
    return me, core, kind


def head_lanes(core, half):
    return pl.ds(pl.multiple_of(core * half, LANES), half)


def part_rows(arrived, rows, cells):
    def pick(shift):
        return indicator(
            cells,
            2 * cells,
            lambda at, spot: spot == lax.div(at, rows) * (2 * rows) + lax.rem(at, rows) + shift,
        )

    both = jnp.concatenate(arrived, axis=1)
    width = arrived[0].shape[1]
    source, upstream = dot(pick(0), both), dot(pick(rows), both).astype(BF16)

    def stack(array):
        return jnp.concatenate(
            [array[:, at * width : (at + 1) * width] for at in range(len(arrived))], axis=0
        )

    return stack(source), stack(upstream)


def normalise(source):
    inverse = lax.rsqrt(jnp.mean(source * source, -1, keepdims=True) + 1e-05)
    return source * inverse, inverse


def project_kernel(
    own, other, weights, start, end, proj, tied, normed_own, bounds, heads_in, heads_out,
    start_here, end_here, sems, *, rows, col_dev
):
    cells = own.shape[0] // 2
    half = own.shape[1] // CORES
    me, core, _ = position()
    first_col = lax.axis_index("pos") * col_dev
    copies = [
        pltpu.make_async_copy(start, start_here, sems.at[0]),
        pltpu.make_async_copy(end, end_here, sems.at[1]),
    ]
    for at in range(3):
        copies.append(
            pltpu.make_async_copy(
                weights.at[at, :, head_lanes(core, half)], heads_in.at[at], sems.at[2 + at]
            )
        )
    copies.append(
        pltpu.make_async_copy(weights.at[3, head_lanes(core, half), :], heads_out, sems.at[5])
    )
    for copy in copies:
        copy.start()

    source, upstream = part_rows([own[...], other[...]], rows, cells)
    normed32, inverse = normalise(source)
    normed = normed32.astype(BF16)
    normed_own[...] = normed32[:cells]
    copies[0].wait()
    copies[1].wait()
    first, last = upright(start_here[...]), upright(end_here[...])
    lane = lax.broadcasted_iota(jnp.int32, bounds.shape, 1)
    bounds[...] = jnp.where(lane == 0, first, jnp.where(lane == 1, last, inverse[:cells]))
    covered = jnp.concatenate(
        [
            row_mask(first, last, first_col + me),
            row_mask(first, last, first_col + jnp.bitwise_xor(me, 1)),
        ],
        axis=0,
    )
    copies[2].wait()
    query = (dot(normed, heads_in[0]) * covered).astype(BF16)
    copies[3].wait()
    keys = (dot(normed, heads_in[1]) * covered).astype(BF16)
    copies[4].wait()
    values = (dot(normed, heads_in[2]) * covered).astype(BF16)
    copies[5].wait()
    back_out = dot(upstream, heads_out[...], (1, 1)).astype(BF16)
    proj[0] = keys
    proj[1] = query
    proj[2] = back_out

    low = first_heads(cells, 2 * LANES)
    chips = tied.shape[0]
    part = cells // chips

    def both_heads(array):
        return jnp.concatenate([jnp.where(low, array, 0), jnp.where(low, 0, array)], axis=0)

    for pair in range(half // LANES):
        logits = dot(both_heads(slab(query, pair)), slab(keys, pair), (1, 1))
        slopes = dot(both_heads(slab(back_out, pair)), slab(values, pair), (1, 1))
        for odd in range(2):
            here = slice(odd * cells, (odd + 1) * cells)
            both = jnp.concatenate(
                [
                    logits[here].reshape(chips, part, cells),
                    slopes[here].reshape(chips, part, cells),
                ],
                axis=1,
            )
            spot = (2 * pair + odd) * 2 * part
            tied[:, spot : spot + 2 * part, :] = both.astype(BF16)


def operand_kernel(weights, bounds, *refs, rows, col_dev, slots):
    *raw, left, ops, heads, heads_back, sem = refs
    width = raw[0].shape[1]
    half = width // CORES
    cells = bounds.shape[0]
    per_block = len(raw) // (2 * len(slots))
    me, core, kind = position()
    first_col = lax.axis_index("pos") * col_dev
    for at, source_of in ((0, 1), (1, 0), (3, 2)):

        @pl.when(kind == at)
        def _():
            copy = pltpu.make_async_copy(
                weights.at[source_of, :, head_lanes(core, half)], heads, sem
            )
            copy.start()
            copy.wait()

    @pl.when(kind == 2)
    def _():
        copy = pltpu.make_async_copy(
            weights.at[3, head_lanes(core, half), :], heads_back, sem
        )
        copy.start()
        copy.wait()

    blocks = []
    for at in range(0, len(raw), per_block):
        pieces = [ref[...] for ref in raw[at : at + per_block]]
        blocks.append(pieces[0] if per_block == 1 else jnp.concatenate(pieces, axis=0))
    source, upstream = part_rows(blocks, rows, cells)
    normed = normalise(source)[0].astype(BF16)
    first, last = bounds[:, 0:1], bounds[:, 1:2]
    covered = jnp.concatenate(
        [
            row_mask(first, last, first_col + jnp.bitwise_xor(me, 2 * slot + side))
            for slot in slots
            for side in range(2)
        ],
        axis=0,
    )

    @pl.when(kind == 2)
    def _():
        ops[...] = dot(upstream, heads_back[...], (1, 1)).astype(BF16)

    @pl.when(kind != 2)
    def _():
        ops[...] = (dot(normed, heads[...]) * covered).astype(BF16)

    @pl.when(kind == KINDS - 1)
    def _():
        left[...] = upstream

    @pl.when(kind < KINDS - 1)
    def _():
        left[...] = normed


def soften_kernel(parts, copies, *, scale, part):
    total = jnp.sum(parts[...].astype(F32), axis=0)
    blocks = total.reshape(-1, 2 * part, total.shape[-1])
    logits = blocks[:, :part] * scale
    slopes = blocks[:, part:]
    expon = jnp.exp(logits)
    probs = expon / jnp.sum(expon, -1, keepdims=True)
    mixed = scale * probs * (slopes - jnp.sum(probs * slopes, -1, keepdims=True))
    result = jnp.concatenate([probs, mixed], axis=1).reshape(total.shape).astype(BF16)
    for chip in range(copies.shape[0]):
        copies[chip] = result


def head_maps(pairs, head, cells):
    part = cells // pairs.shape[0]
    both = pairs[:, head * 2 * part : (head + 1) * 2 * part, :].astype(F32)
    return both[:, :part].reshape(cells, cells), both[:, part:].reshape(cells, cells)


def gradient_kernel(
    pairs, proj, bounds, ops_near, ops_far, weights, left_near, left_far, own, other, product, spare,
    grads, right, heads_in, left, sems, *, col_dev
):
    cells = proj.shape[1] // 2
    half = proj.shape[2]
    me, core, kind = position()
    first_col = lax.axis_index("pos") * col_dev
    copies = [
        pltpu.make_async_copy(
            weights.at[at, :, head_lanes(core, half)], heads_in.at[at], sems.at[at]
        )
        for at in range(3)
    ]
    near = left_near.shape[0]
    copies.append(pltpu.make_async_copy(left_near, left.at[pl.ds(0, near)], sems.at[3]))
    copies.append(
        pltpu.make_async_copy(left_far, left.at[pl.ds(near, left_far.shape[0])], sems.at[4])
    )
    for at in (3, 4, 0, 1, 2):
        copies[at].start()
    first, last = bounds[:, 0:1], bounds[:, 1:2]
    masks = []
    for at in range(2 * KINDS):
        mask = row_mask(first, last, first_col + jnp.bitwise_xor(me, at))
        masks.append(jnp.broadcast_to(mask, (cells, LANES)))
    covered = jnp.concatenate(masks[:2], axis=1)
    plane_covered = jnp.where(kind == KINDS - 1, 1.0, jnp.concatenate(masks, axis=1))
    low = first_heads(cells, 2 * LANES)
    plane_low = first_heads(cells, 2 * KINDS * LANES)
    use_probs = kind >= 2
    use_flip = (kind == 1) | (kind == 2)

    for pair in range(half // LANES):
        lanes = slice(pair * LANES, (pair + 1) * LANES)

        def store(at, maps, operand):
            result = dot(jnp.concatenate(maps, axis=0), operand)
            result = (jnp.where(low, result[:cells], result[cells:]) * covered).astype(BF16)
            grads[at, :cells, lanes] = result[:, :LANES]
            grads[at, cells:, lanes] = result[:, LANES:]

        maps = [head_maps(pairs, 2 * pair + odd, cells) for odd in range(2)]
        flips = [(a.T, b.T) for a, b in maps]

        store(0, [b.astype(BF16) for _, b in maps], slab(proj[0], pair))
        store(1, [b.astype(BF16) for _, b in flips], slab(proj[1], pair))
        store(2, [a.astype(BF16) for a, _ in flips], slab(proj[2], pair))

        chosen = []
        for (a, b), (a_flip, b_flip) in zip(maps, flips):
            flat = jnp.where(use_probs, a, b)
            flip = jnp.where(use_probs, a_flip, b_flip)
            chosen.append(jnp.where(use_flip, flip, flat).astype(BF16))
        cat = jnp.concatenate(
            [
                ops[at : at + cells, lanes]
                for ops in (ops_near, ops_far)
                for at in range(0, ops.shape[0], cells)
            ],
            axis=1,
        )
        result = dot(jnp.concatenate(chosen, axis=0), cat)
        result = jnp.where(plane_low, result[:cells], result[cells:]) * plane_covered
        result = result.astype(BF16)
        for at in range(2 * KINDS):
            right[at * cells : (at + 1) * cells, lanes] = result[
                :, at * LANES : (at + 1) * LANES
            ]

    copies[3].wait()
    copies[4].wait()

    @pl.when(kind < KINDS - 1)
    def _():
        product[...] = dot(left[...], right[...], (0, 0)).astype(BF16)

    @pl.when(kind == KINDS - 1)
    def _():
        rows = dot(right[...], left[...], (0, 0)).astype(BF16)

        @pl.when(core == 0)
        def _():
            product[:half] = rows[:, :half]
            spare[...] = rows[:, half:]

        @pl.when(core == 1)
        def _():
            product[:half] = rows[:, half:]
            spare[...] = rows[:, :half]

    total = None
    for at in range(3):
        copies[at].wait()
        term = dot(grads[at], heads_in[at], (1, 1))
        total = term if total is None else total + term
    own[...] = total[:cells]
    other[...] = total[cells:]


def pack_kernel(grad_own, grad_recv, normed, bounds, product, spare, payload, *, rows):
    cells, width = normed.shape
    tiles = width // LANES
    half = product.shape[1]
    group = rows * tiles
    grad_norm = grad_own[...] + grad_recv[...]
    mean = jnp.mean(grad_norm * normed[...], -1, keepdims=True)
    result = (grad_norm - normed[...] * mean) * bounds[:, 2:3]
    result = result.astype(BF16)
    stack = jnp.concatenate(
        [result[:, t * LANES : (t + 1) * LANES] for t in range(tiles)], axis=0
    )

    def place(at, spot):
        tile, cell = lax.div(spot, cells), lax.rem(spot, cells)
        return at == lax.div(cell, rows) * group + tile * rows + lax.rem(cell, rows)

    _, core, kind = position()

    @pl.when((kind < KINDS - 1) | (core == 0))
    def _():
        payload[:half, :half] = product[:half]

    @pl.when(kind < KINDS - 1)
    def _():
        payload[half:, :half] = product[half:]

    @pl.when((kind == KINDS - 1) & (core == 0))
    def _():
        payload[half:, :half] = spare[...]

    @pl.when((kind == KINDS - 1) & (core == 1))
    def _():
        payload[:half, :half] = spare[...]
        payload[half:, :half] = product[:half]

    payload[:, half:] = dot(indicator(width, tiles * cells, place), stack).astype(BF16)


def finish_kernel(arrived, grad_input, sums):
    count, chunk, wide = arrived.shape
    rows, cols, width = grad_input.shape
    half = wide - LANES
    group = KINDS * CORES
    for kind in range(KINDS):
        for core in range(CORES):
            total = None
            for base in range(0, count, group):
                term = arrived[base + kind * CORES + core, :, :half].astype(F32)
                total = term if total is None else total + term
            spot = kind * width + core * half
            sums[:, spot : spot + half] = total
    flat = arrived[:, :, half:].astype(F32).reshape(count * chunk, LANES).astype(BF16)
    cells = rows * cols

    def place(at, spot):
        tile, cell = lax.div(at, cells), lax.rem(at, cells)
        return spot == lax.rem(cell, cols) * chunk + tile * rows + lax.div(cell, cols)

    tiles = width // LANES
    moved = dot(indicator(tiles * cells, count * chunk, place), flat).astype(BF16)
    for tile in range(tiles):
        for row in range(rows):
            spot = tile * cells + row * cols
            grad_input[row, :, tile * LANES : (tile + 1) * LANES] = moved[spot : spot + cols]


def exchange(array, groups):
    return lax.all_to_all(
        array, "read", split_axis=0, concat_axis=0, tiled=True, axis_index_groups=groups
    )


def call(kernel, args, outs, mib, far=(), scratch=(), cost=None):
    args = [
        pltpu.with_memory_space_constraint(arg, pltpu.HBM) if at in far else arg
        for at, arg in enumerate(args)
    ]
    near, away = (pl.BlockSpec(memory_space=space) for space in (pltpu.VMEM, pltpu.HBM))
    return pl.pallas_call(
        kernel,
        in_specs=[away if at in far else near for at in range(len(args))],
        out_specs=jax.tree.map(lambda _: near, outs),
        out_shape=outs,
        scratch_shapes=scratch,
        cost_estimate=cost,
        compiler_params=pltpu.CompilerParams(vmem_limit_bytes=mib * MIB),
    )(*args)


def shards(features, grad_out, weights, read_start, read_end):
    rows, col_dev, width = features.shape
    count = lax.axis_size("read")
    pos_count = lax.axis_size("pos")
    scale = 1.0 / math.sqrt(HEAD_DIM * col_dev * pos_count)
    reads = rows * count
    chips = count // CORES
    half = width // CORES
    part = reads // chips
    tied_rows = (HEADS // CORES) * 2 * part
    chunk = width // count
    start = read_start.reshape(1, reads)
    end = read_end.reshape(1, reads)

    same_core = [list(range(c, count, CORES)) for c in range(CORES)]

    def swap(array, bits):
        return lax.ppermute(array, "read", [(i, i ^ bits) for i in range(count)])

    shape = jax.ShapeDtypeStruct
    send = jnp.stack([features, grad_out]).transpose(2, 0, 1, 3).reshape(-1, width)
    own = exchange(send, None)
    other = swap(own, 1)
    proj, tied, normed, bounds = call(
        functools.partial(project_kernel, rows=rows, col_dev=col_dev),
        (own, other, weights, start, end),
        (
            shape((KINDS - 1, 2 * reads, half), BF16),
            shape((chips, tied_rows, reads), BF16),
            shape((reads, width), F32),
            shape((reads, LANES), F32),
        ),
        20,
        (2, 3, 4),
        [
            pltpu.VMEM((3, width, half), BF16),
            pltpu.VMEM((half, width), BF16),
            pltpu.VMEM((1, reads), jnp.int32),
            pltpu.VMEM((1, reads), jnp.int32),
            pltpu.SemaphoreType.DMA((6,)),
        ],
    )

    parts = exchange(tied, same_core)
    raw = {1: swap(own, CORES), 2: swap(own, 2 * CORES)}
    if pos_count > 1:
        parts = lax.psum(jnp.sum(parts.astype(F32), 0, keepdims=True), "pos")
    copies = call(
        functools.partial(soften_kernel, scale=scale, part=part),
        (parts,),
        shape((chips, tied_rows, reads), BF16),
        8,
    )
    pairs = exchange(copies, same_core)
    diagonal = [swap(raw[1][:reads], 2 * CORES), swap(raw[2][reads:], CORES)]

    def operands(slots, blocks):
        count_here = 2 * reads * len(slots)
        return call(
            functools.partial(operand_kernel, rows=rows, col_dev=col_dev, slots=slots),
            (weights, bounds, *blocks),
            (shape((count_here, width), BF16), shape((count_here, half), BF16)),
            24,
            (0,),
            [
                pltpu.VMEM((width, half), BF16),
                pltpu.VMEM((half, width), BF16),
                pltpu.SemaphoreType.DMA,
            ],
            pl.CostEstimate(flops=4 * 10**9, bytes_accessed=8 * MIB, transcendentals=0),
        )

    left_near, ops_near = operands(
        (0, 1, 2), (own, other, raw[1], swap(raw[1], 1), raw[2], swap(raw[2], 1))
    )
    left_far, ops_far = operands((3,), (*diagonal, *[swap(a, 1) for a in diagonal]))

    grad_own, grad_other, product, spare = call(
        functools.partial(gradient_kernel, col_dev=col_dev),
        (pairs, proj, bounds, ops_near, ops_far, weights, left_near, left_far),
        (
            shape((reads, width), F32),
            shape((reads, width), F32),
            shape((width, half), BF16),
            shape((half, half), BF16),
        ),
        24,
        (5, 6, 7),
        [
            pltpu.VMEM((3, 2 * reads, half), BF16),
            pltpu.VMEM((2 * KINDS * reads, half), BF16),
            pltpu.VMEM((3, width, half), BF16),
            pltpu.VMEM((2 * KINDS * reads, width), BF16),
            pltpu.SemaphoreType.DMA((5,)),
        ],
    )
    grad_recv = swap(grad_other, 1)
    spare = swap(spare, 1)
    payload = call(
        functools.partial(pack_kernel, rows=rows),
        (grad_own, grad_recv, normed, bounds, product, spare),
        shape((width, half + LANES), BF16),
        8,
    )
    arrived = exchange(payload.reshape(count, chunk, half + LANES), None)
    grad_input, sums = call(
        finish_kernel,
        (arrived,),
        (shape((rows, col_dev, width), BF16), shape((chunk, KINDS * width), F32)),
        8,
    )
    weight_grads = lax.psum_scatter(sums, "pos", scatter_dimension=0, tiled=True)
    return (grad_input, weight_grads)


def solution(mesh):
    in_specs = (P("read", "pos", None), P("read", "pos", None), P(), P(), P())
    out_specs = (P("read", "pos", None), P(("read", "pos"), None))
    return jax.shard_map(shards, mesh=mesh, in_specs=in_specs, out_specs=out_specs, check_vma=False)
```

```python
import functools
import math

import jax
import jax.numpy as jnp
from jax import lax
from jax.experimental import pallas as pl
from jax.experimental.pallas import tpu as pltpu
from jax.sharding import PartitionSpec as P

HEADS = 12
HEAD_DIM = 64
CORES = 2
KINDS = 4
LANES = 128
MIB = 1024 * 1024

BF16 = jnp.bfloat16
F32 = jnp.float32


def dot(left, right, contract=(1, 0)):
    return lax.dot_general(
        left, right, (((contract[0],), (contract[1],)), ((), ())), preferred_element_type=F32
    )


def upright(lanes):
    size = lanes.shape[1]
    rows = lax.broadcasted_iota(jnp.int32, (size, size), 0)
    cols = lax.broadcasted_iota(jnp.int32, (size, size), 1)
    spread = jnp.broadcast_to(lanes.astype(F32), (size, size))
    return jnp.sum(jnp.where(rows == cols, spread, 0.0), -1, keepdims=True)


def row_mask(start, end, column):
    column = column.astype(F32)
    return ((start <= column) & (column < end)).astype(F32)


def first_heads(rows, lanes):
    at = lax.broadcasted_iota(jnp.int32, (rows, lanes), 1)
    return lax.rem(at, LANES) < HEAD_DIM


def slab(array, at):
    reads = array.shape[0] // 2
    lanes = slice(at * LANES, (at + 1) * LANES)
    return jnp.concatenate([array[:reads, lanes], array[reads:, lanes]], axis=1)


def indicator(rows, cols, place):
    at = lax.broadcasted_iota(jnp.int32, (rows, cols), 0)
    spot = lax.broadcasted_iota(jnp.int32, (rows, cols), 1)
    return place(at, spot).astype(F32).astype(BF16)


def position():
    me = lax.axis_index("read")
    core = jnp.bitwise_and(me, CORES - 1)
    kind = jnp.bitwise_and(jnp.right_shift(me, 1), KINDS - 1)
    return me, core, kind


def head_lanes(core, half):
    return pl.ds(pl.multiple_of(core * half, LANES), half)


def part_rows(arrived, rows, cells):
    def pick(shift):
        return indicator(
            cells,
            2 * cells,
            lambda at, spot: spot == lax.div(at, rows) * (2 * rows) + lax.rem(at, rows) + shift,
        )

    both = jnp.concatenate(arrived, axis=1)
    width = arrived[0].shape[1]
    source, upstream = dot(pick(0), both), dot(pick(rows), both).astype(BF16)

    def stack(array):
        return jnp.concatenate(
            [array[:, at * width : (at + 1) * width] for at in range(len(arrived))], axis=0
        )

    return stack(source), stack(upstream)


def normalise(source):
    inverse = lax.rsqrt(jnp.mean(source * source, -1, keepdims=True) + 1e-05)
    return source * inverse, inverse


def project_kernel(
    own, other, weights, start, end, proj, tied, normed_own, bounds, heads_in, heads_out,
    start_here, end_here, sems, *, rows, col_dev
):
    cells = own.shape[0] // 2
    half = own.shape[1] // CORES
    me, core, _ = position()
    first_col = lax.axis_index("pos") * col_dev
    copies = [
        pltpu.make_async_copy(start, start_here, sems.at[0]),
        pltpu.make_async_copy(end, end_here, sems.at[1]),
    ]
    for at in range(3):
        copies.append(
            pltpu.make_async_copy(
                weights.at[at, :, head_lanes(core, half)], heads_in.at[at], sems.at[2 + at]
            )
        )
    copies.append(
        pltpu.make_async_copy(weights.at[3, head_lanes(core, half), :], heads_out, sems.at[5])
    )
    for copy in copies:
        copy.start()

    source, upstream = part_rows([own[...], other[...]], rows, cells)
    normed32, inverse = normalise(source)
    normed = normed32.astype(BF16)
    normed_own[...] = normed32[:cells]
    copies[0].wait()
    copies[1].wait()
    first, last = upright(start_here[...]), upright(end_here[...])
    lane = lax.broadcasted_iota(jnp.int32, bounds.shape, 1)
    bounds[...] = jnp.where(lane == 0, first, jnp.where(lane == 1, last, inverse[:cells]))
    covered = jnp.concatenate(
        [
            row_mask(first, last, first_col + me),
            row_mask(first, last, first_col + jnp.bitwise_xor(me, 1)),
        ],
        axis=0,
    )
    copies[2].wait()
    query = (dot(normed, heads_in[0]) * covered).astype(BF16)
    copies[3].wait()
    keys = (dot(normed, heads_in[1]) * covered).astype(BF16)
    copies[4].wait()
    values = (dot(normed, heads_in[2]) * covered).astype(BF16)
    copies[5].wait()
    back_out = dot(upstream, heads_out[...], (1, 1)).astype(BF16)
    proj[0] = keys
    proj[1] = query
    proj[2] = back_out

    low = first_heads(cells, 2 * LANES)
    chips = tied.shape[0]
    part = cells // chips

    def both_heads(array):
        return jnp.concatenate([jnp.where(low, array, 0), jnp.where(low, 0, array)], axis=0)

    for pair in range(half // LANES):
        logits = dot(both_heads(slab(query, pair)), slab(keys, pair), (1, 1))
        slopes = dot(both_heads(slab(back_out, pair)), slab(values, pair), (1, 1))
        for odd in range(2):
            here = slice(odd * cells, (odd + 1) * cells)
            both = jnp.concatenate(
                [
                    logits[here].reshape(chips, part, cells),
                    slopes[here].reshape(chips, part, cells),
                ],
                axis=1,
            )
            spot = (2 * pair + odd) * 2 * part
            tied[:, spot : spot + 2 * part, :] = both.astype(BF16)


def operand_kernel(weights, bounds, *refs, rows, col_dev):
    *raw, left, ops, heads, heads_back, sem = refs
    width = left.shape[1]
    half = width // CORES
    cells = bounds.shape[0]
    me, core, kind = position()
    first_col = lax.axis_index("pos") * col_dev
    fetches = []
    for at, source_of in ((0, 1), (1, 0), (3, 2)):
        copy = pltpu.make_async_copy(
            weights.at[source_of, :, head_lanes(core, half)], heads, sem
        )
        fetches.append((kind == at, copy))
    copy = pltpu.make_async_copy(weights.at[3, head_lanes(core, half), :], heads_back, sem)
    fetches.append((kind == 2, copy))
    for here, copy in fetches:
        pl.when(here)(copy.start)

    blocks, pieces = [], []
    for ref in raw:
        pieces.append(ref[...])
        if sum(piece.shape[0] for piece in pieces) == 2 * cells:
            blocks.append(jnp.concatenate(pieces, axis=0) if len(pieces) > 1 else pieces[0])
            pieces = []
    source, upstream = part_rows(blocks, rows, cells)
    normed = normalise(source)[0].astype(BF16)
    first, last = bounds[:, 0:1], bounds[:, 1:2]
    covered = jnp.concatenate(
        [
            row_mask(first, last, first_col + jnp.bitwise_xor(me, at))
            for at in range(2 * KINDS)
        ],
        axis=0,
    )
    for here, copy in fetches:
        pl.when(here)(copy.wait)

    @pl.when(kind == 2)
    def _():
        ops[...] = dot(upstream, heads_back[...], (1, 1)).astype(BF16)

    @pl.when(kind != 2)
    def _():
        ops[...] = (dot(normed, heads[...]) * covered).astype(BF16)

    @pl.when(kind == KINDS - 1)
    def _():
        left[...] = upstream

    @pl.when(kind < KINDS - 1)
    def _():
        left[...] = normed


def soften_kernel(parts, copies, *, scale, part):
    total = jnp.sum(parts[...].astype(F32), axis=0)
    blocks = total.reshape(-1, 2 * part, total.shape[-1])
    logits = blocks[:, :part] * scale
    slopes = blocks[:, part:]
    expon = jnp.exp(logits)
    probs = expon / jnp.sum(expon, -1, keepdims=True)
    mixed = scale * probs * (slopes - jnp.sum(probs * slopes, -1, keepdims=True))
    result = jnp.concatenate([probs, mixed], axis=1).reshape(total.shape).astype(BF16)
    for chip in range(copies.shape[0]):
        copies[chip] = result


def head_maps(pairs, head, cells):
    part = cells // pairs.shape[0]
    both = pairs[:, head * 2 * part : (head + 1) * 2 * part, :].astype(F32)
    return both[:, :part].reshape(cells, cells), both[:, part:].reshape(cells, cells)


def gradient_kernel(
    pairs, proj, bounds, ops, weights, left_far, own, other, product, spare, grads, right, heads_in,
    left, sems, *, col_dev
):
    cells = proj.shape[1] // 2
    half = proj.shape[2]
    me, core, kind = position()
    first_col = lax.axis_index("pos") * col_dev
    copies = [
        pltpu.make_async_copy(
            weights.at[at, :, head_lanes(core, half)], heads_in.at[at], sems.at[at]
        )
        for at in range(3)
    ]
    copies.append(pltpu.make_async_copy(left_far, left, sems.at[3]))
    for at in (3, 0, 1, 2):
        copies[at].start()
    first, last = bounds[:, 0:1], bounds[:, 1:2]
    masks = []
    for at in range(2 * KINDS):
        mask = row_mask(first, last, first_col + jnp.bitwise_xor(me, at))
        masks.append(jnp.broadcast_to(mask, (cells, LANES)))
    covered = jnp.concatenate(masks[:2], axis=1)
    plane_covered = jnp.where(kind == KINDS - 1, 1.0, jnp.concatenate(masks, axis=1))
    low = first_heads(cells, 2 * LANES)
    plane_low = first_heads(cells, 2 * KINDS * LANES)
    use_probs = kind >= 2
    use_flip = (kind == 1) | (kind == 2)

    for pair in range(half // LANES):
        lanes = slice(pair * LANES, (pair + 1) * LANES)

        def store(at, maps, operand):
            result = dot(jnp.concatenate(maps, axis=0), operand)
            result = (jnp.where(low, result[:cells], result[cells:]) * covered).astype(BF16)
            grads[at, :cells, lanes] = result[:, :LANES]
            grads[at, cells:, lanes] = result[:, LANES:]

        maps = [head_maps(pairs, 2 * pair + odd, cells) for odd in range(2)]
        flips = [(a.T, b.T) for a, b in maps]

        store(0, [b.astype(BF16) for _, b in maps], slab(proj[0], pair))
        store(1, [b.astype(BF16) for _, b in flips], slab(proj[1], pair))
        store(2, [a.astype(BF16) for a, _ in flips], slab(proj[2], pair))

        chosen = []
        for (a, b), (a_flip, b_flip) in zip(maps, flips):
            flat = jnp.where(use_probs, a, b)
            flip = jnp.where(use_probs, a_flip, b_flip)
            chosen.append(jnp.where(use_flip, flip, flat).astype(BF16))
        cat = jnp.concatenate(
            [ops[at : at + cells, lanes] for at in range(0, ops.shape[0], cells)], axis=1
        )
        result = dot(jnp.concatenate(chosen, axis=0), cat)
        result = jnp.where(plane_low, result[:cells], result[cells:]) * plane_covered
        result = result.astype(BF16)
        for at in range(2 * KINDS):
            right[at * cells : (at + 1) * cells, lanes] = result[
                :, at * LANES : (at + 1) * LANES
            ]

    copies[3].wait()

    @pl.when(kind < KINDS - 1)
    def _():
        product[...] = dot(left[...], right[...], (0, 0)).astype(BF16)

    @pl.when(kind == KINDS - 1)
    def _():
        rows = dot(right[...], left[...], (0, 0)).astype(BF16)

        @pl.when(core == 0)
        def _():
            product[:half] = rows[:, :half]
            spare[...] = rows[:, half:]

        @pl.when(core == 1)
        def _():
            product[:half] = rows[:, half:]
            spare[...] = rows[:, :half]

    total = None
    for at in range(3):
        copies[at].wait()
        term = dot(grads[at], heads_in[at], (1, 1))
        total = term if total is None else total + term
    own[...] = total[:cells]
    other[...] = total[cells:].astype(BF16)


def pack_kernel(grad_own, grad_recv, normed, bounds, product, spare, payload, *, rows):
    cells, width = normed.shape
    tiles = width // LANES
    half = product.shape[1]
    group = rows * tiles
    grad_norm = grad_own[...] + grad_recv[...].astype(F32)
    mean = jnp.mean(grad_norm * normed[...], -1, keepdims=True)
    result = (grad_norm - normed[...] * mean) * bounds[:, 2:3]
    result = result.astype(BF16)
    stack = jnp.concatenate(
        [result[:, t * LANES : (t + 1) * LANES] for t in range(tiles)], axis=0
    )

    def place(at, spot):
        tile, cell = lax.div(spot, cells), lax.rem(spot, cells)
        return at == lax.div(cell, rows) * group + tile * rows + lax.rem(cell, rows)

    _, core, kind = position()

    @pl.when((kind < KINDS - 1) | (core == 0))
    def _():
        payload[:half, :half] = product[:half]

    @pl.when(kind < KINDS - 1)
    def _():
        payload[half:, :half] = product[half:]

    @pl.when((kind == KINDS - 1) & (core == 0))
    def _():
        payload[half:, :half] = spare[...]

    @pl.when((kind == KINDS - 1) & (core == 1))
    def _():
        payload[:half, :half] = spare[...]
        payload[half:, :half] = product[:half]

    payload[:, half:] = dot(indicator(width, tiles * cells, place), stack).astype(BF16)


def finish_kernel(arrived, grad_input, sums):
    count, chunk, wide = arrived.shape
    rows, cols, width = grad_input.shape
    half = wide - LANES
    group = KINDS * CORES
    for kind in range(KINDS):
        for core in range(CORES):
            total = None
            for base in range(0, count, group):
                term = arrived[base + kind * CORES + core, :, :half].astype(F32)
                total = term if total is None else total + term
            spot = kind * width + core * half
            sums[:, spot : spot + half] = total
    flat = arrived[:, :, half:].astype(F32).reshape(count * chunk, LANES).astype(BF16)
    cells = rows * cols

    def place(at, spot):
        tile, cell = lax.div(at, cells), lax.rem(at, cells)
        return spot == lax.rem(cell, cols) * chunk + tile * rows + lax.div(cell, cols)

    tiles = width // LANES
    moved = dot(indicator(tiles * cells, count * chunk, place), flat).astype(BF16)
    for tile in range(tiles):
        for row in range(rows):
            spot = tile * cells + row * cols
            grad_input[row, :, tile * LANES : (tile + 1) * LANES] = moved[spot : spot + cols]


def exchange(array, groups):
    return lax.all_to_all(
        array, "read", split_axis=0, concat_axis=0, tiled=True, axis_index_groups=groups
    )


def call(kernel, args, outs, mib, far=(), scratch=(), cost=None):
    args = [
        pltpu.with_memory_space_constraint(arg, pltpu.HBM) if at in far else arg
        for at, arg in enumerate(args)
    ]
    near, away = (pl.BlockSpec(memory_space=space) for space in (pltpu.VMEM, pltpu.HBM))
    return pl.pallas_call(
        kernel,
        in_specs=[away if at in far else near for at in range(len(args))],
        out_specs=jax.tree.map(lambda _: near, outs),
        out_shape=outs,
        scratch_shapes=scratch,
        cost_estimate=cost,
        compiler_params=pltpu.CompilerParams(vmem_limit_bytes=mib * MIB),
    )(*args)


def shards(features, grad_out, weights, read_start, read_end):
    rows, col_dev, width = features.shape
    count = lax.axis_size("read")
    pos_count = lax.axis_size("pos")
    scale = 1.0 / math.sqrt(HEAD_DIM * col_dev * pos_count)
    reads = rows * count
    chips = count // CORES
    half = width // CORES
    part = reads // chips
    tied_rows = (HEADS // CORES) * 2 * part
    chunk = width // count
    start = read_start.reshape(1, reads)
    end = read_end.reshape(1, reads)

    same_core = [list(range(c, count, CORES)) for c in range(CORES)]

    def swap(array, bits):
        return lax.ppermute(array, "read", [(i, i ^ bits) for i in range(count)])

    shape = jax.ShapeDtypeStruct
    send = jnp.stack([features, grad_out]).transpose(2, 0, 1, 3).reshape(-1, width)
    own = exchange(send, None)
    other = swap(own, 1)
    proj, tied, normed, bounds = call(
        functools.partial(project_kernel, rows=rows, col_dev=col_dev),
        (own, other, weights, start, end),
        (
            shape((KINDS - 1, 2 * reads, half), BF16),
            shape((chips, tied_rows, reads), BF16),
            shape((reads, width), F32),
            shape((reads, LANES), F32),
        ),
        20,
        (2, 3, 4),
        [
            pltpu.VMEM((3, width, half), BF16),
            pltpu.VMEM((half, width), BF16),
            pltpu.VMEM((1, reads), jnp.int32),
            pltpu.VMEM((1, reads), jnp.int32),
            pltpu.SemaphoreType.DMA((6,)),
        ],
    )

    parts = exchange(tied, same_core)
    raw = {1: swap(own, CORES), 2: swap(own, 2 * CORES)}
    if pos_count > 1:
        parts = lax.psum(jnp.sum(parts.astype(F32), 0, keepdims=True), "pos")
    copies = call(
        functools.partial(soften_kernel, scale=scale, part=part),
        (parts,),
        shape((chips, tied_rows, reads), BF16),
        8,
    )
    held_bounds = bounds
    pairs = exchange(copies, same_core)
    diagonal = [swap(raw[1][:reads], 2 * CORES), swap(raw[2][reads:], CORES)]

    blocks = [own, other]
    for near in (raw[1], raw[2]):
        blocks += [near, swap(near, 1)]
    blocks += [*diagonal, *[swap(a, 1) for a in diagonal]]
    cells = 2 * KINDS * reads
    left, ops = call(
        functools.partial(operand_kernel, rows=rows, col_dev=col_dev),
        (weights, held_bounds, *blocks),
        (shape((cells, width), BF16), shape((cells, half), BF16)),
        24,
        (0,),
        [
            pltpu.VMEM((width, half), BF16),
            pltpu.VMEM((half, width), BF16),
            pltpu.SemaphoreType.DMA,
        ],
        pl.CostEstimate(flops=16 * 10**9, bytes_accessed=8 * MIB, transcendentals=0),
    )

    grad_own, grad_other, product, spare = call(
        functools.partial(gradient_kernel, col_dev=col_dev),
        (pairs, proj, bounds, ops, weights, left),
        (
            shape((reads, width), F32),
            shape((reads, width), BF16),
            shape((width, half), BF16),
            shape((half, half), BF16),
        ),
        24,
        (4, 5),
        [
            pltpu.VMEM((3, 2 * reads, half), BF16),
            pltpu.VMEM((cells, half), BF16),
            pltpu.VMEM((3, width, half), BF16),
            pltpu.VMEM((cells, width), BF16),
            pltpu.SemaphoreType.DMA((4,)),
        ],
    )
    grad_recv = swap(grad_other, 1)
    spare = swap(spare, 1)
    payload = call(
        functools.partial(pack_kernel, rows=rows),
        (grad_own, grad_recv, normed, bounds, product, spare),
        shape((width, half + LANES), BF16),
        8,
    )
    arrived = exchange(payload.reshape(count, chunk, half + LANES), None)
    grad_input, sums = call(
        finish_kernel,
        (arrived,),
        (shape((rows, col_dev, width), BF16), shape((chunk, KINDS * width), F32)),
        8,
    )
    weight_grads = lax.psum_scatter(sums, "pos", scatter_dimension=0, tiled=True)
    return (grad_input, weight_grads)


def solution(mesh):
    in_specs = (P("read", "pos", None), P("read", "pos", None), P(), P(), P())
    out_specs = (P("read", "pos", None), P(("read", "pos"), None))
    return jax.shard_map(shards, mesh=mesh, in_specs=in_specs, out_specs=out_specs, check_vma=False)
```

```python
import functools
import math

import jax
import jax.numpy as jnp
from jax import lax
from jax.experimental import pallas as pl
from jax.experimental.pallas import tpu as pltpu
from jax.sharding import PartitionSpec as P

HEADS = 12
HEAD_DIM = 64
CORES = 2
KINDS = 4
LANES = 128
MIB = 1024 * 1024

BF16 = jnp.bfloat16
F32 = jnp.float32


def dot(left, right, contract=(1, 0)):
    return lax.dot_general(
        left, right, (((contract[0],), (contract[1],)), ((), ())), preferred_element_type=F32
    )


def upright(lanes):
    size = lanes.shape[1]
    rows = lax.broadcasted_iota(jnp.int32, (size, size), 0)
    cols = lax.broadcasted_iota(jnp.int32, (size, size), 1)
    spread = jnp.broadcast_to(lanes.astype(F32), (size, size))
    return jnp.sum(jnp.where(rows == cols, spread, 0.0), -1, keepdims=True)


def row_mask(start, end, column):
    column = column.astype(F32)
    return ((start <= column) & (column < end)).astype(F32)


def first_heads(rows, lanes):
    at = lax.broadcasted_iota(jnp.int32, (rows, lanes), 1)
    return lax.rem(at, LANES) < HEAD_DIM


def slab(array, at):
    reads = array.shape[0] // 2
    lanes = slice(at * LANES, (at + 1) * LANES)
    return jnp.concatenate([array[:reads, lanes], array[reads:, lanes]], axis=1)


def indicator(rows, cols, place):
    at = lax.broadcasted_iota(jnp.int32, (rows, cols), 0)
    spot = lax.broadcasted_iota(jnp.int32, (rows, cols), 1)
    return place(at, spot).astype(F32).astype(BF16)


def position():
    me = lax.axis_index("read")
    core = jnp.bitwise_and(me, CORES - 1)
    kind = jnp.bitwise_and(jnp.right_shift(me, 1), KINDS - 1)
    return me, core, kind


def head_lanes(core, half):
    return pl.ds(pl.multiple_of(core * half, LANES), half)


def part_rows(arrived, rows, cells):
    def pick(shift):
        return indicator(
            cells,
            2 * cells,
            lambda at, spot: spot == lax.div(at, rows) * (2 * rows) + lax.rem(at, rows) + shift,
        )

    both = jnp.concatenate(arrived, axis=1)
    width = arrived[0].shape[1]
    source, upstream = dot(pick(0), both), dot(pick(rows), both).astype(BF16)

    def stack(array):
        return jnp.concatenate(
            [array[:, at * width : (at + 1) * width] for at in range(len(arrived))], axis=0
        )

    return stack(source), stack(upstream)


def normalise(source):
    inverse = lax.rsqrt(jnp.mean(source * source, -1, keepdims=True) + 1e-05)
    return source * inverse, inverse


def arrange_kernel(
    features, grad_out, weights, start, end, send, heads_in, heads_out, bounds, arrived, start_here,
    end_here, sems
):
    rows, cols, width = features.shape
    half = width // CORES
    _, core, _ = position()
    copies = [
        pltpu.make_async_copy(features, arrived.at[0], sems.at[0]),
        pltpu.make_async_copy(grad_out, arrived.at[1], sems.at[1]),
        pltpu.make_async_copy(start, start_here, sems.at[2]),
        pltpu.make_async_copy(end, end_here, sems.at[3]),
        pltpu.make_async_copy(
            weights.at[pl.ds(0, 3), :, head_lanes(core, half)], heads_in, sems.at[4]
        ),
        pltpu.make_async_copy(weights.at[3, head_lanes(core, half), :], heads_out, sems.at[5]),
    ]
    for copy in copies:
        copy.start()
    cells = rows * cols

    def place(at, spot):
        return spot == lax.rem(at, 2 * rows) * cols + lax.div(at, 2 * rows)

    order = indicator(2 * cells, 2 * cells, place)
    copies[0].wait()
    copies[1].wait()
    send[...] = dot(order, arrived[...].reshape(2 * cells, width)).astype(BF16)
    copies[2].wait()
    copies[3].wait()
    first, last = upright(start_here[...]), upright(end_here[...])
    lane = lax.broadcasted_iota(jnp.int32, bounds.shape, 1)
    bounds[...] = jnp.where(lane == 0, first, last)
    copies[4].wait()
    copies[5].wait()


def project_kernel(
    own, other, heads_in, heads_out, bounds, proj, tied, normed_own, scales, *, rows, col_dev
):
    cells = own.shape[0] // 2
    half = own.shape[1] // CORES
    me, _, _ = position()
    first_col = lax.axis_index("pos") * col_dev
    source, upstream = part_rows([own[...], other[...]], rows, cells)
    normed32, inverse = normalise(source)
    normed = normed32.astype(BF16)
    normed_own[...] = normed32[:cells]
    first, last = bounds[:, 0:1], bounds[:, 1:2]
    lane = lax.broadcasted_iota(jnp.int32, scales.shape, 1)
    scales[...] = jnp.where(lane == 0, first, jnp.where(lane == 1, last, inverse[:cells]))
    covered = jnp.concatenate(
        [
            row_mask(first, last, first_col + me),
            row_mask(first, last, first_col + jnp.bitwise_xor(me, 1)),
        ],
        axis=0,
    )
    query = (dot(normed, heads_in[0]) * covered).astype(BF16)
    keys = (dot(normed, heads_in[1]) * covered).astype(BF16)
    values = (dot(normed, heads_in[2]) * covered).astype(BF16)
    back_out = dot(upstream, heads_out[...], (1, 1)).astype(BF16)
    proj[0] = keys
    proj[1] = query
    proj[2] = back_out

    low = first_heads(cells, 2 * LANES)
    chips = tied.shape[0]
    part = cells // chips

    def both_heads(array):
        return jnp.concatenate([jnp.where(low, array, 0), jnp.where(low, 0, array)], axis=0)

    for pair in range(half // LANES):
        logits = dot(both_heads(slab(query, pair)), slab(keys, pair), (1, 1))
        slopes = dot(both_heads(slab(back_out, pair)), slab(values, pair), (1, 1))
        for odd in range(2):
            here = slice(odd * cells, (odd + 1) * cells)
            both = jnp.concatenate(
                [
                    logits[here].reshape(chips, part, cells),
                    slopes[here].reshape(chips, part, cells),
                ],
                axis=1,
            )
            spot = (2 * pair + odd) * 2 * part
            tied[:, spot : spot + 2 * part, :] = both.astype(BF16)


def operand_kernel(weights, bounds, *refs, rows, col_dev):
    *raw, left, ops, heads, heads_back, sem = refs
    width = left.shape[1]
    half = width // CORES
    cells = bounds.shape[0]
    me, core, kind = position()
    first_col = lax.axis_index("pos") * col_dev
    fetches = []
    for at, source_of in ((0, 1), (1, 0), (3, 2)):
        copy = pltpu.make_async_copy(
            weights.at[source_of, :, head_lanes(core, half)], heads, sem
        )
        fetches.append((kind == at, copy))
    copy = pltpu.make_async_copy(weights.at[3, head_lanes(core, half), :], heads_back, sem)
    fetches.append((kind == 2, copy))
    for here, copy in fetches:
        pl.when(here)(copy.start)

    blocks, pieces = [], []
    for ref in raw:
        pieces.append(ref[...])
        if sum(piece.shape[0] for piece in pieces) == 2 * cells:
            blocks.append(jnp.concatenate(pieces, axis=0) if len(pieces) > 1 else pieces[0])
            pieces = []
    source, upstream = part_rows(blocks, rows, cells)
    normed = normalise(source)[0].astype(BF16)
    first, last = bounds[:, 0:1], bounds[:, 1:2]
    covered = jnp.concatenate(
        [
            row_mask(first, last, first_col + jnp.bitwise_xor(me, at))
            for at in range(2 * KINDS)
        ],
        axis=0,
    )
    for here, copy in fetches:
        pl.when(here)(copy.wait)

    @pl.when(kind == 2)
    def _():
        ops[...] = dot(upstream, heads_back[...], (1, 1)).astype(BF16)

    @pl.when(kind != 2)
    def _():
        ops[...] = (dot(normed, heads[...]) * covered).astype(BF16)

    @pl.when(kind == KINDS - 1)
    def _():
        left[...] = upstream

    @pl.when(kind < KINDS - 1)
    def _():
        left[...] = normed


def soften_kernel(parts, copies, *, scale, part):
    total = jnp.sum(parts[...].astype(F32), axis=0)
    blocks = total.reshape(-1, 2 * part, total.shape[-1])
    logits = blocks[:, :part] * scale
    slopes = blocks[:, part:]
    expon = jnp.exp(logits)
    probs = expon / jnp.sum(expon, -1, keepdims=True)
    mixed = scale * probs * (slopes - jnp.sum(probs * slopes, -1, keepdims=True))
    result = jnp.concatenate([probs, mixed], axis=1).reshape(total.shape).astype(BF16)
    for chip in range(copies.shape[0]):
        copies[chip] = result


def head_maps(pairs, head, cells):
    part = cells // pairs.shape[0]
    both = pairs[:, head * 2 * part : (head + 1) * 2 * part, :].astype(F32)
    return both[:, :part].reshape(cells, cells), both[:, part:].reshape(cells, cells)


def gradient_kernel(
    pairs, proj, bounds, ops, weights, left_far, own, other, product, spare, grads, right, heads_in,
    left, sems, *, col_dev
):
    cells = proj.shape[1] // 2
    half = proj.shape[2]
    me, core, kind = position()
    first_col = lax.axis_index("pos") * col_dev
    copies = [
        pltpu.make_async_copy(
            weights.at[at, :, head_lanes(core, half)], heads_in.at[at], sems.at[at]
        )
        for at in range(3)
    ]
    copies.append(pltpu.make_async_copy(left_far, left, sems.at[3]))
    for at in (3, 0, 1, 2):
        copies[at].start()
    first, last = bounds[:, 0:1], bounds[:, 1:2]
    masks = []
    for at in range(2 * KINDS):
        mask = row_mask(first, last, first_col + jnp.bitwise_xor(me, at))
        masks.append(jnp.broadcast_to(mask, (cells, LANES)))
    covered = jnp.concatenate(masks[:2], axis=1)
    plane_covered = jnp.where(kind == KINDS - 1, 1.0, jnp.concatenate(masks, axis=1))
    low = first_heads(cells, 2 * LANES)
    plane_low = first_heads(cells, 2 * KINDS * LANES)
    use_probs = kind >= 2
    use_flip = (kind == 1) | (kind == 2)

    for pair in range(half // LANES):
        lanes = slice(pair * LANES, (pair + 1) * LANES)

        def store(at, maps, operand):
            result = dot(jnp.concatenate(maps, axis=0), operand)
            result = (jnp.where(low, result[:cells], result[cells:]) * covered).astype(BF16)
            grads[at, :cells, lanes] = result[:, :LANES]
            grads[at, cells:, lanes] = result[:, LANES:]

        maps = [head_maps(pairs, 2 * pair + odd, cells) for odd in range(2)]
        flips = [(a.T, b.T) for a, b in maps]

        store(0, [b.astype(BF16) for _, b in maps], slab(proj[0], pair))
        store(1, [b.astype(BF16) for _, b in flips], slab(proj[1], pair))
        store(2, [a.astype(BF16) for a, _ in flips], slab(proj[2], pair))

        chosen = []
        for (a, b), (a_flip, b_flip) in zip(maps, flips):
            flat = jnp.where(use_probs, a, b)
            flip = jnp.where(use_probs, a_flip, b_flip)
            chosen.append(jnp.where(use_flip, flip, flat).astype(BF16))
        cat = jnp.concatenate(
            [ops[at : at + cells, lanes] for at in range(0, ops.shape[0], cells)], axis=1
        )
        result = dot(jnp.concatenate(chosen, axis=0), cat)
        result = jnp.where(plane_low, result[:cells], result[cells:]) * plane_covered
        result = result.astype(BF16)
        for at in range(2 * KINDS):
            right[at * cells : (at + 1) * cells, lanes] = result[
                :, at * LANES : (at + 1) * LANES
            ]

    copies[3].wait()

    @pl.when(kind < KINDS - 1)
    def _():
        product[...] = dot(left[...], right[...], (0, 0)).astype(BF16)

    @pl.when(kind == KINDS - 1)
    def _():
        rows = dot(right[...], left[...], (0, 0)).astype(BF16)

        @pl.when(core == 0)
        def _():
            product[:half] = rows[:, :half]
            spare[...] = rows[:, half:]

        @pl.when(core == 1)
        def _():
            product[:half] = rows[:, half:]
            spare[...] = rows[:, :half]

    total = None
    for at in range(3):
        copies[at].wait()
        term = dot(grads[at], heads_in[at], (1, 1))
        total = term if total is None else total + term
    own[...] = total[:cells]
    other[...] = total[cells:].astype(BF16)


def pack_kernel(grad_own, grad_recv, normed, bounds, product, spare, payload, *, rows):
    cells, width = normed.shape
    tiles = width // LANES
    half = product.shape[1]
    group = rows * tiles
    grad_norm = grad_own[...] + grad_recv[...].astype(F32)
    mean = jnp.mean(grad_norm * normed[...], -1, keepdims=True)
    result = (grad_norm - normed[...] * mean) * bounds[:, 2:3]
    result = result.astype(BF16)
    stack = jnp.concatenate(
        [result[:, t * LANES : (t + 1) * LANES] for t in range(tiles)], axis=0
    )

    def place(at, spot):
        tile, cell = lax.div(spot, cells), lax.rem(spot, cells)
        return at == lax.div(cell, rows) * group + tile * rows + lax.rem(cell, rows)

    _, core, kind = position()

    @pl.when((kind < KINDS - 1) | (core == 0))
    def _():
        payload[:half, :half] = product[:half]

    @pl.when(kind < KINDS - 1)
    def _():
        payload[half:, :half] = product[half:]

    @pl.when((kind == KINDS - 1) & (core == 0))
    def _():
        payload[half:, :half] = spare[...]

    @pl.when((kind == KINDS - 1) & (core == 1))
    def _():
        payload[:half, :half] = spare[...]
        payload[half:, :half] = product[:half]

    payload[:, half:] = dot(indicator(width, tiles * cells, place), stack).astype(BF16)


def finish_kernel(arrived, grad_input, sums):
    count, chunk, wide = arrived.shape
    rows, cols, width = grad_input.shape
    half = wide - LANES
    group = KINDS * CORES
    for kind in range(KINDS):
        for core in range(CORES):
            total = None
            for base in range(0, count, group):
                term = arrived[base + kind * CORES + core, :, :half].astype(F32)
                total = term if total is None else total + term
            spot = kind * width + core * half
            sums[:, spot : spot + half] = total
    flat = arrived[:, :, half:].astype(F32).reshape(count * chunk, LANES).astype(BF16)
    cells = rows * cols

    def place(at, spot):
        tile, cell = lax.div(at, cells), lax.rem(at, cells)
        return spot == lax.rem(cell, cols) * chunk + tile * rows + lax.div(cell, cols)

    tiles = width // LANES
    moved = dot(indicator(tiles * cells, count * chunk, place), flat).astype(BF16)
    for tile in range(tiles):
        for row in range(rows):
            spot = tile * cells + row * cols
            grad_input[row, :, tile * LANES : (tile + 1) * LANES] = moved[spot : spot + cols]


def exchange(array, groups):
    return lax.all_to_all(
        array, "read", split_axis=0, concat_axis=0, tiled=True, axis_index_groups=groups
    )


def call(kernel, args, outs, mib, far=(), scratch=(), cost=None):
    args = [
        pltpu.with_memory_space_constraint(arg, pltpu.HBM) if at in far else arg
        for at, arg in enumerate(args)
    ]
    near, away = (pl.BlockSpec(memory_space=space) for space in (pltpu.VMEM, pltpu.HBM))
    return pl.pallas_call(
        kernel,
        in_specs=[away if at in far else near for at in range(len(args))],
        out_specs=jax.tree.map(lambda _: near, outs),
        out_shape=outs,
        scratch_shapes=scratch,
        cost_estimate=cost,
        compiler_params=pltpu.CompilerParams(vmem_limit_bytes=mib * MIB),
    )(*args)


def shards(features, grad_out, weights, read_start, read_end):
    rows, col_dev, width = features.shape
    count = lax.axis_size("read")
    pos_count = lax.axis_size("pos")
    scale = 1.0 / math.sqrt(HEAD_DIM * col_dev * pos_count)
    reads = rows * count
    chips = count // CORES
    half = width // CORES
    part = reads // chips
    tied_rows = (HEADS // CORES) * 2 * part
    chunk = width // count
    start = read_start.reshape(1, reads)
    end = read_end.reshape(1, reads)

    same_core = [list(range(c, count, CORES)) for c in range(CORES)]

    def swap(array, bits):
        return lax.ppermute(array, "read", [(i, i ^ bits) for i in range(count)])

    shape = jax.ShapeDtypeStruct
    send, heads_in, heads_out, bounds = call(
        arrange_kernel,
        (features, grad_out, weights, start, end),
        (
            shape((2 * reads, width), BF16),
            shape((3, width, half), BF16),
            shape((half, width), BF16),
            shape((reads, LANES), F32),
        ),
        8,
        (0, 1, 2, 3, 4),
        [
            pltpu.VMEM((2, *features.shape), BF16),
            pltpu.VMEM((1, reads), jnp.int32),
            pltpu.VMEM((1, reads), jnp.int32),
            pltpu.SemaphoreType.DMA((6,)),
        ],
    )
    own = exchange(send.reshape(count, 2 * rows, width), None).reshape(send.shape)
    other = swap(own, 1)
    proj, tied, normed, bounds = call(
        functools.partial(project_kernel, rows=rows, col_dev=col_dev),
        (own, other, heads_in, heads_out, bounds),
        (
            shape((KINDS - 1, 2 * reads, half), BF16),
            shape((chips, tied_rows, reads), BF16),
            shape((reads, width), F32),
            shape((reads, LANES), F32),
        ),
        16,
    )

    parts = exchange(tied, same_core)
    raw = {1: swap(own, CORES), 2: swap(own, 2 * CORES)}
    if pos_count > 1:
        parts = lax.psum(jnp.sum(parts.astype(F32), 0, keepdims=True), "pos")
    copies = call(
        functools.partial(soften_kernel, scale=scale, part=part),
        (parts,),
        shape((chips, tied_rows, reads), BF16),
        8,
    )
    held_bounds = bounds
    pairs = exchange(copies, same_core)
    diagonal = [swap(raw[1][:reads], 2 * CORES), swap(raw[2][reads:], CORES)]

    blocks = [own, other]
    for near in (raw[1], raw[2]):
        blocks += [near, swap(near, 1)]
    blocks += [*diagonal, *[swap(a, 1) for a in diagonal]]
    cells = 2 * KINDS * reads
    left, ops = call(
        functools.partial(operand_kernel, rows=rows, col_dev=col_dev),
        (weights, held_bounds, *blocks),
        (shape((cells, width), BF16), shape((cells, half), BF16)),
        24,
        (0,),
        [
            pltpu.VMEM((width, half), BF16),
            pltpu.VMEM((half, width), BF16),
            pltpu.SemaphoreType.DMA,
        ],
        pl.CostEstimate(flops=16 * 10**9, bytes_accessed=8 * MIB, transcendentals=0),
    )

    grad_own, grad_other, product, spare = call(
        functools.partial(gradient_kernel, col_dev=col_dev),
        (pairs, proj, bounds, ops, weights, left),
        (
            shape((reads, width), F32),
            shape((reads, width), BF16),
            shape((width, half), BF16),
            shape((half, half), BF16),
        ),
        24,
        (4, 5),
        [
            pltpu.VMEM((3, 2 * reads, half), BF16),
            pltpu.VMEM((cells, half), BF16),
            pltpu.VMEM((3, width, half), BF16),
            pltpu.VMEM((cells, width), BF16),
            pltpu.SemaphoreType.DMA((4,)),
        ],
    )
    grad_recv = swap(grad_other, 1)
    spare = swap(spare, 1)
    payload = call(
        functools.partial(pack_kernel, rows=rows),
        (grad_own, grad_recv, normed, bounds, product, spare),
        shape((width, half + LANES), BF16),
        8,
    )
    arrived = exchange(payload.reshape(count, chunk, half + LANES), None)
    grad_input, sums = call(
        finish_kernel,
        (arrived,),
        (shape((rows, col_dev, width), BF16), shape((chunk, KINDS * width), F32)),
        8,
    )
    weight_grads = lax.psum_scatter(sums, "pos", scatter_dimension=0, tiled=True)
    return (grad_input, weight_grads)


def solution(mesh):
    in_specs = (P("read", "pos", None), P("read", "pos", None), P(), P(), P())
    out_specs = (P("read", "pos", None), P(("read", "pos"), None))
    return jax.shard_map(shards, mesh=mesh, in_specs=in_specs, out_specs=out_specs, check_vma=False)
```

```python
import functools
import math

import jax
import jax.numpy as jnp
from jax import lax
from jax.experimental import pallas as pl
from jax.experimental.pallas import tpu as pltpu
from jax.sharding import PartitionSpec as P

HEADS = 12
HEAD_DIM = 64
CORES = 2
KINDS = 4
LANES = 128
MIB = 1024 * 1024

BF16 = jnp.bfloat16
F16 = jnp.float16
LOGIT_UNIT = 2.0
SLOPE_UNIT = 1024.0
F32 = jnp.float32


def dot(left, right, contract=(1, 0)):
    return lax.dot_general(
        left, right, (((contract[0],), (contract[1],)), ((), ())), preferred_element_type=F32
    )


def upright(lanes):
    size = lanes.shape[1]
    rows = lax.broadcasted_iota(jnp.int32, (size, size), 0)
    cols = lax.broadcasted_iota(jnp.int32, (size, size), 1)
    spread = jnp.broadcast_to(lanes.astype(F32), (size, size))
    return jnp.sum(jnp.where(rows == cols, spread, 0.0), -1, keepdims=True)


def row_mask(start, end, column):
    column = column.astype(F32)
    return ((start <= column) & (column < end)).astype(F32)


def first_heads(rows, lanes):
    at = lax.broadcasted_iota(jnp.int32, (rows, lanes), 1)
    return lax.rem(at, LANES) < HEAD_DIM


def slab(array, at):
    reads = array.shape[0] // 2
    lanes = slice(at * LANES, (at + 1) * LANES)
    return jnp.concatenate([array[:reads, lanes], array[reads:, lanes]], axis=1)


def indicator(rows, cols, place):
    at = lax.broadcasted_iota(jnp.int32, (rows, cols), 0)
    spot = lax.broadcasted_iota(jnp.int32, (rows, cols), 1)
    return place(at, spot).astype(F32).astype(BF16)


def position():
    me = lax.axis_index("read")
    core = jnp.bitwise_and(me, CORES - 1)
    kind = jnp.bitwise_and(jnp.right_shift(me, 1), KINDS - 1)
    return me, core, kind


def head_lanes(core, half):
    return pl.ds(pl.multiple_of(core * half, LANES), half)


def part_rows(arrived, rows, cells):
    def pick(shift):
        return indicator(
            cells,
            2 * cells,
            lambda at, spot: spot == lax.div(at, rows) * (2 * rows) + lax.rem(at, rows) + shift,
        )

    both = jnp.concatenate(arrived, axis=1)
    width = arrived[0].shape[1]
    source, upstream = dot(pick(0), both), dot(pick(rows), both).astype(BF16)

    def stack(array):
        return jnp.concatenate(
            [array[:, at * width : (at + 1) * width] for at in range(len(arrived))], axis=0
        )

    return stack(source), stack(upstream)


def normalise(source):
    inverse = lax.rsqrt(jnp.mean(source * source, -1, keepdims=True) + 1e-05)
    return source * inverse, inverse


def arrange_kernel(
    features, grad_out, weights, start, end, send, heads_in, heads_out, bounds, arrived, start_here,
    end_here, sems
):
    rows, cols, width = features.shape
    half = width // CORES
    _, core, _ = position()
    copies = [
        pltpu.make_async_copy(features, arrived.at[0], sems.at[0]),
        pltpu.make_async_copy(grad_out, arrived.at[1], sems.at[1]),
        pltpu.make_async_copy(start, start_here, sems.at[2]),
        pltpu.make_async_copy(end, end_here, sems.at[3]),
        pltpu.make_async_copy(
            weights.at[pl.ds(0, 3), :, head_lanes(core, half)], heads_in, sems.at[4]
        ),
        pltpu.make_async_copy(weights.at[3, head_lanes(core, half), :], heads_out, sems.at[5]),
    ]
    for copy in copies:
        copy.start()
    cells = rows * cols

    def place(at, spot):
        return spot == lax.rem(at, 2 * rows) * cols + lax.div(at, 2 * rows)

    order = indicator(2 * cells, 2 * cells, place)
    copies[0].wait()
    copies[1].wait()
    send[...] = dot(order, arrived[...].reshape(2 * cells, width)).astype(BF16)
    copies[2].wait()
    copies[3].wait()
    first, last = upright(start_here[...]), upright(end_here[...])
    lane = lax.broadcasted_iota(jnp.int32, bounds.shape, 1)
    bounds[...] = jnp.where(lane == 0, first, last)
    copies[4].wait()
    copies[5].wait()


def project_kernel(
    own, other, heads_in, heads_out, bounds, proj, tied, normed_own, scales, *, rows, col_dev,
    scale
):
    cells = own.shape[0] // 2
    half = own.shape[1] // CORES
    me, _, _ = position()
    first_col = lax.axis_index("pos") * col_dev
    source, upstream = part_rows([own[...], other[...]], rows, cells)
    normed32, inverse = normalise(source)
    normed = normed32.astype(BF16)
    normed_own[...] = normed32[:cells]
    first, last = bounds[:, 0:1], bounds[:, 1:2]
    lane = lax.broadcasted_iota(jnp.int32, scales.shape, 1)
    scales[...] = jnp.where(lane == 0, first, jnp.where(lane == 1, last, inverse[:cells]))
    covered = jnp.concatenate(
        [
            row_mask(first, last, first_col + me),
            row_mask(first, last, first_col + jnp.bitwise_xor(me, 1)),
        ],
        axis=0,
    )
    query = (dot(normed, heads_in[0]) * covered).astype(BF16)
    keys = (dot(normed, heads_in[1]) * covered).astype(BF16)
    values = (dot(normed, heads_in[2]) * covered).astype(BF16)
    back_out = dot(upstream, heads_out[...], (1, 1)).astype(BF16)
    proj[0] = keys
    proj[1] = query
    proj[2] = back_out

    low = first_heads(cells, 2 * LANES)
    chips = tied.shape[0]
    part = cells // chips

    def both_heads(array):
        return jnp.concatenate([jnp.where(low, array, 0), jnp.where(low, 0, array)], axis=0)

    for pair in range(half // LANES):
        logits = dot(both_heads(slab(query, pair)), slab(keys, pair), (1, 1))
        slopes = dot(both_heads(slab(back_out, pair)), slab(values, pair), (1, 1))
        for odd in range(2):
            here = slice(odd * cells, (odd + 1) * cells)
            both = jnp.concatenate(
                [
                    (logits[here] * (scale / LOGIT_UNIT)).reshape(chips, part, cells),
                    (slopes[here] * (1.0 / SLOPE_UNIT)).reshape(chips, part, cells),
                ],
                axis=1,
            )
            spot = (2 * pair + odd) * 2 * part
            tied[:, spot : spot + 2 * part, :] = both


def operand_kernel(weights, bounds, *refs, rows, col_dev):
    *raw, left, ops, heads, heads_back, sem = refs
    width = left.shape[1]
    half = width // CORES
    cells = bounds.shape[0]
    me, core, kind = position()
    first_col = lax.axis_index("pos") * col_dev
    fetches = []
    for at, source_of in ((0, 1), (1, 0), (3, 2)):
        copy = pltpu.make_async_copy(
            weights.at[source_of, :, head_lanes(core, half)], heads, sem
        )
        fetches.append((kind == at, copy))
    copy = pltpu.make_async_copy(weights.at[3, head_lanes(core, half), :], heads_back, sem)
    fetches.append((kind == 2, copy))
    for here, copy in fetches:
        pl.when(here)(copy.start)

    blocks, pieces = [], []
    for ref in raw:
        pieces.append(ref[...])
        if sum(piece.shape[0] for piece in pieces) == 2 * cells:
            blocks.append(jnp.concatenate(pieces, axis=0) if len(pieces) > 1 else pieces[0])
            pieces = []
    source, upstream = part_rows(blocks, rows, cells)
    normed = normalise(source)[0].astype(BF16)
    first, last = bounds[:, 0:1], bounds[:, 1:2]
    covered = jnp.concatenate(
        [
            row_mask(first, last, first_col + jnp.bitwise_xor(me, at))
            for at in range(2 * KINDS)
        ],
        axis=0,
    )
    for here, copy in fetches:
        pl.when(here)(copy.wait)

    @pl.when(kind == 2)
    def _():
        ops[...] = dot(upstream, heads_back[...], (1, 1)).astype(BF16)

    @pl.when(kind != 2)
    def _():
        ops[...] = (dot(normed, heads[...]) * covered).astype(BF16)

    @pl.when(kind == KINDS - 1)
    def _():
        left[...] = upstream

    @pl.when(kind < KINDS - 1)
    def _():
        left[...] = normed


def soften_kernel(parts, copies, *, scale, part):
    total = jnp.sum(parts[...].astype(F32), axis=0)
    blocks = total.reshape(-1, 2 * part, total.shape[-1])
    logits = blocks[:, :part] * LOGIT_UNIT
    slopes = blocks[:, part:] * SLOPE_UNIT
    expon = jnp.exp(logits)
    probs = expon / jnp.sum(expon, -1, keepdims=True)
    mixed = scale * probs * (slopes - jnp.sum(probs * slopes, -1, keepdims=True))
    result = jnp.concatenate([probs, mixed], axis=1).reshape(total.shape).astype(BF16)
    for chip in range(copies.shape[0]):
        copies[chip] = result


def head_maps(pairs, head, cells):
    part = cells // pairs.shape[0]
    both = pairs[:, head * 2 * part : (head + 1) * 2 * part, :].astype(F32)
    return both[:, :part].reshape(cells, cells), both[:, part:].reshape(cells, cells)


def gradient_kernel(
    pairs, proj, bounds, ops, weights, left_far, own, other, product, spare, grads, right, heads_in,
    left, sems, *, col_dev
):
    cells = proj.shape[1] // 2
    half = proj.shape[2]
    me, core, kind = position()
    first_col = lax.axis_index("pos") * col_dev
    copies = [
        pltpu.make_async_copy(
            weights.at[at, :, head_lanes(core, half)], heads_in.at[at], sems.at[at]
        )
        for at in range(3)
    ]
    copies.append(pltpu.make_async_copy(left_far, left, sems.at[3]))
    for at in (3, 0, 1, 2):
        copies[at].start()
    first, last = bounds[:, 0:1], bounds[:, 1:2]
    masks = []
    for at in range(2 * KINDS):
        mask = row_mask(first, last, first_col + jnp.bitwise_xor(me, at))
        masks.append(jnp.broadcast_to(mask, (cells, LANES)))
    covered = jnp.concatenate(masks[:2], axis=1)
    plane_covered = jnp.where(kind == KINDS - 1, 1.0, jnp.concatenate(masks, axis=1))
    low = first_heads(cells, 2 * LANES)
    plane_low = first_heads(cells, 2 * KINDS * LANES)
    use_probs = kind >= 2
    use_flip = (kind == 1) | (kind == 2)

    for pair in range(half // LANES):
        lanes = slice(pair * LANES, (pair + 1) * LANES)

        def store(at, maps, operand):
            result = dot(jnp.concatenate(maps, axis=0), operand)
            result = (jnp.where(low, result[:cells], result[cells:]) * covered).astype(BF16)
            grads[at, :cells, lanes] = result[:, :LANES]
            grads[at, cells:, lanes] = result[:, LANES:]

        maps = [head_maps(pairs, 2 * pair + odd, cells) for odd in range(2)]
        flips = [(a.T, b.T) for a, b in maps]

        store(0, [b.astype(BF16) for _, b in maps], slab(proj[0], pair))
        store(1, [b.astype(BF16) for _, b in flips], slab(proj[1], pair))
        store(2, [a.astype(BF16) for a, _ in flips], slab(proj[2], pair))

        chosen = []
        for (a, b), (a_flip, b_flip) in zip(maps, flips):
            flat = jnp.where(use_probs, a, b)
            flip = jnp.where(use_probs, a_flip, b_flip)
            chosen.append(jnp.where(use_flip, flip, flat).astype(BF16))
        cat = jnp.concatenate(
            [ops[at : at + cells, lanes] for at in range(0, ops.shape[0], cells)], axis=1
        )
        result = dot(jnp.concatenate(chosen, axis=0), cat)
        result = jnp.where(plane_low, result[:cells], result[cells:]) * plane_covered
        result = result.astype(BF16)
        for at in range(2 * KINDS):
            right[at * cells : (at + 1) * cells, lanes] = result[
                :, at * LANES : (at + 1) * LANES
            ]

    copies[3].wait()

    @pl.when(kind < KINDS - 1)
    def _():
        product[...] = dot(left[...], right[...], (0, 0)).astype(BF16)

    @pl.when(kind == KINDS - 1)
    def _():
        rows = dot(right[...], left[...], (0, 0)).astype(BF16)

        @pl.when(core == 0)
        def _():
            product[:half] = rows[:, :half]
            spare[...] = rows[:, half:]

        @pl.when(core == 1)
        def _():
            product[:half] = rows[:, half:]
            spare[...] = rows[:, :half]

    total = None
    for at in range(3):
        copies[at].wait()
        term = dot(grads[at], heads_in[at], (1, 1))
        total = term if total is None else total + term
    own[...] = total[:cells]
    other[...] = total[cells:].astype(BF16)


def pack_kernel(grad_own, grad_recv, normed, bounds, product, spare, payload, *, rows):
    cells, width = normed.shape
    tiles = width // LANES
    half = product.shape[1]
    group = rows * tiles
    grad_norm = grad_own[...] + grad_recv[...].astype(F32)
    mean = jnp.mean(grad_norm * normed[...], -1, keepdims=True)
    result = (grad_norm - normed[...] * mean) * bounds[:, 2:3]
    result = result.astype(BF16)
    stack = jnp.concatenate(
        [result[:, t * LANES : (t + 1) * LANES] for t in range(tiles)], axis=0
    )

    def place(at, spot):
        tile, cell = lax.div(spot, cells), lax.rem(spot, cells)
        return at == lax.div(cell, rows) * group + tile * rows + lax.rem(cell, rows)

    _, core, kind = position()

    @pl.when((kind < KINDS - 1) | (core == 0))
    def _():
        payload[:half, :half] = product[:half]

    @pl.when(kind < KINDS - 1)
    def _():
        payload[half:, :half] = product[half:]

    @pl.when((kind == KINDS - 1) & (core == 0))
    def _():
        payload[half:, :half] = spare[...]

    @pl.when((kind == KINDS - 1) & (core == 1))
    def _():
        payload[:half, :half] = spare[...]
        payload[half:, :half] = product[:half]

    payload[:, half:] = dot(indicator(width, tiles * cells, place), stack).astype(BF16)


def finish_kernel(arrived, grad_input, sums):
    count, chunk, wide = arrived.shape
    rows, cols, width = grad_input.shape
    half = wide - LANES
    group = KINDS * CORES
    for kind in range(KINDS):
        for core in range(CORES):
            total = None
            for base in range(0, count, group):
                term = arrived[base + kind * CORES + core, :, :half].astype(F32)
                total = term if total is None else total + term
            spot = kind * width + core * half
            sums[:, spot : spot + half] = total
    flat = arrived[:, :, half:].astype(F32).reshape(count * chunk, LANES).astype(BF16)
    cells = rows * cols

    def place(at, spot):
        tile, cell = lax.div(at, cells), lax.rem(at, cells)
        return spot == lax.rem(cell, cols) * chunk + tile * rows + lax.div(cell, cols)

    tiles = width // LANES
    moved = dot(indicator(tiles * cells, count * chunk, place), flat).astype(BF16)
    for tile in range(tiles):
        for row in range(rows):
            spot = tile * cells + row * cols
            grad_input[row, :, tile * LANES : (tile + 1) * LANES] = moved[spot : spot + cols]


def exchange(array, groups):
    return lax.all_to_all(
        array, "read", split_axis=0, concat_axis=0, tiled=True, axis_index_groups=groups
    )


def call(kernel, args, outs, mib, far=(), scratch=(), cost=None):
    args = [
        pltpu.with_memory_space_constraint(arg, pltpu.HBM) if at in far else arg
        for at, arg in enumerate(args)
    ]
    near, away = (pl.BlockSpec(memory_space=space) for space in (pltpu.VMEM, pltpu.HBM))
    return pl.pallas_call(
        kernel,
        in_specs=[away if at in far else near for at in range(len(args))],
        out_specs=jax.tree.map(lambda _: near, outs),
        out_shape=outs,
        scratch_shapes=scratch,
        cost_estimate=cost,
        compiler_params=pltpu.CompilerParams(vmem_limit_bytes=mib * MIB),
    )(*args)


def shards(features, grad_out, weights, read_start, read_end):
    rows, col_dev, width = features.shape
    count = lax.axis_size("read")
    pos_count = lax.axis_size("pos")
    scale = 1.0 / math.sqrt(HEAD_DIM * col_dev * pos_count)
    reads = rows * count
    chips = count // CORES
    half = width // CORES
    part = reads // chips
    tied_rows = (HEADS // CORES) * 2 * part
    chunk = width // count
    start = read_start.reshape(1, reads)
    end = read_end.reshape(1, reads)

    same_core = [list(range(c, count, CORES)) for c in range(CORES)]

    def swap(array, bits):
        return lax.ppermute(array, "read", [(i, i ^ bits) for i in range(count)])

    shape = jax.ShapeDtypeStruct
    send, heads_in, heads_out, bounds = call(
        arrange_kernel,
        (features, grad_out, weights, start, end),
        (
            shape((2 * reads, width), BF16),
            shape((3, width, half), BF16),
            shape((half, width), BF16),
            shape((reads, LANES), F32),
        ),
        8,
        (0, 1, 2, 3, 4),
        [
            pltpu.VMEM((2, *features.shape), BF16),
            pltpu.VMEM((1, reads), jnp.int32),
            pltpu.VMEM((1, reads), jnp.int32),
            pltpu.SemaphoreType.DMA((6,)),
        ],
    )
    own = exchange(send.reshape(count, 2 * rows, width), None).reshape(send.shape)
    other = swap(own, 1)
    proj, tied, normed, bounds = call(
        functools.partial(project_kernel, rows=rows, col_dev=col_dev, scale=scale),
        (own, other, heads_in, heads_out, bounds),
        (
            shape((KINDS - 1, 2 * reads, half), BF16),
            shape((chips, tied_rows, reads), F32),
            shape((reads, width), F32),
            shape((reads, LANES), F32),
        ),
        16,
    )

    parts = exchange(tied.astype(F16), same_core)
    raw = {1: swap(own, CORES), 2: swap(own, 2 * CORES)}
    parts = parts.astype(F32)
    if pos_count > 1:
        parts = lax.psum(jnp.sum(parts, 0, keepdims=True), "pos")
    copies = call(
        functools.partial(soften_kernel, scale=scale, part=part),
        (parts,),
        shape((chips, tied_rows, reads), BF16),
        8,
    )
    held_bounds = bounds
    pairs = exchange(copies, same_core)
    diagonal = [swap(raw[1][:reads], 2 * CORES), swap(raw[2][reads:], CORES)]

    blocks = [own, other]
    for near in (raw[1], raw[2]):
        blocks += [near, swap(near, 1)]
    blocks += [*diagonal, *[swap(a, 1) for a in diagonal]]
    cells = 2 * KINDS * reads
    left, ops = call(
        functools.partial(operand_kernel, rows=rows, col_dev=col_dev),
        (weights, held_bounds, *blocks),
        (shape((cells, width), BF16), shape((cells, half), BF16)),
        24,
        (0,),
        [
            pltpu.VMEM((width, half), BF16),
            pltpu.VMEM((half, width), BF16),
            pltpu.SemaphoreType.DMA,
        ],
        pl.CostEstimate(flops=40 * 10**9, bytes_accessed=8 * MIB, transcendentals=0),
    )

    grad_own, grad_other, product, spare = call(
        functools.partial(gradient_kernel, col_dev=col_dev),
        (pairs, proj, bounds, ops, weights, left),
        (
            shape((reads, width), F32),
            shape((reads, width), BF16),
            shape((width, half), BF16),
            shape((half, half), BF16),
        ),
        24,
        (4, 5),
        [
            pltpu.VMEM((3, 2 * reads, half), BF16),
            pltpu.VMEM((cells, half), BF16),
            pltpu.VMEM((3, width, half), BF16),
            pltpu.VMEM((cells, width), BF16),
            pltpu.SemaphoreType.DMA((4,)),
        ],
    )
    grad_recv = swap(grad_other, 1)
    spare = swap(spare, 1)
    payload = call(
        functools.partial(pack_kernel, rows=rows),
        (grad_own, grad_recv, normed, bounds, product, spare),
        shape((width, half + LANES), BF16),
        8,
    )
    arrived = exchange(payload.reshape(count, chunk, half + LANES), None)
    grad_input, sums = call(
        finish_kernel,
        (arrived,),
        (shape((rows, col_dev, width), BF16), shape((chunk, KINDS * width), F32)),
        8,
    )
    weight_grads = lax.psum_scatter(sums, "pos", scatter_dimension=0, tiled=True)
    return (grad_input, weight_grads)


def solution(mesh):
    in_specs = (P("read", "pos", None), P("read", "pos", None), P(), P(), P())
    out_specs = (P("read", "pos", None), P(("read", "pos"), None))
    return jax.shard_map(shards, mesh=mesh, in_specs=in_specs, out_specs=out_specs, check_vma=False)
```

```python
import functools
import math

import jax
import jax.numpy as jnp
from jax import lax
from jax.experimental import pallas as pl
from jax.experimental.pallas import tpu as pltpu
from jax.sharding import PartitionSpec as P

HEADS = 12
HEAD_DIM = 64
CORES = 2
KINDS = 4
LANES = 128
MIB = 1024 * 1024

BF16 = jnp.bfloat16
F16 = jnp.float16
LOGIT_UNIT = 2.0
SLOPE_UNIT = 1024.0
F32 = jnp.float32


def dot(left, right, contract=(1, 0)):
    return lax.dot_general(
        left, right, (((contract[0],), (contract[1],)), ((), ())), preferred_element_type=F32
    )


def upright(lanes):
    size = lanes.shape[1]
    rows = lax.broadcasted_iota(jnp.int32, (size, size), 0)
    cols = lax.broadcasted_iota(jnp.int32, (size, size), 1)
    spread = jnp.broadcast_to(lanes.astype(F32), (size, size))
    return jnp.sum(jnp.where(rows == cols, spread, 0.0), -1, keepdims=True)


def row_mask(start, end, column):
    column = column.astype(F32)
    return ((start <= column) & (column < end)).astype(F32)


def first_heads(rows, lanes):
    at = lax.broadcasted_iota(jnp.int32, (rows, lanes), 1)
    return lax.rem(at, LANES) < HEAD_DIM


def slab(array, at):
    reads = array.shape[0] // 2
    lanes = slice(at * LANES, (at + 1) * LANES)
    return jnp.concatenate([array[:reads, lanes], array[reads:, lanes]], axis=1)


def indicator(rows, cols, place):
    at = lax.broadcasted_iota(jnp.int32, (rows, cols), 0)
    spot = lax.broadcasted_iota(jnp.int32, (rows, cols), 1)
    return place(at, spot).astype(F32).astype(BF16)


def position():
    me = lax.axis_index("read")
    core = jnp.bitwise_and(me, CORES - 1)
    kind = jnp.bitwise_and(jnp.right_shift(me, 1), KINDS - 1)
    return me, core, kind


def head_lanes(core, half):
    return pl.ds(pl.multiple_of(core * half, LANES), half)


def part_rows(arrived, rows, cells):
    def pick(shift):
        return indicator(
            cells,
            2 * cells,
            lambda at, spot: spot == lax.div(at, rows) * (2 * rows) + lax.rem(at, rows) + shift,
        )

    both = jnp.concatenate(arrived, axis=1)
    width = arrived[0].shape[1]
    source, upstream = dot(pick(0), both), dot(pick(rows), both).astype(BF16)

    def stack(array):
        return jnp.concatenate(
            [array[:, at * width : (at + 1) * width] for at in range(len(arrived))], axis=0
        )

    return stack(source), stack(upstream)


def normalise(source):
    inverse = lax.rsqrt(jnp.mean(source * source, -1, keepdims=True) + 1e-05)
    return source * inverse, inverse


def arrange_kernel(
    features, grad_out, weights, start, end, send, heads_in, heads_out, bounds, arrived, start_here,
    end_here, sems
):
    rows, cols, width = features.shape
    half = width // CORES
    _, core, _ = position()
    copies = [
        pltpu.make_async_copy(features, arrived.at[0], sems.at[0]),
        pltpu.make_async_copy(grad_out, arrived.at[1], sems.at[1]),
        pltpu.make_async_copy(start, start_here, sems.at[2]),
        pltpu.make_async_copy(end, end_here, sems.at[3]),
        pltpu.make_async_copy(
            weights.at[pl.ds(0, 3), :, head_lanes(core, half)], heads_in, sems.at[4]
        ),
        pltpu.make_async_copy(weights.at[3, head_lanes(core, half), :], heads_out, sems.at[5]),
    ]
    for copy in copies:
        copy.start()
    cells = rows * cols

    def place(at, spot):
        return spot == lax.rem(at, 2 * rows) * cols + lax.div(at, 2 * rows)

    order = indicator(2 * cells, 2 * cells, place)
    copies[0].wait()
    copies[1].wait()
    send[...] = dot(order, arrived[...].reshape(2 * cells, width)).astype(BF16)
    copies[2].wait()
    copies[3].wait()
    first, last = upright(start_here[...]), upright(end_here[...])
    lane = lax.broadcasted_iota(jnp.int32, bounds.shape, 1)
    bounds[...] = jnp.where(lane == 0, first, last)
    copies[4].wait()
    copies[5].wait()


def project_kernel(
    own, other, heads_in, heads_out, bounds, proj, tied, normed_own, scales, *, rows, col_dev,
    scale
):
    cells = own.shape[0] // 2
    half = own.shape[1] // CORES
    me, _, _ = position()
    first_col = lax.axis_index("pos") * col_dev
    source, upstream = part_rows([own[...], other[...]], rows, cells)
    normed32, inverse = normalise(source)
    normed = normed32.astype(BF16)
    normed_own[...] = normed32[:cells]
    first, last = bounds[:, 0:1], bounds[:, 1:2]
    lane = lax.broadcasted_iota(jnp.int32, scales.shape, 1)
    scales[...] = jnp.where(lane == 0, first, jnp.where(lane == 1, last, inverse[:cells]))
    covered = jnp.concatenate(
        [
            row_mask(first, last, first_col + me),
            row_mask(first, last, first_col + jnp.bitwise_xor(me, 1)),
        ],
        axis=0,
    )
    query = (dot(normed, heads_in[0]) * covered).astype(BF16)
    keys = (dot(normed, heads_in[1]) * covered).astype(BF16)
    values = (dot(normed, heads_in[2]) * covered).astype(BF16)
    back_out = dot(upstream, heads_out[...], (1, 1)).astype(BF16)
    proj[0] = keys
    proj[1] = query
    proj[2] = back_out

    low = first_heads(cells, 2 * LANES)
    chips = tied.shape[0]
    part = cells // chips

    def both_heads(array):
        return jnp.concatenate([jnp.where(low, array, 0), jnp.where(low, 0, array)], axis=0)

    for pair in range(half // LANES):
        logits = dot(both_heads(slab(query, pair)), slab(keys, pair), (1, 1))
        slopes = dot(both_heads(slab(back_out, pair)), slab(values, pair), (1, 1))
        for odd in range(2):
            here = slice(odd * cells, (odd + 1) * cells)
            both = jnp.concatenate(
                [
                    (logits[here] * (scale / LOGIT_UNIT)).reshape(chips, part, cells),
                    (slopes[here] * (1.0 / SLOPE_UNIT)).reshape(chips, part, cells),
                ],
                axis=1,
            )
            spot = (2 * pair + odd) * 2 * part
            tied[:, spot : spot + 2 * part, :] = both


def halve_kernel(rows, half, *, first):
    half[...] = rows[first : first + half.shape[0]]


def operand_kernel(weights, bounds, *refs, rows, col_dev):
    *raw, left, ops, heads, heads_back, sem = refs
    width = left.shape[1]
    half = width // CORES
    cells = bounds.shape[0]
    me, core, kind = position()
    first_col = lax.axis_index("pos") * col_dev
    fetches = []
    for at, source_of in ((0, 1), (1, 0), (3, 2)):
        copy = pltpu.make_async_copy(
            weights.at[source_of, :, head_lanes(core, half)], heads, sem
        )
        fetches.append((kind == at, copy))
    copy = pltpu.make_async_copy(weights.at[3, head_lanes(core, half), :], heads_back, sem)
    fetches.append((kind == 2, copy))
    for here, copy in fetches:
        pl.when(here)(copy.start)

    blocks, pieces = [], []
    for ref in raw:
        pieces.append(ref[...])
        if sum(piece.shape[0] for piece in pieces) == 2 * cells:
            blocks.append(jnp.concatenate(pieces, axis=0) if len(pieces) > 1 else pieces[0])
            pieces = []
    source, upstream = part_rows(blocks, rows, cells)
    normed = normalise(source)[0].astype(BF16)
    first, last = bounds[:, 0:1], bounds[:, 1:2]
    covered = jnp.concatenate(
        [
            row_mask(first, last, first_col + jnp.bitwise_xor(me, at))
            for at in range(2 * KINDS)
        ],
        axis=0,
    )
    for here, copy in fetches:
        pl.when(here)(copy.wait)

    @pl.when(kind == 2)
    def _():
        ops[...] = dot(upstream, heads_back[...], (1, 1)).astype(BF16)

    @pl.when(kind != 2)
    def _():
        ops[...] = (dot(normed, heads[...]) * covered).astype(BF16)

    @pl.when(kind == KINDS - 1)
    def _():
        left[...] = upstream

    @pl.when(kind < KINDS - 1)
    def _():
        left[...] = normed


def soften_kernel(parts, copies, *, scale, part):
    total = jnp.sum(parts[...].astype(F32), axis=0)
    blocks = total.reshape(-1, 2 * part, total.shape[-1])
    logits = blocks[:, :part] * LOGIT_UNIT
    slopes = blocks[:, part:] * SLOPE_UNIT
    expon = jnp.exp(logits)
    probs = expon / jnp.sum(expon, -1, keepdims=True)
    mixed = scale * probs * (slopes - jnp.sum(probs * slopes, -1, keepdims=True))
    result = jnp.concatenate([probs, mixed], axis=1).reshape(total.shape).astype(BF16)
    for chip in range(copies.shape[0]):
        copies[chip] = result


def head_maps(pairs, head, cells):
    part = cells // pairs.shape[0]
    both = pairs[:, head * 2 * part : (head + 1) * 2 * part, :].astype(F32)
    return both[:, :part].reshape(cells, cells), both[:, part:].reshape(cells, cells)


def gradient_kernel(
    pairs, proj, bounds, ops, weights, left_far, own, other, product, spare, grads, right, heads_in,
    left, sems, *, col_dev
):
    cells = proj.shape[1] // 2
    half = proj.shape[2]
    me, core, kind = position()
    first_col = lax.axis_index("pos") * col_dev
    copies = [
        pltpu.make_async_copy(
            weights.at[at, :, head_lanes(core, half)], heads_in.at[at], sems.at[at]
        )
        for at in range(3)
    ]
    copies.append(pltpu.make_async_copy(left_far, left, sems.at[3]))
    for at in (3, 0, 1, 2):
        copies[at].start()
    first, last = bounds[:, 0:1], bounds[:, 1:2]
    masks = []
    for at in range(2 * KINDS):
        mask = row_mask(first, last, first_col + jnp.bitwise_xor(me, at))
        masks.append(jnp.broadcast_to(mask, (cells, LANES)))
    covered = jnp.concatenate(masks[:2], axis=1)
    plane_covered = jnp.where(kind == KINDS - 1, 1.0, jnp.concatenate(masks, axis=1))
    low = first_heads(cells, 2 * LANES)
    plane_low = first_heads(cells, 2 * KINDS * LANES)
    use_probs = kind >= 2
    use_flip = (kind == 1) | (kind == 2)

    for pair in range(half // LANES):
        lanes = slice(pair * LANES, (pair + 1) * LANES)

        def store(at, maps, operand):
            result = dot(jnp.concatenate(maps, axis=0), operand)
            result = (jnp.where(low, result[:cells], result[cells:]) * covered).astype(BF16)
            grads[at, :cells, lanes] = result[:, :LANES]
            grads[at, cells:, lanes] = result[:, LANES:]

        maps = [head_maps(pairs, 2 * pair + odd, cells) for odd in range(2)]
        flips = [(a.T, b.T) for a, b in maps]

        store(0, [b.astype(BF16) for _, b in maps], slab(proj[0], pair))
        store(1, [b.astype(BF16) for _, b in flips], slab(proj[1], pair))
        store(2, [a.astype(BF16) for a, _ in flips], slab(proj[2], pair))

        chosen = []
        for (a, b), (a_flip, b_flip) in zip(maps, flips):
            flat = jnp.where(use_probs, a, b)
            flip = jnp.where(use_probs, a_flip, b_flip)
            chosen.append(jnp.where(use_flip, flip, flat).astype(BF16))
        cat = jnp.concatenate(
            [ops[at : at + cells, lanes] for at in range(0, ops.shape[0], cells)], axis=1
        )
        result = dot(jnp.concatenate(chosen, axis=0), cat)
        result = jnp.where(plane_low, result[:cells], result[cells:]) * plane_covered
        result = result.astype(BF16)
        for at in range(2 * KINDS):
            right[at * cells : (at + 1) * cells, lanes] = result[
                :, at * LANES : (at + 1) * LANES
            ]

    copies[3].wait()

    @pl.when(kind < KINDS - 1)
    def _():
        product[...] = dot(left[...], right[...], (0, 0)).astype(BF16)

    @pl.when(kind == KINDS - 1)
    def _():
        rows = dot(right[...], left[...], (0, 0)).astype(BF16)

        @pl.when(core == 0)
        def _():
            product[:half] = rows[:, :half]
            spare[...] = rows[:, half:]

        @pl.when(core == 1)
        def _():
            product[:half] = rows[:, half:]
            spare[...] = rows[:, :half]

    total = None
    for at in range(3):
        copies[at].wait()
        term = dot(grads[at], heads_in[at], (1, 1))
        total = term if total is None else total + term
    own[...] = total[:cells]
    other[...] = total[cells:].astype(BF16)


def pack_kernel(grad_own, grad_recv, normed, bounds, product, spare, payload, *, rows):
    cells, width = normed.shape
    tiles = width // LANES
    half = product.shape[1]
    group = rows * tiles
    grad_norm = grad_own[...] + grad_recv[...].astype(F32)
    mean = jnp.mean(grad_norm * normed[...], -1, keepdims=True)
    result = (grad_norm - normed[...] * mean) * bounds[:, 2:3]
    result = result.astype(BF16)
    stack = jnp.concatenate(
        [result[:, t * LANES : (t + 1) * LANES] for t in range(tiles)], axis=0
    )

    def place(at, spot):
        tile, cell = lax.div(spot, cells), lax.rem(spot, cells)
        return at == lax.div(cell, rows) * group + tile * rows + lax.rem(cell, rows)

    _, core, kind = position()

    @pl.when((kind < KINDS - 1) | (core == 0))
    def _():
        payload[:half, :half] = product[:half]

    @pl.when(kind < KINDS - 1)
    def _():
        payload[half:, :half] = product[half:]

    @pl.when((kind == KINDS - 1) & (core == 0))
    def _():
        payload[half:, :half] = spare[...]

    @pl.when((kind == KINDS - 1) & (core == 1))
    def _():
        payload[:half, :half] = spare[...]
        payload[half:, :half] = product[:half]

    payload[:, half:] = dot(indicator(width, tiles * cells, place), stack).astype(BF16)


def finish_kernel(arrived, grad_input, sums):
    count, chunk, wide = arrived.shape
    rows, cols, width = grad_input.shape
    half = wide - LANES
    group = KINDS * CORES
    for kind in range(KINDS):
        for core in range(CORES):
            total = None
            for base in range(0, count, group):
                term = arrived[base + kind * CORES + core, :, :half].astype(F32)
                total = term if total is None else total + term
            spot = kind * width + core * half
            sums[:, spot : spot + half] = total
    flat = arrived[:, :, half:].astype(F32).reshape(count * chunk, LANES).astype(BF16)
    cells = rows * cols

    def place(at, spot):
        tile, cell = lax.div(at, cells), lax.rem(at, cells)
        return spot == lax.rem(cell, cols) * chunk + tile * rows + lax.div(cell, cols)

    tiles = width // LANES
    moved = dot(indicator(tiles * cells, count * chunk, place), flat).astype(BF16)
    for tile in range(tiles):
        for row in range(rows):
            spot = tile * cells + row * cols
            grad_input[row, :, tile * LANES : (tile + 1) * LANES] = moved[spot : spot + cols]


def exchange(array, groups):
    return lax.all_to_all(
        array, "read", split_axis=0, concat_axis=0, tiled=True, axis_index_groups=groups
    )


def call(kernel, args, outs, mib, far=(), scratch=(), cost=None):
    args = [
        pltpu.with_memory_space_constraint(arg, pltpu.HBM) if at in far else arg
        for at, arg in enumerate(args)
    ]
    near, away = (pl.BlockSpec(memory_space=space) for space in (pltpu.VMEM, pltpu.HBM))
    return pl.pallas_call(
        kernel,
        in_specs=[away if at in far else near for at in range(len(args))],
        out_specs=jax.tree.map(lambda _: near, outs),
        out_shape=outs,
        scratch_shapes=scratch,
        cost_estimate=cost,
        compiler_params=pltpu.CompilerParams(vmem_limit_bytes=mib * MIB),
    )(*args)


def shards(features, grad_out, weights, read_start, read_end):
    rows, col_dev, width = features.shape
    count = lax.axis_size("read")
    pos_count = lax.axis_size("pos")
    scale = 1.0 / math.sqrt(HEAD_DIM * col_dev * pos_count)
    reads = rows * count
    chips = count // CORES
    half = width // CORES
    part = reads // chips
    tied_rows = (HEADS // CORES) * 2 * part
    chunk = width // count
    start = read_start.reshape(1, reads)
    end = read_end.reshape(1, reads)

    same_core = [list(range(c, count, CORES)) for c in range(CORES)]

    def swap(array, bits):
        return lax.ppermute(array, "read", [(i, i ^ bits) for i in range(count)])

    shape = jax.ShapeDtypeStruct
    send, heads_in, heads_out, bounds = call(
        arrange_kernel,
        (features, grad_out, weights, start, end),
        (
            shape((2 * reads, width), BF16),
            shape((3, width, half), BF16),
            shape((half, width), BF16),
            shape((reads, LANES), F32),
        ),
        8,
        (0, 1, 2, 3, 4),
        [
            pltpu.VMEM((2, *features.shape), BF16),
            pltpu.VMEM((1, reads), jnp.int32),
            pltpu.VMEM((1, reads), jnp.int32),
            pltpu.SemaphoreType.DMA((6,)),
        ],
    )
    own = exchange(send.reshape(count, 2 * rows, width), None).reshape(send.shape)
    other = swap(own, 1)
    proj, tied, normed, bounds = call(
        functools.partial(project_kernel, rows=rows, col_dev=col_dev, scale=scale),
        (own, other, heads_in, heads_out, bounds),
        (
            shape((KINDS - 1, 2 * reads, half), BF16),
            shape((chips, tied_rows, reads), F32),
            shape((reads, width), F32),
            shape((reads, LANES), F32),
        ),
        16,
    )

    parts = exchange(tied.astype(F16), same_core)
    raw = {1: swap(own, CORES), 2: swap(own, 2 * CORES)}
    parts = lax.psum(jnp.sum(parts.astype(F32), 0, keepdims=True), "pos")
    copies = call(
        functools.partial(soften_kernel, scale=scale, part=part),
        (parts,),
        shape((chips, tied_rows, reads), BF16),
        8,
    )
    held_bounds = bounds
    pairs = exchange(copies, same_core)
    halves = call(
        functools.partial(halve_kernel, first=0),
        (raw[1],),
        shape((reads, width), BF16),
        4,
        cost=pl.CostEstimate(flops=6 * 10**9, bytes_accessed=MIB, transcendentals=0),
    )
    diagonal = [swap(halves, 2 * CORES), swap(raw[2][reads:], CORES)]

    blocks = [own, other]
    for near in (raw[1], raw[2]):
        blocks += [near, swap(near, 1)]
    blocks += [*diagonal, *[swap(a, 1) for a in diagonal]]
    cells = 2 * KINDS * reads
    left, ops = call(
        functools.partial(operand_kernel, rows=rows, col_dev=col_dev),
        (weights, held_bounds, *blocks),
        (shape((cells, width), BF16), shape((cells, half), BF16)),
        24,
        (0,),
        [
            pltpu.VMEM((width, half), BF16),
            pltpu.VMEM((half, width), BF16),
            pltpu.SemaphoreType.DMA,
        ],
        pl.CostEstimate(flops=40 * 10**9, bytes_accessed=8 * MIB, transcendentals=0),
    )

    grad_own, grad_other, product, spare = call(
        functools.partial(gradient_kernel, col_dev=col_dev),
        (pairs, proj, bounds, ops, weights, left),
        (
            shape((reads, width), F32),
            shape((reads, width), BF16),
            shape((width, half), BF16),
            shape((half, half), BF16),
        ),
        24,
        (4, 5),
        [
            pltpu.VMEM((3, 2 * reads, half), BF16),
            pltpu.VMEM((cells, half), BF16),
            pltpu.VMEM((3, width, half), BF16),
            pltpu.VMEM((cells, width), BF16),
            pltpu.SemaphoreType.DMA((4,)),
        ],
    )
    grad_recv = swap(grad_other, 1)
    spare = swap(spare, 1)
    payload = call(
        functools.partial(pack_kernel, rows=rows),
        (grad_own, grad_recv, normed, bounds, product, spare),
        shape((width, half + LANES), BF16),
        8,
    )
    arrived = exchange(payload.reshape(count, chunk, half + LANES), None)
    grad_input, sums = call(
        finish_kernel,
        (arrived,),
        (shape((rows, col_dev, width), BF16), shape((chunk, KINDS * width), F32)),
        8,
    )
    weight_grads = lax.psum_scatter(sums, "pos", scatter_dimension=0, tiled=True)
    return (grad_input, weight_grads)


def solution(mesh):
    in_specs = (P("read", "pos", None), P("read", "pos", None), P(), P(), P())
    out_specs = (P("read", "pos", None), P(("read", "pos"), None))
    return jax.shard_map(shards, mesh=mesh, in_specs=in_specs, out_specs=out_specs, check_vma=False)
```

```python
import functools
import math

import jax
import jax.numpy as jnp
from jax import lax
from jax.experimental import pallas as pl
from jax.experimental.pallas import tpu as pltpu
from jax.sharding import PartitionSpec as P

HEADS = 12
HEAD_DIM = 64
CORES = 2
KINDS = 4
LANES = 128
MIB = 1024 * 1024

BF16 = jnp.bfloat16
F16 = jnp.float16
LOGIT_UNIT = 2.0
SLOPE_UNIT = 1024.0
F32 = jnp.float32


def dot(left, right, contract=(1, 0)):
    return lax.dot_general(
        left, right, (((contract[0],), (contract[1],)), ((), ())), preferred_element_type=F32
    )


def upright(lanes):
    size = lanes.shape[1]
    rows = lax.broadcasted_iota(jnp.int32, (size, size), 0)
    cols = lax.broadcasted_iota(jnp.int32, (size, size), 1)
    spread = jnp.broadcast_to(lanes.astype(F32), (size, size))
    return jnp.sum(jnp.where(rows == cols, spread, 0.0), -1, keepdims=True)


def row_mask(start, end, column):
    column = column.astype(F32)
    return ((start <= column) & (column < end)).astype(F32)


def first_heads(rows, lanes):
    at = lax.broadcasted_iota(jnp.int32, (rows, lanes), 1)
    return lax.rem(at, LANES) < HEAD_DIM


def slab(array, at):
    reads = array.shape[0] // 2
    lanes = slice(at * LANES, (at + 1) * LANES)
    return jnp.concatenate([array[:reads, lanes], array[reads:, lanes]], axis=1)


def indicator(rows, cols, place):
    at = lax.broadcasted_iota(jnp.int32, (rows, cols), 0)
    spot = lax.broadcasted_iota(jnp.int32, (rows, cols), 1)
    return place(at, spot).astype(F32).astype(BF16)


def position():
    me = lax.axis_index("read")
    core = jnp.bitwise_and(me, CORES - 1)
    kind = jnp.bitwise_and(jnp.right_shift(me, 1), KINDS - 1)
    return me, core, kind


def head_lanes(core, half):
    return pl.ds(pl.multiple_of(core * half, LANES), half)


def part_rows(arrived, rows, cells):
    def pick(shift):
        return indicator(
            cells,
            2 * cells,
            lambda at, spot: spot == lax.div(at, rows) * (2 * rows) + lax.rem(at, rows) + shift,
        )

    both = jnp.concatenate(arrived, axis=1)
    width = arrived[0].shape[1]
    source, upstream = dot(pick(0), both), dot(pick(rows), both).astype(BF16)

    def stack(array):
        return jnp.concatenate(
            [array[:, at * width : (at + 1) * width] for at in range(len(arrived))], axis=0
        )

    return stack(source), stack(upstream)


def normalise(source):
    inverse = lax.rsqrt(jnp.mean(source * source, -1, keepdims=True) + 1e-05)
    return source * inverse, inverse


def arrange_kernel(
    features, grad_out, weights, start, end, send, heads_in, heads_out, bounds, arrived, start_here,
    end_here, sems
):
    rows, cols, width = features.shape
    half = width // CORES
    _, core, _ = position()
    copies = [
        pltpu.make_async_copy(features, arrived.at[0], sems.at[0]),
        pltpu.make_async_copy(grad_out, arrived.at[1], sems.at[1]),
        pltpu.make_async_copy(start, start_here, sems.at[2]),
        pltpu.make_async_copy(end, end_here, sems.at[3]),
        pltpu.make_async_copy(
            weights.at[pl.ds(0, 3), :, head_lanes(core, half)], heads_in, sems.at[4]
        ),
        pltpu.make_async_copy(weights.at[3, head_lanes(core, half), :], heads_out, sems.at[5]),
    ]
    for copy in copies:
        copy.start()
    cells = rows * cols

    def place(at, spot):
        return spot == lax.rem(at, 2 * rows) * cols + lax.div(at, 2 * rows)

    order = indicator(2 * cells, 2 * cells, place)
    copies[0].wait()
    copies[1].wait()
    send[...] = dot(order, arrived[...].reshape(2 * cells, width)).astype(BF16)
    copies[2].wait()
    copies[3].wait()
    first, last = upright(start_here[...]), upright(end_here[...])
    lane = lax.broadcasted_iota(jnp.int32, bounds.shape, 1)
    bounds[...] = jnp.where(lane == 0, first, last)
    copies[4].wait()
    copies[5].wait()


def project_kernel(
    own, other, heads_in, heads_out, bounds, proj, tied, normed_own, scales, *, rows, col_dev,
    scale
):
    cells = own.shape[0] // 2
    half = own.shape[1] // CORES
    me, _, _ = position()
    first_col = lax.axis_index("pos") * col_dev
    source, upstream = part_rows([own[...], other[...]], rows, cells)
    normed32, inverse = normalise(source)
    normed = normed32.astype(BF16)
    normed_own[...] = normed32[:cells]
    first, last = bounds[:, 0:1], bounds[:, 1:2]
    lane = lax.broadcasted_iota(jnp.int32, scales.shape, 1)
    scales[...] = jnp.where(lane == 0, first, jnp.where(lane == 1, last, inverse[:cells]))
    covered = jnp.concatenate(
        [
            row_mask(first, last, first_col + me),
            row_mask(first, last, first_col + jnp.bitwise_xor(me, 1)),
        ],
        axis=0,
    )
    query = (dot(normed, heads_in[0]) * covered).astype(BF16)
    keys = (dot(normed, heads_in[1]) * covered).astype(BF16)
    values = (dot(normed, heads_in[2]) * covered).astype(BF16)
    back_out = dot(upstream, heads_out[...], (1, 1)).astype(BF16)
    proj[0] = keys
    proj[1] = query
    proj[2] = back_out

    low = first_heads(cells, 2 * LANES)
    chips = tied.shape[0]
    part = cells // chips

    def both_heads(array):
        return jnp.concatenate([jnp.where(low, array, 0), jnp.where(low, 0, array)], axis=0)

    for pair in range(half // LANES):
        logits = dot(both_heads(slab(query, pair)), slab(keys, pair), (1, 1))
        slopes = dot(both_heads(slab(back_out, pair)), slab(values, pair), (1, 1))
        for odd in range(2):
            here = slice(odd * cells, (odd + 1) * cells)
            both = jnp.concatenate(
                [
                    (logits[here] * (scale / LOGIT_UNIT)).reshape(chips, part, cells),
                    (slopes[here] * (1.0 / SLOPE_UNIT)).reshape(chips, part, cells),
                ],
                axis=1,
            )
            spot = (2 * pair + odd) * 2 * part
            tied[:, spot : spot + 2 * part, :] = both


def operand_kernel(weights, bounds, *refs, rows, col_dev):
    *raw, left, ops, heads, heads_back, sem = refs
    width = left.shape[1]
    half = width // CORES
    cells = bounds.shape[0]
    me, core, kind = position()
    first_col = lax.axis_index("pos") * col_dev
    fetches = []
    for at, source_of in ((0, 1), (1, 0), (3, 2)):
        copy = pltpu.make_async_copy(
            weights.at[source_of, :, head_lanes(core, half)], heads, sem
        )
        fetches.append((kind == at, copy))
    copy = pltpu.make_async_copy(weights.at[3, head_lanes(core, half), :], heads_back, sem)
    fetches.append((kind == 2, copy))
    for here, copy in fetches:
        pl.when(here)(copy.start)

    blocks, pieces = [], []
    for ref in raw:
        pieces.append(ref[...])
        if sum(piece.shape[0] for piece in pieces) == 2 * cells:
            blocks.append(jnp.concatenate(pieces, axis=0) if len(pieces) > 1 else pieces[0])
            pieces = []
    source, upstream = part_rows(blocks, rows, cells)
    normed = normalise(source)[0].astype(BF16)
    first, last = bounds[:, 0:1], bounds[:, 1:2]
    covered = jnp.concatenate(
        [
            row_mask(first, last, first_col + jnp.bitwise_xor(me, at))
            for at in range(2 * KINDS)
        ],
        axis=0,
    )
    for here, copy in fetches:
        pl.when(here)(copy.wait)

    @pl.when(kind == 2)
    def _():
        ops[...] = dot(upstream, heads_back[...], (1, 1)).astype(BF16)

    @pl.when(kind != 2)
    def _():
        ops[...] = (dot(normed, heads[...]) * covered).astype(BF16)

    @pl.when(kind == KINDS - 1)
    def _():
        left[...] = upstream

    @pl.when(kind < KINDS - 1)
    def _():
        left[...] = normed


def soften_kernel(parts, copies, *, scale, part):
    total = jnp.sum(parts[...].astype(F32), axis=0)
    blocks = total.reshape(-1, 2 * part, total.shape[-1])
    logits = blocks[:, :part] * LOGIT_UNIT
    slopes = blocks[:, part:] * SLOPE_UNIT
    expon = jnp.exp(logits)
    probs = expon / jnp.sum(expon, -1, keepdims=True)
    mixed = scale * probs * (slopes - jnp.sum(probs * slopes, -1, keepdims=True))
    result = jnp.concatenate([probs, mixed], axis=1).reshape(total.shape).astype(BF16)
    for chip in range(copies.shape[0]):
        copies[chip] = result


def head_maps(pairs, head, cells):
    part = cells // pairs.shape[0]
    both = pairs[:, head * 2 * part : (head + 1) * 2 * part, :].astype(F32)
    return both[:, :part].reshape(cells, cells), both[:, part:].reshape(cells, cells)


def gradient_kernel(
    pairs, proj, bounds, ops, weights, left_far, own, other, product, spare, grads, right, heads_in,
    left, sems, *, col_dev
):
    cells = proj.shape[1] // 2
    half = proj.shape[2]
    me, core, kind = position()
    first_col = lax.axis_index("pos") * col_dev
    copies = [
        pltpu.make_async_copy(
            weights.at[at, :, head_lanes(core, half)], heads_in.at[at], sems.at[at]
        )
        for at in range(3)
    ]
    copies.append(pltpu.make_async_copy(left_far, left, sems.at[3]))
    for at in (3, 0, 1, 2):
        copies[at].start()
    first, last = bounds[:, 0:1], bounds[:, 1:2]
    masks = []
    for at in range(2 * KINDS):
        mask = row_mask(first, last, first_col + jnp.bitwise_xor(me, at))
        masks.append(jnp.broadcast_to(mask, (cells, LANES)))
    covered = jnp.concatenate(masks[:2], axis=1)
    plane_covered = jnp.where(kind == KINDS - 1, 1.0, jnp.concatenate(masks, axis=1))
    low = first_heads(cells, 2 * LANES)
    plane_low = first_heads(cells, 2 * KINDS * LANES)
    use_probs = kind >= 2
    use_flip = (kind == 1) | (kind == 2)

    for pair in range(half // LANES):
        lanes = slice(pair * LANES, (pair + 1) * LANES)

        def store(at, maps, operand):
            result = dot(jnp.concatenate(maps, axis=0), operand)
            result = (jnp.where(low, result[:cells], result[cells:]) * covered).astype(BF16)
            grads[at, :cells, lanes] = result[:, :LANES]
            grads[at, cells:, lanes] = result[:, LANES:]

        maps = [head_maps(pairs, 2 * pair + odd, cells) for odd in range(2)]
        flips = [(a.T, b.T) for a, b in maps]

        store(0, [b.astype(BF16) for _, b in maps], slab(proj[0], pair))
        store(1, [b.astype(BF16) for _, b in flips], slab(proj[1], pair))
        store(2, [a.astype(BF16) for a, _ in flips], slab(proj[2], pair))

        chosen = []
        for (a, b), (a_flip, b_flip) in zip(maps, flips):
            flat = jnp.where(use_probs, a, b)
            flip = jnp.where(use_probs, a_flip, b_flip)
            chosen.append(jnp.where(use_flip, flip, flat).astype(BF16))
        cat = jnp.concatenate(
            [ops[at : at + cells, lanes] for at in range(0, ops.shape[0], cells)], axis=1
        )
        result = dot(jnp.concatenate(chosen, axis=0), cat)
        result = jnp.where(plane_low, result[:cells], result[cells:]) * plane_covered
        result = result.astype(BF16)
        for at in range(2 * KINDS):
            right[at * cells : (at + 1) * cells, lanes] = result[
                :, at * LANES : (at + 1) * LANES
            ]

    copies[3].wait()

    @pl.when(kind < KINDS - 1)
    def _():
        product[...] = dot(left[...], right[...], (0, 0)).astype(BF16)

    @pl.when(kind == KINDS - 1)
    def _():
        rows = dot(right[...], left[...], (0, 0)).astype(BF16)

        @pl.when(core == 0)
        def _():
            product[:half] = rows[:, :half]
            spare[...] = rows[:, half:]

        @pl.when(core == 1)
        def _():
            product[:half] = rows[:, half:]
            spare[...] = rows[:, :half]

    total = None
    for at in range(3):
        copies[at].wait()
        term = dot(grads[at], heads_in[at], (1, 1))
        total = term if total is None else total + term
    own[...] = total[:cells]
    other[...] = total[cells:].astype(BF16)


def pack_kernel(grad_own, grad_recv, normed, bounds, product, spare, payload, *, rows):
    cells, width = normed.shape
    tiles = width // LANES
    half = product.shape[1]
    group = rows * tiles
    grad_norm = grad_own[...] + grad_recv[...].astype(F32)
    mean = jnp.mean(grad_norm * normed[...], -1, keepdims=True)
    result = (grad_norm - normed[...] * mean) * bounds[:, 2:3]
    result = result.astype(BF16)
    stack = jnp.concatenate(
        [result[:, t * LANES : (t + 1) * LANES] for t in range(tiles)], axis=0
    )

    def place(at, spot):
        tile, cell = lax.div(spot, cells), lax.rem(spot, cells)
        return at == lax.div(cell, rows) * group + tile * rows + lax.rem(cell, rows)

    _, core, kind = position()

    @pl.when((kind < KINDS - 1) | (core == 0))
    def _():
        payload[:half, :half] = product[:half]

    @pl.when(kind < KINDS - 1)
    def _():
        payload[half:, :half] = product[half:]

    @pl.when((kind == KINDS - 1) & (core == 0))
    def _():
        payload[half:, :half] = spare[...]

    @pl.when((kind == KINDS - 1) & (core == 1))
    def _():
        payload[:half, :half] = spare[...]
        payload[half:, :half] = product[:half]

    payload[:, half:] = dot(indicator(width, tiles * cells, place), stack).astype(BF16)


def finish_kernel(arrived, grad_input, sums):
    count, chunk, wide = arrived.shape
    rows, cols, width = grad_input.shape
    half = wide - LANES
    group = KINDS * CORES
    for kind in range(KINDS):
        for core in range(CORES):
            total = None
            for base in range(0, count, group):
                term = arrived[base + kind * CORES + core, :, :half].astype(F32)
                total = term if total is None else total + term
            spot = kind * width + core * half
            sums[:, spot : spot + half] = total
    flat = arrived[:, :, half:].astype(F32).reshape(count * chunk, LANES).astype(BF16)
    cells = rows * cols

    def place(at, spot):
        tile, cell = lax.div(at, cells), lax.rem(at, cells)
        return spot == lax.rem(cell, cols) * chunk + tile * rows + lax.div(cell, cols)

    tiles = width // LANES
    moved = dot(indicator(tiles * cells, count * chunk, place), flat).astype(BF16)
    for tile in range(tiles):
        for row in range(rows):
            spot = tile * cells + row * cols
            grad_input[row, :, tile * LANES : (tile + 1) * LANES] = moved[spot : spot + cols]


def exchange(array, groups):
    return lax.all_to_all(
        array, "read", split_axis=0, concat_axis=0, tiled=True, axis_index_groups=groups
    )


def call(kernel, args, outs, mib, far=(), scratch=(), cost=None):
    args = [
        pltpu.with_memory_space_constraint(arg, pltpu.HBM) if at in far else arg
        for at, arg in enumerate(args)
    ]
    near, away = (pl.BlockSpec(memory_space=space) for space in (pltpu.VMEM, pltpu.HBM))
    return pl.pallas_call(
        kernel,
        in_specs=[away if at in far else near for at in range(len(args))],
        out_specs=jax.tree.map(lambda _: near, outs),
        out_shape=outs,
        scratch_shapes=scratch,
        cost_estimate=cost,
        compiler_params=pltpu.CompilerParams(vmem_limit_bytes=mib * MIB),
    )(*args)


def shards(features, grad_out, weights, read_start, read_end):
    rows, col_dev, width = features.shape
    count = lax.axis_size("read")
    pos_count = lax.axis_size("pos")
    scale = 1.0 / math.sqrt(HEAD_DIM * col_dev * pos_count)
    reads = rows * count
    chips = count // CORES
    half = width // CORES
    part = reads // chips
    tied_rows = (HEADS // CORES) * 2 * part
    chunk = width // count
    start = read_start.reshape(1, reads)
    end = read_end.reshape(1, reads)

    same_core = [list(range(c, count, CORES)) for c in range(CORES)]

    def swap(array, bits):
        return lax.ppermute(array, "read", [(i, i ^ bits) for i in range(count)])

    shape = jax.ShapeDtypeStruct
    send, heads_in, heads_out, bounds = call(
        arrange_kernel,
        (features, grad_out, weights, start, end),
        (
            shape((2 * reads, width), BF16),
            shape((3, width, half), BF16),
            shape((half, width), BF16),
            shape((reads, LANES), F32),
        ),
        8,
        (0, 1, 2, 3, 4),
        [
            pltpu.VMEM((2, *features.shape), BF16),
            pltpu.VMEM((1, reads), jnp.int32),
            pltpu.VMEM((1, reads), jnp.int32),
            pltpu.SemaphoreType.DMA((6,)),
        ],
    )
    own = exchange(send.reshape(count, 2 * rows, width), None).reshape(send.shape)
    other = swap(own, 1)
    proj, tied, normed, bounds = call(
        functools.partial(project_kernel, rows=rows, col_dev=col_dev, scale=scale),
        (own, other, heads_in, heads_out, bounds),
        (
            shape((KINDS - 1, 2 * reads, half), BF16),
            shape((chips, tied_rows, reads), F32),
            shape((reads, width), F32),
            shape((reads, LANES), F32),
        ),
        16,
    )

    parts = exchange(tied.astype(F16), same_core)
    raw = {1: swap(own, CORES), 2: swap(own, 2 * CORES)}
    parts = parts.astype(F32)
    if pos_count > 1:
        parts = lax.psum(jnp.sum(parts, 0, keepdims=True), "pos")
    copies = call(
        functools.partial(soften_kernel, scale=scale, part=part),
        (parts,),
        shape((chips, tied_rows, reads), BF16),
        8,
    )
    held_bounds = bounds
    pairs = exchange(copies, same_core)
    diagonal = [swap(raw[1][:reads], 2 * CORES), swap(raw[2][reads:], CORES)]

    blocks = [own, other]
    for near in (raw[1], raw[2]):
        blocks += [near, swap(near, 1)]
    blocks += [*diagonal, *[swap(a, 1) for a in diagonal]]
    cells = 2 * KINDS * reads
    left, ops = call(
        functools.partial(operand_kernel, rows=rows, col_dev=col_dev),
        (weights, held_bounds, *blocks),
        (shape((cells, width), BF16), shape((cells, half), BF16)),
        24,
        (0,),
        [
            pltpu.VMEM((width, half), BF16),
            pltpu.VMEM((half, width), BF16),
            pltpu.SemaphoreType.DMA,
        ],
        pl.CostEstimate(flops=40 * 10**9, bytes_accessed=8 * MIB, transcendentals=0),
    )

    grad_own, grad_other, product, spare = call(
        functools.partial(gradient_kernel, col_dev=col_dev),
        (pairs, proj, bounds, ops, weights, left),
        (
            shape((reads, width), F32),
            shape((reads, width), BF16),
            shape((width, half), BF16),
            shape((half, half), BF16),
        ),
        24,
        (4, 5),
        [
            pltpu.VMEM((3, 2 * reads, half), BF16),
            pltpu.VMEM((cells, half), BF16),
            pltpu.VMEM((3, width, half), BF16),
            pltpu.VMEM((cells, width), BF16),
            pltpu.SemaphoreType.DMA((4,)),
        ],
    )
    grad_recv = swap(grad_other, 1)
    last = [i for i in range(count) if i // CORES % KINDS == KINDS - 1]
    spare = lax.ppermute(spare, "read", [(i, i ^ 1) for i in last])
    payload = call(
        functools.partial(pack_kernel, rows=rows),
        (grad_own, grad_recv, normed, bounds, product, spare),
        shape((width, half + LANES), BF16),
        8,
    )
    arrived = exchange(payload.reshape(count, chunk, half + LANES), None)
    grad_input, sums = call(
        finish_kernel,
        (arrived,),
        (shape((rows, col_dev, width), BF16), shape((chunk, KINDS * width), F32)),
        8,
    )
    weight_grads = lax.psum_scatter(sums, "pos", scatter_dimension=0, tiled=True)
    return (grad_input, weight_grads)


def solution(mesh):
    in_specs = (P("read", "pos", None), P("read", "pos", None), P(), P(), P())
    out_specs = (P("read", "pos", None), P(("read", "pos"), None))
    return jax.shard_map(shards, mesh=mesh, in_specs=in_specs, out_specs=out_specs, check_vma=False)
```
